32 devices in a mesh: seq: 8 (over z, core), fsdp: 4 (over y, x).
Axes of the slice: x: 2, y: 2, z: 4, core: 2. Of those that a mesh axis runs over, the one named last changes fastest.
Arguments:
- queries: bfloat16 [4, 1024, 1024], P('fsdp', 'seq'), may hold values from -6 to 6
- keys: bfloat16 [4, 1024, 1024], P('fsdp', 'seq'), may hold values from -6 to 6
- values: bfloat16 [4, 1024, 1024], P('fsdp', 'seq'), may hold values from -6 to 6
- d_out: bfloat16 [4, 1024, 2048], P('fsdp', 'seq'), may hold values from -6 to 6
- w_out: bfloat16 [1024, 2048], P('fsdp'), may hold values from -0.1875 to 0.1875
- pattern: int32 [8, 4], replicated, may hold values from 0 to 7, as said below
- valid: int32 [4, 8], P('fsdp'), may hold values from 2 to 128, as said below
Outputs:
- d_queries: bfloat16 [4, 1024, 1024], P('fsdp', 'seq')
- d_keys: bfloat16 [4, 1024, 1024], P('fsdp', 'seq')
- d_values: bfloat16 [4, 1024, 1024], P('fsdp', 'seq')
The draws below stay inside these ranges and needn't reach their ends.
Inputs may be any that keep to these rules, and one draw needn't show every extreme that they name: Row b of the pattern, for a query block of shard p, lists the first block of shard p, block b itself, one block of shard p - 1 and one block of shard p + 1; at the first and last shard the missing neighbour's entry repeats the first block of shard p. A block listed twice is attended once. The valid patches of a shard are its first ones; every sample has a shard whose 128 patches are all valid.
All inputs are finite; a program needn't handle non-finite values.
Results may differ from the reference program's by a relative error of at most 0.018.
Values may be sent and summed in bfloat16 or wider, within the bound.
No kernel may reach another device: no remote copies, remote signals or barrier semaphores. Data moves between devices by JAX's collectives and lax.ppermute only.
A program may use at most 64 MiB of HBM per device.

```python
import jax
import jax.numpy as jnp
from jax import lax

D = 2048
HEADS = 8
HD = 128
BLOCK = 128
BLK_DEV = 1
TOK_DEV = 128
SEQ = 1024
QBLOCKS = 8
SAMPLES = 4
N_SEQ = 8


def paired_rows(key):
    key_q, key_k = jax.random.split(jax.random.fold_in(key, 7), 2)
    shape = (SAMPLES, SEQ, HEADS * HD)
    query_draw = jnp.clip(jax.random.normal(key_q, shape, jnp.float32), -6.0, 6.0)
    key_draw = jnp.clip(jax.random.normal(key_k, shape, jnp.float32), -6.0, 6.0)
    return (query_draw, key_draw)


def draw_queries(key, part):
    return paired_rows(key)[0].astype(jnp.bfloat16)


def draw_keys(key, part):
    return paired_rows(key)[1].astype(jnp.bfloat16)


def draw_pattern(key, part):
    key_l, key_r = jax.random.split(jax.random.fold_in(key, 13))
    rows = jnp.arange(QBLOCKS, dtype=jnp.int32)
    shard = rows // BLK_DEV
    first = shard * BLK_DEV
    left_pick = jax.random.randint(key_l, (QBLOCKS,), 0, BLK_DEV)
    right_pick = jax.random.randint(key_r, (QBLOCKS,), 0, BLK_DEV)
    left = jnp.where(shard > 0, (shard - 1) * BLK_DEV + left_pick, first)
    right = jnp.where(shard < N_SEQ - 1, (shard + 1) * BLK_DEV + right_pick, first)
    return jnp.stack([first, rows, left, right], axis=1).astype(jnp.int32)


def draw_valid(key, part):
    key_a, key_b = jax.random.split(jax.random.fold_in(key, 11))
    counts = jax.random.randint(key_a, (SAMPLES, N_SEQ), 2, TOK_DEV + 1)
    full = jax.random.randint(key_b, (SAMPLES, 1), 0, N_SEQ)
    return jnp.where(jnp.arange(N_SEQ)[None, :] == full, TOK_DEV, counts).astype(jnp.int32)


def block_scale(rng, dims, cuts, low, top_value):
    gain = 1.0
    for dim, parts in cuts:
        heights = jax.random.uniform(jax.random.fold_in(jax.random.fold_in(rng, 6), dim), (parts,), jnp.float32, low / len(cuts), top_value / len(cuts))
        gain = gain * jnp.repeat(jnp.exp(heights), dims[dim] // parts).reshape((-1,) + (1,) * (len(dims) - 1 - dim))
    return gain


def gaussian(key, shape, scale, most, pieces=(), kind=jnp.bfloat16):
    entries = scale * jax.random.normal(key, shape, jnp.float32)
    if pieces:
        entries = entries * block_scale(key, shape, pieces, -0.22, 0.18)
    return jnp.clip(entries, -most, most).astype(kind)


def setup_inputs(seed: int = 0) -> dict:
    arg_keys = jax.random.split(jax.random.key(seed), 8)
    queries = draw_queries(jax.random.fold_in(arg_keys[7], 71), 0)
    keys = draw_keys(jax.random.fold_in(arg_keys[7], 71), 0)
    values = gaussian(arg_keys[2], (SAMPLES, SEQ, HEADS * HD), 1.0, 6.0, ((0, 4), (1, 8)))
    d_out = gaussian(arg_keys[3], (SAMPLES, SEQ, D), 1.0, 6.0, ((0, 4), (1, 8)))
    w_out = gaussian(arg_keys[4], (HEADS * HD, D), (HEADS * HD) ** -0.5, 0.1875, ((0, 4),))
    pattern = draw_pattern(jax.random.fold_in(arg_keys[7], 71), 0)
    valid = draw_valid(jax.random.fold_in(arg_keys[7], 71), 0)
    return dict(queries=queries, keys=keys, values=values, d_out=d_out, w_out=w_out, pattern=pattern, valid=valid)


def head_split(rows):
    return rows.reshape(rows.shape[0], HEADS, HD)


def allowed_mask(pattern, valid_row, query_shard, key_shard, query_span, key_span, pad_value):
    per_shard = BLK_DEV * BLOCK
    padded = jnp.pad(pattern, ((BLK_DEV, BLK_DEV), (0, 0)), constant_values=pad_value)
    listed_rows = lax.dynamic_slice_in_dim(padded, ((query_shard + 1) * BLK_DEV).astype(jnp.int32), query_span * BLK_DEV, 0)
    key_blocks = key_shard * BLK_DEV + jnp.arange(key_span * BLK_DEV, dtype=jnp.int32)
    listed = jnp.any(listed_rows[:, :, None] == key_blocks[None, None, :], axis=1)
    key_pos = jnp.arange(key_span * per_shard, dtype=jnp.int32)
    owner = key_shard + key_pos // per_shard
    shards = jnp.arange(valid_row.shape[0], dtype=jnp.int32)
    owner_count = jnp.sum(jnp.where(owner[:, None] == shards[None, :], valid_row[None, :], 0), axis=1)
    key_ok = (key_pos % per_shard) < owner_count
    rows_q = query_span * BLK_DEV
    rows_k = key_span * BLK_DEV
    spread = jnp.broadcast_to(listed[:, None, :, None], (rows_q, BLOCK, rows_k, BLOCK))
    return spread.reshape(rows_q * BLOCK, rows_k * BLOCK) & key_ok[None, :]


def block_grads(q_rows, k_rows, v_rows, d_rows, mask):
    scale = HD ** -0.5
    high = lax.Precision.HIGHEST
    q_heads = head_split(q_rows).astype(jnp.float32)
    k_heads = head_split(k_rows).astype(jnp.float32)
    v_heads = head_split(v_rows).astype(jnp.float32)
    d_heads = head_split(d_rows).astype(jnp.float32)
    score = jnp.einsum("qhd,khd->hqk", q_heads, k_heads, precision=high) * scale
    score = jnp.where(mask[None], score, -jnp.inf)
    top = jnp.max(score, axis=2, keepdims=True)
    lse = top + jnp.log(jnp.sum(jnp.exp(score - top), axis=2, keepdims=True))
    prob = jnp.exp(score - lse)
    prob_b = prob.astype(jnp.bfloat16).astype(jnp.float32)
    out = jnp.einsum("hqk,khd->hqd", prob_b, v_heads, precision=high)
    delta = jnp.sum(jnp.transpose(d_heads, (1, 0, 2)) * out, axis=2, keepdims=True)
    d_prob = jnp.einsum("qhd,khd->hqk", d_heads, v_heads, precision=high)
    d_score = (prob * (d_prob - delta)).astype(jnp.bfloat16).astype(jnp.float32)
    d_query = jnp.einsum("hqk,khd->qhd", d_score, k_heads, precision=high) * scale
    key_grad = jnp.einsum("hqk,qhd->khd", d_score, q_heads, precision=high) * scale
    value_grad = jnp.einsum("hqk,qhd->khd", prob_b, d_heads, precision=high)
    width = HEADS * HD
    return (d_query.reshape(-1, width).astype(jnp.bfloat16), key_grad.reshape(-1, width), value_grad.reshape(-1, width))


def reference(queries, keys, values, d_out, w_out, pattern, valid):
    pad_value = -(QBLOCKS + BLK_DEV + 1)
    edge = ((TOK_DEV, TOK_DEV), (0, 0))
    width = HEADS * HD

    def one_sample(items):
        q_all, k_all, v_all, dy_all, valid_row = items
        d_attn = jnp.dot(dy_all, w_out.T, preferred_element_type=jnp.float32).astype(jnp.bfloat16)
        k_pad = jnp.pad(k_all, edge)
        v_pad = jnp.pad(v_all, edge)

        def step(carry, shard):
            key_acc, value_acc = carry
            start = (shard * TOK_DEV).astype(jnp.int32)
            q_rows = lax.dynamic_slice_in_dim(q_all, start, TOK_DEV, 0)
            d_rows = lax.dynamic_slice_in_dim(d_attn, start, TOK_DEV, 0)
            k_band = lax.dynamic_slice_in_dim(k_pad, start, 3 * TOK_DEV, 0)
            v_band = lax.dynamic_slice_in_dim(v_pad, start, 3 * TOK_DEV, 0)
            mask = allowed_mask(pattern, valid_row, shard, shard - 1, 1, 3, pad_value)
            d_query, key_band, value_band = block_grads(q_rows, k_band, v_band, d_rows, mask)
            key_acc = lax.dynamic_update_slice_in_dim(key_acc, lax.dynamic_slice_in_dim(key_acc, start, 3 * TOK_DEV, 0) + key_band, start, 0)
            value_acc = lax.dynamic_update_slice_in_dim(value_acc, lax.dynamic_slice_in_dim(value_acc, start, 3 * TOK_DEV, 0) + value_band, start, 0)
            return (key_acc, value_acc), d_query

        zeros = jnp.zeros((SEQ + 2 * TOK_DEV, width), jnp.float32)
        (key_acc, value_acc), d_query = lax.scan(step, (zeros, zeros), jnp.arange(N_SEQ, dtype=jnp.int32))
        return (d_query.reshape(SEQ, width), key_acc[TOK_DEV:TOK_DEV + SEQ].astype(jnp.bfloat16), value_acc[TOK_DEV:TOK_DEV + SEQ].astype(jnp.bfloat16))

    d_queries, d_keys, d_values = lax.map(one_sample, (queries, keys, values, d_out, valid))
    return (d_queries, d_keys, d_values)
```

```python
import functools

import jax
import jax.numpy as jnp
from jax import lax
from jax.experimental import pallas as pl
from jax.experimental.pallas import tpu as pltpu
from jax.sharding import PartitionSpec as P

HD = 128
F32 = jnp.float32
BF16 = jnp.bfloat16
NT = (((1,), (1,)), ((), ()))
NN = (((1,), (0,)), ((), ()))
TN = (((0,), (0,)), ((), ()))


def dot(a, b, dims):
    return lax.dot_general(a, b, dims, preferred_element_type=F32)


def swap(n, offset):
    pairs = []
    for i in range(offset, n - 1, 2):
        pairs += [(i, i + 1), (i + 1, i)]
    return pairs


def key_limits(pat_ref, val_ref):
    shard = lax.axis_index("seq")
    count = val_ref.shape[1]
    odd = lax.rem(shard, 2)
    blocks = (shard, shard + 1 - 2 * odd, shard - 1 + 2 * odd)
    limits = []
    for block in blocks:
        listed = pat_ref[shard, 0] == block
        for entry in range(1, pat_ref.shape[1]):
            listed = jnp.logical_or(listed, pat_ref[shard, entry] == block)
        inside = jnp.logical_and(block >= 0, block < count)
        held = val_ref[0, jnp.clip(block, 0, count - 1)]
        limits.append(jnp.where(jnp.logical_and(listed, inside), held, 0))
    return limits


def attention_kernel(
    plan, head_ref, pat_ref, val_ref, q_ref, k_ref, v_ref, core_ref, far_ref, dy_ref, *refs
):
    w_refs = refs[: len(plan)]
    dq_ref, own_ref, to_core_ref, to_far_ref = refs[len(plan) :]
    scale = HD ** (-0.5)
    rows = lax.broadcasted_iota(jnp.int32, (HD, HD), 0)
    open_keys = jnp.concatenate([rows < limit for limit in key_limits(pat_ref, val_ref)], axis=0)
    index = 0
    for w_ref, heads in zip(w_refs, plan):
        for head in range(heads):
            cols = pl.ds(pl.multiple_of(head_ref[index, 0] * HD, HD), HD)
            dest = pl.ds(pl.multiple_of(head_ref[index, 1] * HD, HD), HD)
            index += 1
            d = dot(dy_ref[0], w_ref[head * HD : (head + 1) * HD, :], NT).astype(BF16)
            q = q_ref[0, :, cols]
            k = jnp.concatenate([k_ref[0, :, cols], core_ref[0, :, cols], far_ref[0, :, cols]], 0)
            v = jnp.concatenate([v_ref[0, :, cols], core_ref[1, :, cols], far_ref[1, :, cols]], 0)
            score = jnp.where(open_keys, dot(k, q, NT) * scale, -jnp.inf)
            top = jnp.max(score, axis=0, keepdims=True)
            raised = jnp.exp(score - top)
            prob = raised * (1.0 / jnp.sum(raised, axis=0, keepdims=True))
            prob_b = prob.astype(BF16)
            d_prob = dot(v, d, NT)
            delta = jnp.sum(prob_b.astype(F32) * d_prob, axis=0, keepdims=True)
            d_score = (prob * (d_prob - delta)).astype(BF16)
            dq_ref[:, dest] = (dot(d_score, k, TN) * scale).astype(BF16)
            dk = dot(d_score, q, NN) * scale
            dv = dot(prob_b, d, NN)
            own_ref[0, :, dest] = dk[:HD]
            own_ref[1, :, dest] = dv[:HD]
            to_core_ref[0, :, dest] = dk[HD : 2 * HD].astype(BF16)
            to_core_ref[1, :, dest] = dv[HD : 2 * HD].astype(BF16)
            to_far_ref[0, :, dest] = dk[2 * HD :].astype(BF16)
            to_far_ref[1, :, dest] = dv[2 * HD :].astype(BF16)


def attention(weights, table, pattern, valid, q, k, v, kv_core, kv_far, d_out):
    plan = tuple(w.shape[0] // HD for w in weights)
    heads = sum(plan)
    tok = q.shape[1]
    smem = pl.BlockSpec(memory_space=pltpu.SMEM)
    vmem = pl.BlockSpec(memory_space=pltpu.VMEM)
    width = heads * HD
    return pl.pallas_call(
        functools.partial(attention_kernel, plan),
        out_shape=(
            jax.ShapeDtypeStruct((tok, width), BF16),
            jax.ShapeDtypeStruct((2, tok, width), F32),
            jax.ShapeDtypeStruct((2, tok, width), BF16),
            jax.ShapeDtypeStruct((2, tok, width), BF16),
        ),
        in_specs=[smem] * 3 + [vmem] * (6 + len(weights)),
        out_specs=(vmem,) * 4,
        cost_estimate=pl.CostEstimate(
            flops=heads * 2 * tok * HD * (d_out.shape[2] + 15 * HD),
            bytes_accessed=heads * 800_000,
            transcendentals=heads * 3 * tok * HD,
        ),
        compiler_params=pltpu.CompilerParams(vmem_limit_bytes=32 * 2**20),
        name="attention",
    )(table, pattern, valid, q, k, v, kv_core, kv_far, d_out, *weights)


def finish_kernel(plan, table_ref, *refs):
    ins, (dq_ref, dk_ref, dv_ref) = refs[:-3], refs[-3:]
    index = 0
    for part, heads in enumerate(plan):
        dq, own, core, far = ins[4 * part : 4 * part + 4]
        for head in range(heads):
            dest = pl.ds(pl.multiple_of(table_ref[index] * HD, HD), HD)
            index += 1
            cols = slice(head * HD, (head + 1) * HD)
            dq_ref[0, :, dest] = dq[:, cols]
            for half, out_ref in enumerate((dk_ref, dv_ref)):
                total = own[half, :, cols] + core[half, :, cols].astype(F32)
                out_ref[0, :, dest] = (total + far[half, :, cols].astype(F32)).astype(BF16)


def finish(parts, table, shape):
    plan = tuple(part[0].shape[1] // HD for part in parts)
    vmem = pl.BlockSpec(memory_space=pltpu.VMEM)
    return pl.pallas_call(
        functools.partial(finish_kernel, plan),
        out_shape=(jax.ShapeDtypeStruct(shape, BF16),) * 3,
        in_specs=[pl.BlockSpec(memory_space=pltpu.SMEM)] + [vmem] * (4 * len(parts)),
        out_specs=(vmem,) * 3,
        compiler_params=pltpu.CompilerParams(vmem_limit_bytes=32 * 2**20),
        name="finish",
    )(table, *[x for part in parts for x in part])


def body(queries, keys, values, d_out, w_out, pattern, valid):
    n_seq, n_fsdp = lax.axis_size("seq"), lax.axis_size("fsdp")
    shard, group = lax.axis_index("seq"), lax.axis_index("fsdp")
    core = lax.rem(shard, 2)
    heads = queries.shape[2] // HD
    near = functools.partial(lax.ppermute, axis_name="seq", perm=swap(n_seq, 0))
    far = functools.partial(lax.ppermute, axis_name="seq", perm=swap(n_seq, 1))

    def flip(x, bit):
        return lax.ppermute(x, "fsdp", [(i, i ^ bit) for i in range(n_fsdp)])

    pipelined = n_fsdp == 4 and w_out.shape[0] == 2 * HD
    if pipelined:
        mine = lax.dynamic_slice_in_dim(w_out, core * HD, HD, 0)
        from_x = flip(mine, 1)
        from_y = flip(mine, 2)

    kv = jnp.concatenate([keys, values], axis=0)
    kv_core, kv_far = near(kv), far(kv)
    run = functools.partial(
        attention,
        pattern=pattern,
        valid=valid,
        q=queries,
        k=keys,
        v=values,
        kv_core=kv_core,
        kv_far=kv_far,
        d_out=d_out,
    )

    def part(weights, table):
        dq, own, to_core, to_far = run(weights, table)
        return dq, own, near(to_core), far(to_far)

    if pipelined:
        half = HD // 2
        diag = jnp.concatenate([flip(from_y[:half], 1), flip(from_x[half:], 2)], axis=0)
        g0, g1, g2, g3 = (2 * (group ^ bit) for bit in range(4))
        pair = lambda g, at: [[g + core, at + core], [g + 1 - core, at + 1 - core]]
        table = lambda rows: jnp.array(rows, jnp.int32)
        parts = [
            part([w_out], jnp.stack([jnp.stack([g0, 0 * g0]), jnp.stack([g0 + 1, 0 * g0 + 1])])),
            part(
                [from_x, near(from_x), from_y, near(from_y)],
                jnp.stack([jnp.stack(r) for r in pair(g1, 0) + pair(g2, 2)]),
            ),
            part([diag, near(diag)], jnp.stack([jnp.stack(r) for r in pair(g3, 0)])),
        ]
        places = jnp.stack([g0, g0 + 1, g1, g1 + 1, g2, g2 + 1, g3, g3 + 1])
    else:
        every = jnp.arange(heads, dtype=jnp.int32)
        full = lax.all_gather(w_out, "fsdp", axis=0, tiled=True)
        parts = [part([full], jnp.stack([every, every], axis=1))]
        places = every
    return finish(parts, places.astype(jnp.int32), queries.shape)


def solution(mesh):
    rows = P("fsdp", "seq", None)
    in_specs = (rows, rows, rows, rows, P("fsdp", None), P(), P("fsdp", None))
    return jax.shard_map(
        body, mesh=mesh, in_specs=in_specs, out_specs=(rows,) * 3, check_vma=False
    )
```

```python
import functools

import jax
import jax.numpy as jnp
from jax import lax
from jax.experimental import pallas as pl
from jax.experimental.pallas import tpu as pltpu
from jax.sharding import PartitionSpec as P

HD = 128
PAIR = 2 * HD
F32 = jnp.float32
BF16 = jnp.bfloat16
NT = (((1,), (1,)), ((), ()))
NN = (((1,), (0,)), ((), ()))
TN = (((0,), (0,)), ((), ()))
ANY = pl.BlockSpec(memory_space=pl.ANY)
VMEM = pl.BlockSpec(memory_space=pltpu.VMEM)
SMEM = pl.BlockSpec(memory_space=pltpu.SMEM)
PARAMS = pltpu.CompilerParams(vmem_limit_bytes=40 * 2**20)


def dot(a, b, dims):
    return lax.dot_general(a, b, dims, preferred_element_type=F32)


def swap(n, offset):
    pairs = []
    for i in range(offset, n - 1, 2):
        pairs += [(i, i + 1), (i + 1, i)]
    return pairs


def place():
    return lax.rem(lax.axis_index("seq"), 2), lax.axis_index("fsdp")


def run_copies(copies):
    for copy in copies:
        copy.start()
    for copy in copies:
        copy.wait()


def prep_kernel(w_ref, k_ref, v_ref, first_ref, second_ref, kv_ref, sems):
    core, _ = place()
    half = first_ref.shape[0]
    pairs = [
        (w_ref.at[pl.ds(pl.multiple_of(core * half, half), half), :], first_ref),
        (w_ref.at[pl.ds(pl.multiple_of((1 - core) * half, half), half), :], second_ref),
        (k_ref, kv_ref.at[pl.ds(0, 1)]),
        (v_ref, kv_ref.at[pl.ds(1, 1)]),
    ]
    run_copies([pltpu.make_async_copy(s, d, sems.at[i]) for i, (s, d) in enumerate(pairs)])


def prep(w_out, keys, values):
    half = jax.ShapeDtypeStruct((w_out.shape[0] // 2, w_out.shape[1]), BF16)
    return pl.pallas_call(
        prep_kernel,
        out_shape=(half, half, jax.ShapeDtypeStruct((2,) + keys.shape[1:], BF16)),
        in_specs=[ANY] * 3,
        out_specs=(ANY,) * 3,
        scratch_shapes=[pltpu.SemaphoreType.DMA((4,))],
        compiler_params=PARAMS,
        name="prep",
    )(w_out, keys, values)


def key_limits(pat_ref, val_ref):
    shard = lax.axis_index("seq")
    count = val_ref.shape[1]
    odd = lax.rem(shard, 2)
    blocks = (shard, shard + 1 - 2 * odd, shard - 1 + 2 * odd)
    limits = []
    for block in blocks:
        listed = pat_ref[shard, 0] == block
        for entry in range(1, pat_ref.shape[1]):
            listed = jnp.logical_or(listed, pat_ref[shard, entry] == block)
        inside = jnp.logical_and(block >= 0, block < count)
        held = val_ref[0, jnp.clip(block, 0, count - 1)]
        limits.append(jnp.where(jnp.logical_and(listed, inside), held, 0))
    return limits


def diagonal(x):
    zero = jnp.zeros((x.shape[0], HD), x.dtype)
    return jnp.concatenate(
        [
            jnp.concatenate([x[:, :HD], zero], axis=1),
            jnp.concatenate([zero, x[:, HD:]], axis=1),
        ],
        axis=0,
    )


def attention_kernel(chunks, pieces, pat_ref, val_ref, q_ref, k_ref, v_ref, core_ref, far_ref, dy_ref, *refs):
    core, group = place()
    slots = chunks(core, group)
    plan = pieces(core)
    n_w = len(refs) - 4 - 5
    w_refs = refs[:n_w]
    dq_ref, own_ref, to_core_ref, to_far_ref, dy, w, q, kv, sems = refs[n_w:]
    scale = HD ** (-0.5)
    tok = q.shape[1]
    copies = []

    def fetch(source, target):
        copy = pltpu.make_async_copy(source, target, sems.at[len(copies)])
        copy.start()
        copies.append(copy)
        return copy

    first = [fetch(dy_ref.at[0], dy)]
    waits = []
    for slot, (chunk, _) in enumerate(slots):
        wanted = [
            fetch(
                w_refs[index].at[pl.ds(row, rows), :],
                w.at[slot, pl.ds(to, rows), :],
            )
            for index, row, to, rows in plan[slot]
        ]
        cols = pl.ds(pl.multiple_of(chunk * PAIR, PAIR), PAIR)
        wanted.append(fetch(q_ref.at[0, :, cols], q.at[slot]))
        for side, source in enumerate((k_ref, v_ref)):
            wanted.append(fetch(source.at[0, :, cols], kv.at[slot, side, pl.ds(0, tok), :]))
            wanted.append(fetch(core_ref.at[side, :, cols], kv.at[slot, side, pl.ds(tok, tok), :]))
            wanted.append(fetch(far_ref.at[side, :, cols], kv.at[slot, side, pl.ds(2 * tok, tok), :]))
        waits.append(wanted)

    rows = lax.broadcasted_iota(jnp.int32, (tok, PAIR), 0)
    open_keys = jnp.concatenate([rows < limit for limit in key_limits(pat_ref, val_ref)], axis=0)
    for slot in range(len(slots)):
        for copy in first + waits[slot]:
            copy.wait()
        first = []
        cols = pl.ds(pl.multiple_of(slots[slot][1] * PAIR, PAIR), PAIR)
        d = diagonal(dot(dy[...], w[slot], NT).astype(BF16))
        qd = diagonal(q[slot])
        k, v = kv[slot, 0], kv[slot, 1]
        score = jnp.where(open_keys, dot(k, qd, NT) * scale, -jnp.inf)
        top = jnp.max(score, axis=0, keepdims=True)
        raised = jnp.exp(score - top)
        prob = raised * (1.0 / jnp.sum(raised, axis=0, keepdims=True))
        prob_b = prob.astype(BF16)
        d_prob = dot(v, d, NT)
        delta = jnp.sum(prob_b.astype(F32) * d_prob, axis=0, keepdims=True)
        d_score = (prob * (d_prob - delta)).astype(BF16)
        both = dot(d_score, k, TN) * scale
        dq_ref[:, cols] = jnp.concatenate([both[:tok, :HD], both[tok:, HD:]], axis=1).astype(BF16)
        for side, grad in enumerate((dot(d_score, qd, NN) * scale, dot(prob_b, d, NN))):
            own_ref[side, :, cols] = grad[:tok]
            to_core_ref[side, :, cols] = grad[tok : 2 * tok].astype(BF16)
            to_far_ref[side, :, cols] = grad[2 * tok :].astype(BF16)


def attention(name, chunks, pieces, weights, pattern, valid, q, k, v, kv_core, kv_far, d_out):
    count = len(chunks(0, 0))
    tok, depth = q.shape[1], d_out.shape[2]
    width = count * PAIR
    n_copies = 1 + sum(len(slot) + 7 for slot in pieces(0))
    return pl.pallas_call(
        functools.partial(attention_kernel, chunks, pieces),
        out_shape=(
            jax.ShapeDtypeStruct((tok, width), BF16),
            jax.ShapeDtypeStruct((2, tok, width), F32),
            jax.ShapeDtypeStruct((2, tok, width), BF16),
            jax.ShapeDtypeStruct((2, tok, width), BF16),
        ),
        in_specs=[SMEM] * 2 + [ANY] * (6 + len(weights)),
        out_specs=(VMEM,) * 4,
        scratch_shapes=[
            pltpu.VMEM((tok, depth), BF16),
            pltpu.VMEM((count, PAIR, depth), BF16),
            pltpu.VMEM((count, tok, PAIR), BF16),
            pltpu.VMEM((count, 2, 3 * tok, PAIR), BF16),
            pltpu.SemaphoreType.DMA((n_copies,)),
        ],
        cost_estimate=pl.CostEstimate(
            flops=count * 4 * tok * HD * (depth + 15 * HD),
            bytes_accessed=count * 1_800_000,
            transcendentals=count * 6 * tok * HD,
        ),
        compiler_params=PARAMS,
        name=name,
    )(pattern, valid, q, k, v, kv_core, kv_far, d_out, *weights)


def finish_kernel(chunks, n_parts, n_old, *refs):
    core, group = place()
    ins = refs[: 4 * n_parts]
    outs = refs[4 * n_parts + n_old : 4 * n_parts + n_old + 3]
    stage, sems = refs[-2:]
    tok = stage.shape[1]
    copies = []
    slot = 0
    for part in range(n_parts):
        dq, own, near, far = ins[4 * part : 4 * part + 4]
        for at in range(dq.shape[1] // PAIR):
            cols = slice(at * PAIR, (at + 1) * PAIR)
            chunk = chunks(core, group)[slot]
            dest = pl.ds(pl.multiple_of(chunk * PAIR, PAIR), PAIR)
            stage[3 * slot] = dq[:, cols]
            for side in range(2):
                total = own[side, :, cols] + near[side, :, cols].astype(F32)
                stage[3 * slot + 1 + side] = (total + far[side, :, cols].astype(F32)).astype(BF16)
            for index in range(3):
                copy = pltpu.make_async_copy(
                    stage.at[3 * slot + index], outs[index].at[0, :, dest], sems.at[3 * slot + index]
                )
                copy.start()
                copies.append(copy)
            slot += 1
    for copy in copies:
        copy.wait()


def finish(name, chunks, parts, shape, old=()):
    count = len(chunks(0, 0))
    ins = [x for part in parts for x in part]
    out = jax.ShapeDtypeStruct(shape, BF16)
    return pl.pallas_call(
        functools.partial(finish_kernel, chunks, len(parts), len(old)),
        out_shape=(out,) * 3,
        in_specs=[VMEM] * len(ins) + [ANY] * len(old),
        out_specs=(ANY,) * 3,
        scratch_shapes=[
            pltpu.VMEM((3 * count, shape[1], PAIR), BF16),
            pltpu.SemaphoreType.DMA((3 * count,)),
        ],
        input_output_aliases={len(ins) + i: i for i in range(len(old))},
        compiler_params=PARAMS,
        name=name,
    )(*ins, *old)


def body(queries, keys, values, d_out, w_out, pattern, valid):
    n_seq, n_fsdp = lax.axis_size("seq"), lax.axis_size("fsdp")
    n_chunks = queries.shape[2] // PAIR
    near = functools.partial(lax.ppermute, axis_name="seq", perm=swap(n_seq, 0))
    far = functools.partial(lax.ppermute, axis_name="seq", perm=swap(n_seq, 1))

    def cross(x, bits):
        pairs = [
            (s * n_fsdp + g, s * n_fsdp + (g ^ bits[s % 2]))
            for s in range(n_seq)
            for g in range(n_fsdp)
        ]
        return lax.ppermute(x, ("seq", "fsdp"), pairs)

    def part(name, chunks, pieces, weights, halo):
        dq, own, to_core, to_far = attention(
            name, chunks, pieces, weights, pattern, valid, queries, keys, values, *halo, d_out
        )
        return dq, own, near(to_core), far(to_far)

    first, second, kv = prep(w_out, keys, values)
    if n_fsdp == 4 and n_chunks == 4 and w_out.shape[0] == PAIR:
        got_a = cross(first, (1, 2))
        got_b = cross(second, (1, 2))
        halo = near(kv), far(kv)
        part_a = part("heads_own", lambda core, group: [(group, 0)], lambda core: [[(0, 0, 0, PAIR)]], [w_out], halo)
        got_d = cross(got_a, (2, 1))
        got_b, part_a = lax.optimization_barrier((got_b, part_a))
        halves = lambda first, at: [(first, 0, at * HD, HD), (first + 1, 0, (1 - at) * HD, HD)]
        part_b = part(
            "heads_side",
            lambda core, group: [(group ^ (1 + core), core), (group ^ (2 - core), 1 - core)],
            lambda core: [halves(0, core), halves(2, 1 - core)],
            [got_a, got_b, near(got_a), near(got_b)],
            halo,
        )
        part_c = part(
            "heads_far",
            lambda core, group: [(group ^ 3, 0)],
            lambda core: [halves(0, core)],
            [got_d, near(got_d)],
            halo,
        )
        ab = lambda core, group: [group, group ^ 1, group ^ 2]
        last = lambda core, group: [group ^ 3]
        old = finish("finish_first", ab, [part_a, part_b], queries.shape)
        return finish("finish_last", last, [part_c], queries.shape, old)
    full = lax.all_gather(w_out, "fsdp", axis=0, tiled=True)
    halo = near(kv), far(kv)
    chunks = lambda core, group: [(slot, slot) for slot in range(n_chunks)]
    order = lambda core, group: list(range(n_chunks))
    pieces = lambda core: [[(0, slot * PAIR, 0, PAIR)] for slot in range(n_chunks)]
    return finish("finish", order, [part("heads_all", chunks, pieces, [full], halo)], queries.shape)


def solution(mesh):
    rows = P("fsdp", "seq", None)
    in_specs = (rows, rows, rows, rows, P("fsdp", None), P(), P("fsdp", None))
    return jax.shard_map(
        body, mesh=mesh, in_specs=in_specs, out_specs=(rows,) * 3, check_vma=False
    )
```

```python
import functools

import jax
import jax.numpy as jnp
from jax import lax
from jax.experimental import pallas as pl
from jax.experimental.pallas import tpu as pltpu
from jax.sharding import PartitionSpec as P

HD = 128
PAIR = 2 * HD
F32 = jnp.float32
BF16 = jnp.bfloat16
NT = (((1,), (1,)), ((), ()))
NN = (((1,), (0,)), ((), ()))
TN = (((0,), (0,)), ((), ()))
HBM = pl.BlockSpec(memory_space=pltpu.HBM)
ANY = pl.BlockSpec(memory_space=pl.ANY)
VMEM = pl.BlockSpec(memory_space=pltpu.VMEM)
SMEM = pl.BlockSpec(memory_space=pltpu.SMEM)
PARAMS = pltpu.CompilerParams(vmem_limit_bytes=40 * 2**20)
WIDE = pltpu.CompilerParams(vmem_limit_bytes=58 * 2**20)


def dot(a, b, dims):
    return lax.dot_general(a, b, dims, preferred_element_type=F32)


def swap(n, offset):
    pairs = []
    for i in range(offset, n - 1, 2):
        pairs += [(i, i + 1), (i + 1, i)]
    return pairs


def place():
    return lax.rem(lax.axis_index("seq"), 2), lax.axis_index("fsdp")


def run_copies(copies):
    for copy in copies:
        copy.start()
    for copy in copies:
        copy.wait()


def prep_kernel(w_ref, k_ref, v_ref, first_ref, second_ref, kv_ref, sems):
    core, _ = place()
    half = first_ref.shape[0]
    pairs = [
        (w_ref.at[pl.ds(pl.multiple_of(core * half, half), half), :], first_ref),
        (w_ref.at[pl.ds(pl.multiple_of((1 - core) * half, half), half), :], second_ref),
        (k_ref, kv_ref.at[pl.ds(0, 1)]),
        (v_ref, kv_ref.at[pl.ds(1, 1)]),
    ]
    run_copies([pltpu.make_async_copy(s, d, sems.at[i]) for i, (s, d) in enumerate(pairs)])


def prep(w_out, keys, values):
    half = jax.ShapeDtypeStruct((w_out.shape[0] // 2, w_out.shape[1]), BF16)
    return pl.pallas_call(
        prep_kernel,
        out_shape=(half, half, jax.ShapeDtypeStruct((2,) + keys.shape[1:], BF16)),
        in_specs=[HBM] * 3,
        out_specs=(ANY,) * 3,
        scratch_shapes=[pltpu.SemaphoreType.DMA((4,))],
        compiler_params=WIDE,
        name="prep",
    )(w_out, keys, values)


def stage_kernel(dy_ref, q_ref, w_ref, turned_ref, q_out, w_rows, dy, sems):
    pairs = [(dy_ref.at[0], dy), (q_ref.at[0], q_out), (w_ref, w_rows)]
    copies = [pltpu.make_async_copy(s, d, sems.at[i]) for i, (s, d) in enumerate(pairs)]
    for copy in copies:
        copy.start()
    copies[0].wait()
    turned_ref[...] = dy[...].T
    for copy in copies[1:]:
        copy.wait()


def stage(d_out, queries, w_out):
    tok, depth = d_out.shape[1:]
    return pl.pallas_call(
        stage_kernel,
        out_shape=(
            jax.ShapeDtypeStruct((depth, tok), BF16),
            jax.ShapeDtypeStruct(queries.shape[1:], BF16),
            jax.ShapeDtypeStruct(w_out.shape, BF16),
        ),
        in_specs=[HBM] * 3,
        out_specs=(VMEM,) * 3,
        scratch_shapes=[pltpu.VMEM((tok, depth), BF16), pltpu.SemaphoreType.DMA((3,))],
        compiler_params=PARAMS,
        name="stage",
    )(d_out, queries, w_out)


def key_limits(pat_ref, val_ref):
    shard = lax.axis_index("seq")
    count = val_ref.shape[1]
    odd = lax.rem(shard, 2)
    blocks = (shard, shard + 1 - 2 * odd, shard - 1 + 2 * odd)
    limits = []
    for block in blocks:
        listed = pat_ref[shard, 0] == block
        for entry in range(1, pat_ref.shape[1]):
            listed = jnp.logical_or(listed, pat_ref[shard, entry] == block)
        inside = jnp.logical_and(block >= 0, block < count)
        held = val_ref[0, jnp.clip(block, 0, count - 1)]
        limits.append(jnp.where(jnp.logical_and(listed, inside), held, 0))
    return limits


def diagonal(x):
    zero = jnp.zeros((x.shape[0], HD), x.dtype)
    return jnp.concatenate(
        [
            jnp.concatenate([x[:, :HD], zero], axis=1),
            jnp.concatenate([zero, x[:, HD:]], axis=1),
        ],
        axis=0,
    )


def columns(chunk):
    return pl.ds(pl.multiple_of(chunk * PAIR, PAIR), PAIR)


def attention_kernel(steps, pat_ref, val_ref, dy_ref, q_ref, own_kv, core_kv, far_kv, *refs):
    core, group = place()
    w_refs = refs[:-4]
    dq_ref, own_ref, to_core_ref, to_far_ref = refs[-4:]
    scale = HD ** (-0.5)
    tok = q_ref.shape[0]
    rows = lax.broadcasted_iota(jnp.int32, (tok, PAIR), 0)
    open_keys = jnp.concatenate([rows < limit for limit in key_limits(pat_ref, val_ref)], axis=0)
    for chunk, slot, halves, lead in steps(core, group):
        cols, dest = columns(chunk), columns(slot)
        w = jnp.concatenate([w_refs[i][row : row + HD, :] for i, row in halves], axis=0)
        turned = dot(w, dy_ref[...], NN)
        one, two = turned[:HD], turned[HD:]
        if not isinstance(lead, int):
            one, two = jnp.where(lead == 0, one, two), jnp.where(lead == 0, two, one)
        zero = jnp.zeros_like(one)
        d = jnp.concatenate(
            [jnp.concatenate([one, zero], axis=1), jnp.concatenate([zero, two], axis=1)], axis=0
        ).astype(BF16)
        qd = diagonal(q_ref[:, cols])
        k, v = (
            jnp.concatenate([ref[side, :, cols] for ref in (own_kv, core_kv, far_kv)], axis=0)
            for side in range(2)
        )
        score = jnp.where(open_keys, dot(k, qd, NT) * scale, -jnp.inf)
        top = jnp.max(score, axis=0, keepdims=True)
        raised = jnp.exp(score - top)
        prob = raised * (1.0 / jnp.sum(raised, axis=0, keepdims=True))
        prob_b = prob.astype(BF16)
        d_prob = dot(v, d, NN)
        delta = jnp.sum(prob_b.astype(F32) * d_prob, axis=0, keepdims=True)
        d_score = (prob * (d_prob - delta)).astype(BF16)
        both = dot(d_score, k, TN) * scale
        dq_ref[:, dest] = jnp.concatenate([both[:tok, :HD], both[tok:, HD:]], axis=1).astype(BF16)
        for side, grad in enumerate((dot(d_score, qd, NN) * scale, dot(prob_b, d, NT))):
            own_ref[side, :, dest] = grad[:tok]
            to_core_ref[side, :, dest] = grad[tok : 2 * tok].astype(BF16)
            to_far_ref[side, :, dest] = grad[2 * tok :].astype(BF16)


def attention(name, steps, weights, pattern, valid, staged, halo):
    count = len(steps(0, 0))
    turned, q = staged
    depth, tok = turned.shape
    width = count * PAIR
    return pl.pallas_call(
        functools.partial(attention_kernel, steps),
        out_shape=(
            jax.ShapeDtypeStruct((tok, width), BF16),
            jax.ShapeDtypeStruct((2, tok, width), F32),
            jax.ShapeDtypeStruct((2, tok, width), BF16),
            jax.ShapeDtypeStruct((2, tok, width), BF16),
        ),
        in_specs=[SMEM] * 2 + [VMEM] * (5 + len(weights)),
        out_specs=(VMEM,) * 4,
        cost_estimate=pl.CostEstimate(
            flops=count * 4 * tok * HD * (depth + 15 * HD),
            bytes_accessed=count * 1_800_000,
            transcendentals=count * 6 * tok * HD,
        ),
        compiler_params=PARAMS,
        name=name,
    )(pattern, valid, turned, q, *halo, *weights)


def finish_kernel(chunks, n_parts, n_old, *refs):
    core, group = place()
    ins = refs[: 4 * n_parts]
    outs = refs[4 * n_parts + n_old : 4 * n_parts + n_old + 3]
    stage, sems = refs[-2:]
    tok = stage.shape[1]
    copies = []
    slot = 0
    for part in range(n_parts):
        dq, own, near, far = ins[4 * part : 4 * part + 4]
        for at in range(dq.shape[1] // PAIR):
            cols = slice(at * PAIR, (at + 1) * PAIR)
            chunk = chunks(core, group)[slot]
            dest = pl.ds(pl.multiple_of(chunk * PAIR, PAIR), PAIR)
            stage[3 * slot] = dq[:, cols]
            for side in range(2):
                total = own[side, :, cols] + near[side, :, cols].astype(F32)
                stage[3 * slot + 1 + side] = (total + far[side, :, cols].astype(F32)).astype(BF16)
            for index in range(3):
                copy = pltpu.make_async_copy(
                    stage.at[3 * slot + index], outs[index].at[0, :, dest], sems.at[3 * slot + index]
                )
                copy.start()
                copies.append(copy)
            slot += 1
    for copy in copies:
        copy.wait()


def finish(name, chunks, parts, shape, old=()):
    count = len(chunks(0, 0))
    ins = [x for part in parts for x in part]
    out = jax.ShapeDtypeStruct(shape, BF16)
    return pl.pallas_call(
        functools.partial(finish_kernel, chunks, len(parts), len(old)),
        out_shape=(out,) * 3,
        in_specs=[VMEM] * len(ins) + [ANY] * len(old),
        out_specs=(ANY,) * 3,
        scratch_shapes=[
            pltpu.VMEM((3 * count, shape[1], PAIR), BF16),
            pltpu.SemaphoreType.DMA((3 * count,)),
        ],
        input_output_aliases={len(ins) + i: i for i in range(len(old))},
        compiler_params=PARAMS,
        name=name,
    )(*ins, *old)


def body(queries, keys, values, d_out, w_out, pattern, valid):
    n_seq, n_fsdp = lax.axis_size("seq"), lax.axis_size("fsdp")
    n_chunks = queries.shape[2] // PAIR
    near = functools.partial(lax.ppermute, axis_name="seq", perm=swap(n_seq, 0))
    far = functools.partial(lax.ppermute, axis_name="seq", perm=swap(n_seq, 1))

    def cross(x, bits):
        pairs = [
            (s * n_fsdp + g, s * n_fsdp + (g ^ bits[s % 2]))
            for s in range(n_seq)
            for g in range(n_fsdp)
        ]
        return lax.ppermute(x, ("seq", "fsdp"), pairs)

    def part(name, steps, weights):
        dq, own, to_core, to_far = attention(name, steps, weights, pattern, valid, staged, halo)
        return dq, own, near(to_core), far(to_far)

    first, second, kv = prep(w_out, keys, values)
    *staged, w_rows = stage(d_out, queries, w_out)
    if n_fsdp == 4 and n_chunks == 4 and w_out.shape[0] == PAIR:
        second, *staged = lax.optimization_barrier((second, *staged))
        got_a = cross(first, (1, 2))
        got_b = cross(second, (1, 2))
        halo = kv, near(kv), far(kv)
        got_d = cross(got_a, (2, 1))
        part_a = part("heads_own", lambda core, group: [(group, 0, ((0, 0), (0, HD)), 0)], [w_rows])
        got_b, part_a = lax.optimization_barrier((got_b, part_a))
        part_b = part(
            "heads_side",
            lambda core, group: [
                (group ^ (1 + core), core, ((0, 0), (1, 0)), core),
                (group ^ (2 - core), 1 - core, ((2, 0), (3, 0)), 1 - core),
            ],
            [got_a, got_b, near(got_a), near(got_b)],
        )
        part_c = part(
            "heads_far",
            lambda core, group: [(group ^ 3, 0, ((0, 0), (1, 0)), core)],
            [got_d, near(got_d)],
        )
        ab = lambda core, group: [group, group ^ 1, group ^ 2]
        last = lambda core, group: [group ^ 3]
        old = finish("finish_first", ab, [part_a, part_b], queries.shape)
        return finish("finish_last", last, [part_c], queries.shape, old)
    full = lax.all_gather(w_out, "fsdp", axis=0, tiled=True)
    halo = kv, near(kv), far(kv)
    order = lambda core, group: list(range(n_chunks))
    steps = lambda core, group: [
        (i, i, ((0, i * PAIR), (0, i * PAIR + HD)), 0) for i in range(n_chunks)
    ]
    return finish("finish", order, [part("heads_all", steps, [full])], queries.shape)


def solution(mesh):
    rows = P("fsdp", "seq", None)
    in_specs = (rows, rows, rows, rows, P("fsdp", None), P(), P("fsdp", None))
    return jax.shard_map(
        body, mesh=mesh, in_specs=in_specs, out_specs=(rows,) * 3, check_vma=False
    )
```

```python
import functools

import jax
import jax.numpy as jnp
from jax import lax
from jax.experimental import pallas as pl
from jax.experimental.pallas import tpu as pltpu
from jax.sharding import PartitionSpec as P

HD = 128
PAIR = 2 * HD
PIECES = 2
BRIEF = pl.CostEstimate(flops=1, bytes_accessed=1, transcendentals=0)
F32 = jnp.float32
BF16 = jnp.bfloat16
NT = (((1,), (1,)), ((), ()))
NN = (((1,), (0,)), ((), ()))
TN = (((0,), (0,)), ((), ()))
HBM = pl.BlockSpec(memory_space=pltpu.HBM)
ANY = pl.BlockSpec(memory_space=pl.ANY)
VMEM = pl.BlockSpec(memory_space=pltpu.VMEM)
SMEM = pl.BlockSpec(memory_space=pltpu.SMEM)
PARAMS = pltpu.CompilerParams(vmem_limit_bytes=40 * 2**20)
WIDE = pltpu.CompilerParams(vmem_limit_bytes=58 * 2**20)


def dot(a, b, dims):
    return lax.dot_general(a, b, dims, preferred_element_type=F32)


def swap(n, offset):
    pairs = []
    for i in range(offset, n - 1, 2):
        pairs += [(i, i + 1), (i + 1, i)]
    return pairs


def place():
    return lax.rem(lax.axis_index("seq"), 2), lax.axis_index("fsdp")


def relay(pairs, buffers, sems):
    arrivals, moves = [], []
    for i, (source, target) in enumerate(pairs):
        arrivals.append(pltpu.make_async_copy(source, buffers[i], sems.at[0, i]))
        moves.append(pltpu.make_async_copy(buffers[i], target, sems.at[1, i]))
    for copy in arrivals:
        copy.start()
    for arrival, move in zip(arrivals, moves):
        arrival.wait()
        move.start()
    for move in moves:
        move.wait()


def half_rows(w_ref, half, which, piece):
    rows = half // PIECES
    start = pl.multiple_of(which * half + piece * rows, rows)
    return w_ref.at[pl.ds(start, rows), :]


def prep_kernel(w_ref, k_ref, v_ref, first_ref, second_ref, kv_ref, w_buffer, kv_buffer, sems):
    core, _ = place()
    half = first_ref.shape[0]
    rows = half // PIECES
    pairs, buffers = [], []
    for which, target in ((core, first_ref), (1 - core, second_ref)):
        for i in range(PIECES):
            pairs.append((half_rows(w_ref, half, which, i), target.at[pl.ds(i * rows, rows), :]))
            buffers.append(w_buffer.at[len(buffers)])
    pairs += [(k_ref.at[0], kv_ref.at[0]), (v_ref.at[0], kv_ref.at[1])]
    relay(pairs, buffers + [kv_buffer.at[0], kv_buffer.at[1]], sems)


def prep(w_out, keys, values):
    rows, depth = w_out.shape
    kv = (2,) + keys.shape[1:]
    half = jax.ShapeDtypeStruct((rows // 2, depth), BF16)
    return pl.pallas_call(
        prep_kernel,
        out_shape=(half, half, jax.ShapeDtypeStruct(kv, BF16)),
        in_specs=[HBM] * 3,
        out_specs=(ANY,) * 3,
        scratch_shapes=[
            pltpu.VMEM((2 * PIECES, rows // (2 * PIECES), depth), BF16),
            pltpu.VMEM(kv, BF16),
            pltpu.SemaphoreType.DMA((2, 2 + 2 * PIECES)),
        ],
        cost_estimate=BRIEF,
        compiler_params=WIDE,
        name="prep",
    )(w_out, keys, values)


def stage_kernel(dy_ref, q_ref, w_ref, turned_ref, q_out, w_rows, dy, sems):
    pairs = [(dy_ref.at[0], dy), (q_ref.at[0], q_out), (w_ref, w_rows)]
    copies = [pltpu.make_async_copy(s, d, sems.at[i]) for i, (s, d) in enumerate(pairs)]
    for copy in copies:
        copy.start()
    copies[0].wait()
    turned_ref[...] = dy[...].T
    for copy in copies[1:]:
        copy.wait()


def stage(d_out, queries, w_out):
    tok, depth = d_out.shape[1:]
    return pl.pallas_call(
        stage_kernel,
        out_shape=(
            jax.ShapeDtypeStruct((depth, tok), BF16),
            jax.ShapeDtypeStruct(queries.shape[1:], BF16),
            jax.ShapeDtypeStruct(w_out.shape, BF16),
        ),
        in_specs=[HBM] * 3,
        out_specs=(VMEM,) * 3,
        scratch_shapes=[pltpu.VMEM((tok, depth), BF16), pltpu.SemaphoreType.DMA((3,))],
        cost_estimate=BRIEF,
        compiler_params=PARAMS,
        name="stage",
    )(d_out, queries, w_out)


def key_limits(pat_ref, val_ref):
    shard = lax.axis_index("seq")
    count = val_ref.shape[1]
    odd = lax.rem(shard, 2)
    blocks = (shard, shard + 1 - 2 * odd, shard - 1 + 2 * odd)
    limits = []
    for block in blocks:
        listed = pat_ref[shard, 0] == block
        for entry in range(1, pat_ref.shape[1]):
            listed = jnp.logical_or(listed, pat_ref[shard, entry] == block)
        inside = jnp.logical_and(block >= 0, block < count)
        held = val_ref[0, jnp.clip(block, 0, count - 1)]
        limits.append(jnp.where(jnp.logical_and(listed, inside), held, 0))
    return limits


def diagonal(x):
    zero = jnp.zeros((x.shape[0], HD), x.dtype)
    return jnp.concatenate(
        [
            jnp.concatenate([x[:, :HD], zero], axis=1),
            jnp.concatenate([zero, x[:, HD:]], axis=1),
        ],
        axis=0,
    )


def columns(chunk):
    return pl.ds(pl.multiple_of(chunk * PAIR, PAIR), PAIR)


def attention_kernel(steps, pat_ref, val_ref, dy_ref, q_ref, own_kv, core_kv, far_kv, *refs):
    core, group = place()
    w_refs = refs[:-4]
    dq_ref, own_ref, to_core_ref, to_far_ref = refs[-4:]
    scale = HD ** (-0.5)
    tok = q_ref.shape[0]
    rows = lax.broadcasted_iota(jnp.int32, (tok, PAIR), 0)
    open_keys = jnp.concatenate([rows < limit for limit in key_limits(pat_ref, val_ref)], axis=0)
    for chunk, slot, halves, lead in steps(core, group):
        cols, dest = columns(chunk), columns(slot)
        w = jnp.concatenate([w_refs[i][row : row + HD, :] for i, row in halves], axis=0)
        turned = dot(w, dy_ref[...], NN)
        one, two = turned[:HD], turned[HD:]
        if not isinstance(lead, int):
            one, two = jnp.where(lead == 0, one, two), jnp.where(lead == 0, two, one)
        zero = jnp.zeros_like(one)
        d = jnp.concatenate(
            [jnp.concatenate([one, zero], axis=1), jnp.concatenate([zero, two], axis=1)], axis=0
        ).astype(BF16)
        qd = diagonal(q_ref[:, cols])
        k, v = (
            jnp.concatenate([ref[side, :, cols] for ref in (own_kv, core_kv, far_kv)], axis=0)
            for side in range(2)
        )
        score = jnp.where(open_keys, dot(k, qd, NT) * scale, -jnp.inf)
        top = jnp.max(score, axis=0, keepdims=True)
        raised = jnp.exp(score - top)
        prob = raised * (1.0 / jnp.sum(raised, axis=0, keepdims=True))
        prob_b = prob.astype(BF16)
        d_prob = dot(v, d, NN)
        delta = jnp.sum(prob_b.astype(F32) * d_prob, axis=0, keepdims=True)
        d_score = (prob * (d_prob - delta)).astype(BF16)
        both = dot(d_score, k, TN) * scale
        dq_ref[:, dest] = jnp.concatenate([both[:tok, :HD], both[tok:, HD:]], axis=1).astype(BF16)
        for side, grad in enumerate((dot(d_score, qd, NN) * scale, dot(prob_b, d, NT))):
            own_ref[side, :, dest] = grad[:tok]
            to_core_ref[side, :, dest] = grad[tok : 2 * tok].astype(BF16)
            to_far_ref[side, :, dest] = grad[2 * tok :].astype(BF16)


def attention(name, steps, weights, pattern, valid, staged, halo):
    count = len(steps(0, 0))
    turned, q = staged
    depth, tok = turned.shape
    width = count * PAIR
    return pl.pallas_call(
        functools.partial(attention_kernel, steps),
        out_shape=(
            jax.ShapeDtypeStruct((tok, width), BF16),
            jax.ShapeDtypeStruct((2, tok, width), F32),
            jax.ShapeDtypeStruct((2, tok, width), BF16),
            jax.ShapeDtypeStruct((2, tok, width), BF16),
        ),
        in_specs=[SMEM] * 2 + [VMEM] * (5 + len(weights)),
        out_specs=(VMEM,) * 4,
        cost_estimate=BRIEF,
        compiler_params=PARAMS,
        name=name,
    )(pattern, valid, turned, q, *halo, *weights)


def finish_kernel(chunks, n_parts, n_old, *refs):
    core, group = place()
    ins = refs[: 4 * n_parts]
    outs = refs[4 * n_parts + n_old : 4 * n_parts + n_old + 3]
    stage, sems = refs[-2:]
    tok = stage.shape[1]
    copies = []
    slot = 0
    for part in range(n_parts):
        dq, own, near, far = ins[4 * part : 4 * part + 4]
        for at in range(dq.shape[1] // PAIR):
            cols = slice(at * PAIR, (at + 1) * PAIR)
            chunk = chunks(core, group)[slot]
            dest = pl.ds(pl.multiple_of(chunk * PAIR, PAIR), PAIR)
            stage[3 * slot] = dq[:, cols]
            for side in range(2):
                total = own[side, :, cols] + near[side, :, cols].astype(F32)
                stage[3 * slot + 1 + side] = (total + far[side, :, cols].astype(F32)).astype(BF16)
            for index in range(3):
                copy = pltpu.make_async_copy(
                    stage.at[3 * slot + index], outs[index].at[0, :, dest], sems.at[3 * slot + index]
                )
                copy.start()
                copies.append(copy)
            slot += 1
    for copy in copies:
        copy.wait()


def finish(name, chunks, parts, shape, old=()):
    count = len(chunks(0, 0))
    ins = [x for part in parts for x in part]
    out = jax.ShapeDtypeStruct(shape, BF16)
    return pl.pallas_call(
        functools.partial(finish_kernel, chunks, len(parts), len(old)),
        out_shape=(out,) * 3,
        in_specs=[VMEM] * len(ins) + [ANY] * len(old),
        out_specs=(ANY,) * 3,
        scratch_shapes=[
            pltpu.VMEM((3 * count, shape[1], PAIR), BF16),
            pltpu.SemaphoreType.DMA((3 * count,)),
        ],
        input_output_aliases={len(ins) + i: i for i in range(len(old))},
        cost_estimate=BRIEF,
        compiler_params=PARAMS,
        name=name,
    )(*ins, *old)


def body(queries, keys, values, d_out, w_out, pattern, valid):
    n_seq, n_fsdp = lax.axis_size("seq"), lax.axis_size("fsdp")
    n_chunks = queries.shape[2] // PAIR
    near = functools.partial(lax.ppermute, axis_name="seq", perm=swap(n_seq, 0))
    far = functools.partial(lax.ppermute, axis_name="seq", perm=swap(n_seq, 1))

    def cross(x, bits):
        pairs = [
            (s * n_fsdp + g, s * n_fsdp + (g ^ bits[s % 2]))
            for s in range(n_seq)
            for g in range(n_fsdp)
        ]
        return lax.ppermute(x, ("seq", "fsdp"), pairs)

    def part(name, steps, weights):
        dq, own, to_core, to_far = attention(name, steps, weights, pattern, valid, staged, halo)
        back = far(to_far)
        return dq, own, near(to_core), back

    first, second, kv = prep(w_out, keys, values)
    *staged, w_rows = stage(d_out, queries, w_out)
    if n_fsdp == 4 and n_chunks == 4 and w_out.shape[0] == PAIR:
        second, *staged = lax.optimization_barrier((second, *staged))
        got_a = cross(first, (1, 2))
        got_b = cross(second, (1, 2))
        kv_far = far(kv)
        halo = kv, near(kv), kv_far
        got_d = cross(got_a, (2, 1))
        part_a = part("heads_own", lambda core, group: [(group, 0, ((0, 0), (0, HD)), 0)], [w_rows])
        got_b, dq = lax.optimization_barrier((got_b, part_a[0]))
        part_a = (dq,) + part_a[1:]
        part_b = part(
            "heads_side",
            lambda core, group: [
                (group ^ (1 + core), core, ((0, 0), (1, 0)), core),
                (group ^ (2 - core), 1 - core, ((2, 0), (3, 0)), 1 - core),
            ],
            [got_a, got_b, near(got_a), near(got_b)],
        )
        part_c = part(
            "heads_far",
            lambda core, group: [(group ^ 3, 0, ((0, 0), (1, 0)), core)],
            [got_d, near(got_d)],
        )
        ab = lambda core, group: [group, group ^ 1, group ^ 2]
        last = lambda core, group: [group ^ 3]
        old = finish("finish_first", ab, [part_a, part_b], queries.shape)
        return finish("finish_last", last, [part_c], queries.shape, old)
    full = lax.all_gather(w_out, "fsdp", axis=0, tiled=True)
    halo = kv, near(kv), far(kv)
    order = lambda core, group: list(range(n_chunks))
    steps = lambda core, group: [
        (i, i, ((0, i * PAIR), (0, i * PAIR + HD)), 0) for i in range(n_chunks)
    ]
    return finish("finish", order, [part("heads_all", steps, [full])], queries.shape)


def solution(mesh):
    rows = P("fsdp", "seq", None)
    in_specs = (rows, rows, rows, rows, P("fsdp", None), P(), P("fsdp", None))
    return jax.shard_map(
        body, mesh=mesh, in_specs=in_specs, out_specs=(rows,) * 3, check_vma=False
    )
```

```python
import functools

import jax
import jax.numpy as jnp
from jax import lax
from jax.experimental import pallas as pl
from jax.experimental.pallas import tpu as pltpu
from jax.sharding import PartitionSpec as P

HD = 128
PAIR = 2 * HD
BRIEF = pl.CostEstimate(flops=1, bytes_accessed=1, transcendentals=0)
F32 = jnp.float32
BF16 = jnp.bfloat16
NT = (((1,), (1,)), ((), ()))
NN = (((1,), (0,)), ((), ()))
TN = (((0,), (0,)), ((), ()))
HBM = pl.BlockSpec(memory_space=pltpu.HBM)
ANY = pl.BlockSpec(memory_space=pl.ANY)
VMEM = pl.BlockSpec(memory_space=pltpu.VMEM)
SMEM = pl.BlockSpec(memory_space=pltpu.SMEM)
PARAMS = pltpu.CompilerParams(vmem_limit_bytes=40 * 2**20)
WIDE = pltpu.CompilerParams(vmem_limit_bytes=58 * 2**20)


def dot(a, b, dims):
    return lax.dot_general(a, b, dims, preferred_element_type=F32)


def swap(n, offset):
    pairs = []
    for i in range(offset, n - 1, 2):
        pairs += [(i, i + 1), (i + 1, i)]
    return pairs


def place():
    return lax.rem(lax.axis_index("seq"), 2), lax.axis_index("fsdp")


def relay(pairs, buffers, sems):
    arrivals, moves = [], []
    for i, (source, target) in enumerate(pairs):
        arrivals.append(pltpu.make_async_copy(source, buffers[i], sems.at[0, i]))
        moves.append(pltpu.make_async_copy(buffers[i], target, sems.at[1, i]))
    for copy in arrivals:
        copy.start()
    for arrival, move in zip(arrivals, moves):
        arrival.wait()
        move.start()
    for move in moves:
        move.wait()


def join_kernel(k_ref, v_ref, kv_ref, buffer, sems):
    relay([(k_ref.at[0], kv_ref.at[0]), (v_ref.at[0], kv_ref.at[1])], [buffer.at[0], buffer.at[1]], sems)


def join(keys, values):
    shape = (2,) + keys.shape[1:]
    return pl.pallas_call(
        join_kernel,
        out_shape=jax.ShapeDtypeStruct(shape, BF16),
        in_specs=[HBM] * 2,
        out_specs=ANY,
        scratch_shapes=[pltpu.VMEM(shape, BF16), pltpu.SemaphoreType.DMA((2, 2))],
        cost_estimate=BRIEF,
        compiler_params=WIDE,
        name="join",
    )(keys, values)


def onward_kernel(w_ref, out_ref):
    core, _ = place()
    half = out_ref.shape[0]
    out_ref[...] = w_ref[pl.ds(pl.multiple_of(core * half, half), half), :]


def onward(got):
    return pl.pallas_call(
        onward_kernel,
        out_shape=jax.ShapeDtypeStruct((got.shape[0] // 2, got.shape[1]), BF16),
        in_specs=[VMEM],
        out_specs=VMEM,
        cost_estimate=BRIEF,
        compiler_params=PARAMS,
        name="onward",
    )(got)


def stage_kernel(dy_ref, q_ref, w_ref, turned_ref, q_out, w_rows, dy, sems):
    pairs = [(dy_ref.at[0], dy), (q_ref.at[0], q_out), (w_ref, w_rows)]
    copies = [pltpu.make_async_copy(s, d, sems.at[i]) for i, (s, d) in enumerate(pairs)]
    for copy in copies:
        copy.start()
    copies[0].wait()
    turned_ref[...] = dy[...].T
    for copy in copies[1:]:
        copy.wait()


def stage(d_out, queries, w_out):
    tok, depth = d_out.shape[1:]
    return pl.pallas_call(
        stage_kernel,
        out_shape=(
            jax.ShapeDtypeStruct((depth, tok), BF16),
            jax.ShapeDtypeStruct(queries.shape[1:], BF16),
            jax.ShapeDtypeStruct(w_out.shape, BF16),
        ),
        in_specs=[HBM] * 3,
        out_specs=(VMEM,) * 3,
        scratch_shapes=[pltpu.VMEM((tok, depth), BF16), pltpu.SemaphoreType.DMA((3,))],
        cost_estimate=BRIEF,
        compiler_params=PARAMS,
        name="stage",
    )(d_out, queries, w_out)


def key_limits(pat_ref, val_ref):
    shard = lax.axis_index("seq")
    count = val_ref.shape[1]
    odd = lax.rem(shard, 2)
    blocks = (shard, shard + 1 - 2 * odd, shard - 1 + 2 * odd)
    limits = []
    for block in blocks:
        listed = pat_ref[shard, 0] == block
        for entry in range(1, pat_ref.shape[1]):
            listed = jnp.logical_or(listed, pat_ref[shard, entry] == block)
        inside = jnp.logical_and(block >= 0, block < count)
        held = val_ref[0, jnp.clip(block, 0, count - 1)]
        limits.append(jnp.where(jnp.logical_and(listed, inside), held, 0))
    return limits


def diagonal(x):
    zero = jnp.zeros((x.shape[0], HD), x.dtype)
    return jnp.concatenate(
        [
            jnp.concatenate([x[:, :HD], zero], axis=1),
            jnp.concatenate([zero, x[:, HD:]], axis=1),
        ],
        axis=0,
    )


def columns(chunk):
    return pl.ds(pl.multiple_of(chunk * PAIR, PAIR), PAIR)


def attention_kernel(steps, carried, pat_ref, val_ref, dy_ref, q_ref, own_kv, core_kv, far_kv, *refs):
    core, group = place()
    w_refs, earlier, outs = refs[: -4 - carried], refs[-4 - carried : -4], refs[-4:]
    dq_ref, own_ref, to_core_ref, to_far_ref = outs
    for old, out in zip(earlier, outs):
        out[..., : old.shape[-1]] = old[...]
    scale = HD ** (-0.5)
    tok = q_ref.shape[0]
    rows = lax.broadcasted_iota(jnp.int32, (tok, PAIR), 0)
    open_keys = jnp.concatenate([rows < limit for limit in key_limits(pat_ref, val_ref)], axis=0)
    for chunk, slot, halves, lead in steps(core, group):
        cols, dest = columns(chunk), columns(slot)
        w = jnp.concatenate([w_refs[i][row : row + HD, :] for i, row in halves], axis=0)
        turned = dot(w, dy_ref[...], NN)
        one, two = turned[:HD], turned[HD:]
        if not isinstance(lead, int):
            one, two = jnp.where(lead == 0, one, two), jnp.where(lead == 0, two, one)
        zero = jnp.zeros_like(one)
        d = jnp.concatenate(
            [jnp.concatenate([one, zero], axis=1), jnp.concatenate([zero, two], axis=1)], axis=0
        ).astype(BF16)
        qd = diagonal(q_ref[:, cols])
        k, v = (
            jnp.concatenate([ref[side, :, cols] for ref in (own_kv, core_kv, far_kv)], axis=0)
            for side in range(2)
        )
        score = jnp.where(open_keys, dot(k, qd, NT) * scale, -jnp.inf)
        top = jnp.max(score, axis=0, keepdims=True)
        raised = jnp.exp(score - top)
        prob = raised * (1.0 / jnp.sum(raised, axis=0, keepdims=True))
        prob_b = prob.astype(BF16)
        d_prob = dot(v, d, NN)
        delta = jnp.sum(prob_b.astype(F32) * d_prob, axis=0, keepdims=True)
        d_score = (prob * (d_prob - delta)).astype(BF16)
        both = dot(d_score, k, TN) * scale
        dq_ref[:, dest] = jnp.concatenate([both[:tok, :HD], both[tok:, HD:]], axis=1).astype(BF16)
        for side, grad in enumerate((dot(d_score, qd, NN) * scale, dot(prob_b, d, NT))):
            own_ref[side, :, dest] = grad[:tok]
            to_core_ref[side, :, dest] = grad[tok : 2 * tok].astype(BF16)
            to_far_ref[side, :, dest] = grad[2 * tok :].astype(BF16)


def attention(name, steps, weights, earlier, pattern, valid, staged, halo):
    count = len(steps(0, 0))
    turned, q = staged
    depth, tok = turned.shape
    width = count * PAIR + (earlier[0].shape[1] if earlier else 0)
    return pl.pallas_call(
        functools.partial(attention_kernel, steps, len(earlier)),
        out_shape=(
            jax.ShapeDtypeStruct((tok, width), BF16),
            jax.ShapeDtypeStruct((2, tok, width), F32),
            jax.ShapeDtypeStruct((2, tok, width), BF16),
            jax.ShapeDtypeStruct((2, tok, width), BF16),
        ),
        in_specs=[SMEM] * 2 + [VMEM] * (5 + len(weights) + len(earlier)),
        out_specs=(VMEM,) * 4,
        cost_estimate=BRIEF,
        compiler_params=PARAMS,
        name=name,
    )(pattern, valid, turned, q, *halo, *weights, *earlier)


def finish_kernel(chunks, n_parts, n_old, *refs):
    core, group = place()
    ins = refs[: 4 * n_parts]
    outs = refs[4 * n_parts + n_old : 4 * n_parts + n_old + 3]
    stage, sems = refs[-2:]
    tok = stage.shape[1]
    copies = []
    slot = 0
    for part in range(n_parts):
        dq, own, near, far = ins[4 * part : 4 * part + 4]
        for at in range(dq.shape[1] // PAIR):
            cols = slice(at * PAIR, (at + 1) * PAIR)
            chunk = chunks(core, group)[slot]
            dest = pl.ds(pl.multiple_of(chunk * PAIR, PAIR), PAIR)
            stage[3 * slot] = dq[:, cols]
            for side in range(2):
                total = own[side, :, cols] + near[side, :, cols].astype(F32)
                stage[3 * slot + 1 + side] = (total + far[side, :, cols].astype(F32)).astype(BF16)
            for index in range(3):
                copy = pltpu.make_async_copy(
                    stage.at[3 * slot + index], outs[index].at[0, :, dest], sems.at[3 * slot + index]
                )
                copy.start()
                copies.append(copy)
            slot += 1
    for copy in copies:
        copy.wait()


def finish(name, chunks, parts, shape, old=()):
    count = len(chunks(0, 0))
    ins = [x for part in parts for x in part]
    out = jax.ShapeDtypeStruct(shape, BF16)
    return pl.pallas_call(
        functools.partial(finish_kernel, chunks, len(parts), len(old)),
        out_shape=(out,) * 3,
        in_specs=[VMEM] * len(ins) + [ANY] * len(old),
        out_specs=(ANY,) * 3,
        scratch_shapes=[
            pltpu.VMEM((3 * count, shape[1], PAIR), BF16),
            pltpu.SemaphoreType.DMA((3 * count,)),
        ],
        input_output_aliases={len(ins) + i: i for i in range(len(old))},
        cost_estimate=BRIEF,
        compiler_params=PARAMS,
        name=name,
    )(*ins, *old)


def body(queries, keys, values, d_out, w_out, pattern, valid):
    n_seq, n_fsdp = lax.axis_size("seq"), lax.axis_size("fsdp")
    n_chunks = queries.shape[2] // PAIR
    near = functools.partial(lax.ppermute, axis_name="seq", perm=swap(n_seq, 0))
    far = functools.partial(lax.ppermute, axis_name="seq", perm=swap(n_seq, 1))

    def cross(x, bits):
        pairs = [
            (s * n_fsdp + g, s * n_fsdp + (g ^ bits[s % 2]))
            for s in range(n_seq)
            for g in range(n_fsdp)
        ]
        return lax.ppermute(x, ("seq", "fsdp"), pairs)

    def heads(name, steps, weights, earlier=()):
        return attention(name, steps, weights, earlier, pattern, valid, staged, halo)

    def exchange(part):
        dq, own, to_core, to_far = part
        back = far(to_far)
        return dq, own, near(to_core), back

    kv = join(keys, values)
    *staged, w_rows = stage(d_out, queries, w_out)
    if n_fsdp == 4 and n_chunks == 4 and w_out.shape[0] == PAIR:
        got = cross(w_out, (1, 2))
        kv_far = far(kv)
        halo = kv, near(kv), kv_far
        part = heads("heads_own", lambda core, group: [(group, 0, ((0, 0), (0, HD)), 0)], [w_rows])
        got, dq = lax.optimization_barrier((got, part[0]))
        part = (dq, *part[1:])
        got_d = cross(onward(got), (2, 1))
        part = heads(
            "heads_side",
            lambda core, group: [
                (group ^ (1 + core), 1 + core, ((0, 0), (0, HD)), 0),
                (group ^ (2 - core), 2 - core, ((1, 0), (1, HD)), 0),
            ],
            [got, near(got)],
            part,
        )
        got_d, dq = lax.optimization_barrier((got_d, part[0]))
        sums = exchange((dq, *part[1:]))
        last_sums = exchange(
            heads(
                "heads_far",
                lambda core, group: [(group ^ 3, 0, ((0, 0), (1, 0)), core)],
                [got_d, near(got_d)],
            )
        )
        ab = lambda core, group: [group, group ^ 1, group ^ 2]
        last = lambda core, group: [group ^ 3]
        old = finish("finish_first", ab, [sums], queries.shape)
        return finish("finish_last", last, [last_sums], queries.shape, old)
    full = lax.all_gather(w_out, "fsdp", axis=0, tiled=True)
    halo = kv, near(kv), far(kv)
    order = lambda core, group: list(range(n_chunks))
    steps = lambda core, group: [
        (i, i, ((0, i * PAIR), (0, i * PAIR + HD)), 0) for i in range(n_chunks)
    ]
    return finish("finish", order, [exchange(heads("heads_all", steps, [full]))], queries.shape)


def solution(mesh):
    rows = P("fsdp", "seq", None)
    in_specs = (rows, rows, rows, rows, P("fsdp", None), P(), P("fsdp", None))
    return jax.shard_map(
        body, mesh=mesh, in_specs=in_specs, out_specs=(rows,) * 3, check_vma=False
    )
```

```python
import functools

import jax
import jax.numpy as jnp
from jax import lax
from jax.experimental import pallas as pl
from jax.experimental.pallas import tpu as pltpu
from jax.sharding import PartitionSpec as P

HD = 128
PAIR = 2 * HD
BRIEF = pl.CostEstimate(flops=1, bytes_accessed=1, transcendentals=0)
F32 = jnp.float32
BF16 = jnp.bfloat16
NT = (((1,), (1,)), ((), ()))
NN = (((1,), (0,)), ((), ()))
TN = (((0,), (0,)), ((), ()))
HBM = pl.BlockSpec(memory_space=pltpu.HBM)
ANY = pl.BlockSpec(memory_space=pl.ANY)
VMEM = pl.BlockSpec(memory_space=pltpu.VMEM)
SMEM = pl.BlockSpec(memory_space=pltpu.SMEM)
PARAMS = pltpu.CompilerParams(vmem_limit_bytes=40 * 2**20)
WIDE = pltpu.CompilerParams(vmem_limit_bytes=58 * 2**20)


def dot(a, b, dims):
    return lax.dot_general(a, b, dims, preferred_element_type=F32)


def swap(n, offset):
    pairs = []
    for i in range(offset, n - 1, 2):
        pairs += [(i, i + 1), (i + 1, i)]
    return pairs


def place():
    return lax.rem(lax.axis_index("seq"), 2), lax.axis_index("fsdp")


def relay(pairs, buffers, sems):
    arrivals, moves = [], []
    for i, (source, target) in enumerate(pairs):
        arrivals.append(pltpu.make_async_copy(source, buffers[i], sems.at[0, i]))
        moves.append(pltpu.make_async_copy(buffers[i], target, sems.at[1, i]))
    for copy in arrivals:
        copy.start()
    for arrival, move in zip(arrivals, moves):
        arrival.wait()
        move.start()
    for move in moves:
        move.wait()


def join_kernel(k_ref, v_ref, kv_ref, buffer, sems):
    relay([(k_ref.at[0], kv_ref.at[0]), (v_ref.at[0], kv_ref.at[1])], [buffer.at[0], buffer.at[1]], sems)


def join(keys, values):
    shape = (2,) + keys.shape[1:]
    return pl.pallas_call(
        join_kernel,
        out_shape=jax.ShapeDtypeStruct(shape, BF16),
        in_specs=[HBM] * 2,
        out_specs=ANY,
        scratch_shapes=[pltpu.VMEM(shape, BF16), pltpu.SemaphoreType.DMA((2, 2))],
        cost_estimate=BRIEF,
        compiler_params=WIDE,
        name="join",
    )(keys, values)


def onward_kernel(w_ref, out_ref):
    core, _ = place()
    half = out_ref.shape[0]
    out_ref[...] = w_ref[pl.ds(pl.multiple_of(core * half, half), half), :]


def onward(got):
    return pl.pallas_call(
        onward_kernel,
        out_shape=jax.ShapeDtypeStruct((got.shape[0] // 2, got.shape[1]), BF16),
        in_specs=[VMEM],
        out_specs=VMEM,
        cost_estimate=BRIEF,
        compiler_params=PARAMS,
        name="onward",
    )(got)


def key_limits(pat_ref, val_ref):
    shard = lax.axis_index("seq")
    count = val_ref.shape[1]
    odd = lax.rem(shard, 2)
    blocks = (shard, shard + 1 - 2 * odd, shard - 1 + 2 * odd)
    limits = []
    for block in blocks:
        listed = pat_ref[shard, 0] == block
        for entry in range(1, pat_ref.shape[1]):
            listed = jnp.logical_or(listed, pat_ref[shard, entry] == block)
        inside = jnp.logical_and(block >= 0, block < count)
        held = val_ref[0, jnp.clip(block, 0, count - 1)]
        limits.append(jnp.where(jnp.logical_and(listed, inside), held, 0))
    return limits


def stage_kernel(pat_ref, val_ref, dy_ref, q_ref, turned_ref, q_out, limit_ref, dy, sems):
    copies = [
        pltpu.make_async_copy(dy_ref.at[0], dy, sems.at[0]),
        pltpu.make_async_copy(q_ref.at[0], q_out, sems.at[1]),
    ]
    for copy in copies:
        copy.start()
    limit_ref[...] = jnp.zeros_like(limit_ref)
    for row, limit in enumerate(key_limits(pat_ref, val_ref)):
        limit_ref[row : row + 1, :] = jnp.full((1, PAIR), limit, jnp.int32)
    copies[0].wait()
    turned_ref[...] = dy[...].T
    copies[1].wait()


def stage(d_out, queries, pattern, valid):
    tok, depth = d_out.shape[1:]
    return pl.pallas_call(
        stage_kernel,
        out_shape=(
            jax.ShapeDtypeStruct((depth, tok), BF16),
            jax.ShapeDtypeStruct(queries.shape[1:], BF16),
            jax.ShapeDtypeStruct((8, PAIR), jnp.int32),
        ),
        in_specs=[SMEM] * 2 + [HBM] * 2,
        out_specs=(VMEM,) * 3,
        scratch_shapes=[pltpu.VMEM((tok, depth), BF16), pltpu.SemaphoreType.DMA((2,))],
        cost_estimate=BRIEF,
        compiler_params=PARAMS,
        name="stage",
    )(pattern, valid, d_out, queries)


def diagonal(x):
    zero = jnp.zeros((x.shape[0], HD), x.dtype)
    return jnp.concatenate(
        [
            jnp.concatenate([x[:, :HD], zero], axis=1),
            jnp.concatenate([zero, x[:, HD:]], axis=1),
        ],
        axis=0,
    )


def columns(chunk):
    return pl.ds(pl.multiple_of(chunk * PAIR, PAIR), PAIR)


def attention_kernel(steps, carried, dy_ref, q_ref, limit_ref, own_kv, core_kv, far_kv, *refs):
    core, group = place()
    w_refs, earlier, outs = refs[: -4 - carried], refs[-4 - carried : -4], refs[-4:]
    dq_ref, own_ref, to_core_ref, to_far_ref = outs
    for old, out in zip(earlier, outs):
        out[..., : old.shape[-1]] = old[...]
    scale = HD ** (-0.5)
    tok = q_ref.shape[0]
    rows = lax.broadcasted_iota(jnp.int32, (tok, PAIR), 0)
    open_keys = jnp.concatenate([rows < limit_ref[i : i + 1, :] for i in range(3)], axis=0)
    for chunk, slot, halves, lead in steps(core, group):
        cols, dest = columns(chunk), columns(slot)
        w = jnp.concatenate([w_refs[i][row : row + HD, :] for i, row in halves], axis=0)
        turned = dot(w, dy_ref[...], NN)
        one, two = turned[:HD], turned[HD:]
        if not isinstance(lead, int):
            one, two = jnp.where(lead == 0, one, two), jnp.where(lead == 0, two, one)
        zero = jnp.zeros_like(one)
        d = jnp.concatenate(
            [jnp.concatenate([one, zero], axis=1), jnp.concatenate([zero, two], axis=1)], axis=0
        ).astype(BF16)
        qd = diagonal(q_ref[:, cols])
        k, v = (
            jnp.concatenate([ref[side, :, cols] for ref in (own_kv, core_kv, far_kv)], axis=0)
            for side in range(2)
        )
        score = jnp.where(open_keys, dot(k, qd, NT) * scale, -jnp.inf)
        top = jnp.max(score, axis=0, keepdims=True)
        raised = jnp.exp(score - top)
        prob = raised * (1.0 / jnp.sum(raised, axis=0, keepdims=True))
        prob_b = prob.astype(BF16)
        d_prob = dot(v, d, NN)
        delta = jnp.sum(prob_b.astype(F32) * d_prob, axis=0, keepdims=True)
        d_score = (prob * (d_prob - delta)).astype(BF16)
        both = dot(d_score, k, TN) * scale
        dq_ref[:, dest] = jnp.concatenate([both[:tok, :HD], both[tok:, HD:]], axis=1).astype(BF16)
        for side, grad in enumerate((dot(d_score, qd, NN) * scale, dot(prob_b, d, NT))):
            own_ref[side, :, dest] = grad[:tok]
            to_core_ref[side, :, dest] = grad[tok : 2 * tok].astype(BF16)
            to_far_ref[side, :, dest] = grad[2 * tok :].astype(BF16)


def attention(name, steps, weights, earlier, staged, halo):
    count = len(steps(0, 0))
    tok = staged[0].shape[1]
    width = count * PAIR + (earlier[0].shape[1] if earlier else 0)
    return pl.pallas_call(
        functools.partial(attention_kernel, steps, len(earlier)),
        out_shape=(
            jax.ShapeDtypeStruct((tok, width), BF16),
            jax.ShapeDtypeStruct((2, tok, width), F32),
            jax.ShapeDtypeStruct((2, tok, width), BF16),
            jax.ShapeDtypeStruct((2, tok, width), BF16),
        ),
        in_specs=[VMEM] * (6 + len(weights) + len(earlier)),
        out_specs=(VMEM,) * 4,
        cost_estimate=BRIEF,
        compiler_params=PARAMS,
        name=name,
    )(*staged, *halo, *weights, *earlier)


def finish_kernel(chunks, n_parts, n_old, *refs):
    core, group = place()
    ins = refs[: 4 * n_parts]
    outs = refs[4 * n_parts + n_old : 4 * n_parts + n_old + 3]
    stage, sems = refs[-2:]
    tok = stage.shape[1]
    copies = []
    slot = 0
    for part in range(n_parts):
        dq, own, near, far = ins[4 * part : 4 * part + 4]
        for at in range(dq.shape[1] // PAIR):
            cols = slice(at * PAIR, (at + 1) * PAIR)
            chunk = chunks(core, group)[slot]
            dest = pl.ds(pl.multiple_of(chunk * PAIR, PAIR), PAIR)
            stage[3 * slot] = dq[:, cols]
            for side in range(2):
                total = own[side, :, cols] + near[side, :, cols].astype(F32)
                stage[3 * slot + 1 + side] = (total + far[side, :, cols].astype(F32)).astype(BF16)
            for index in range(3):
                copy = pltpu.make_async_copy(
                    stage.at[3 * slot + index], outs[index].at[0, :, dest], sems.at[3 * slot + index]
                )
                copy.start()
                copies.append(copy)
            slot += 1
    for copy in copies:
        copy.wait()


def finish(name, chunks, parts, shape, old=()):
    count = len(chunks(0, 0))
    ins = [x for part in parts for x in part]
    out = jax.ShapeDtypeStruct(shape, BF16)
    return pl.pallas_call(
        functools.partial(finish_kernel, chunks, len(parts), len(old)),
        out_shape=(out,) * 3,
        in_specs=[VMEM] * len(ins) + [ANY] * len(old),
        out_specs=(ANY,) * 3,
        scratch_shapes=[
            pltpu.VMEM((3 * count, shape[1], PAIR), BF16),
            pltpu.SemaphoreType.DMA((3 * count,)),
        ],
        input_output_aliases={len(ins) + i: i for i in range(len(old))},
        cost_estimate=BRIEF,
        compiler_params=PARAMS,
        name=name,
    )(*ins, *old)


def body(queries, keys, values, d_out, w_out, pattern, valid):
    n_seq, n_fsdp = lax.axis_size("seq"), lax.axis_size("fsdp")
    n_chunks = queries.shape[2] // PAIR
    near = functools.partial(lax.ppermute, axis_name="seq", perm=swap(n_seq, 0))
    far = functools.partial(lax.ppermute, axis_name="seq", perm=swap(n_seq, 1))

    def cross(x, bits):
        pairs = [
            (s * n_fsdp + g, s * n_fsdp + (g ^ bits[s % 2]))
            for s in range(n_seq)
            for g in range(n_fsdp)
        ]
        return lax.ppermute(x, ("seq", "fsdp"), pairs)

    def heads(name, steps, weights, earlier=()):
        return attention(name, steps, weights, earlier, staged, halo)

    def exchange(part):
        dq, own, to_core, to_far = part
        back = far(to_far)
        return dq, own, near(to_core), back

    kv = join(keys, values)
    staged = stage(d_out, queries, pattern, valid)
    if n_fsdp == 4 and n_chunks == 4 and w_out.shape[0] == PAIR:
        got = cross(w_out, (1, 2))
        early = got, kv, near(kv), far(kv), *staged
        got, *early = lax.optimization_barrier(early)
        halo, staged = early[:3], early[3:]
        got_d = cross(onward(got), (2, 1))
        part = heads("heads_own", lambda core, group: [(group, 0, ((0, 0), (0, HD)), 0)], [w_out])
        part = heads(
            "heads_side",
            lambda core, group: [
                (group ^ (1 + core), 1 + core, ((0, 0), (0, HD)), 0),
                (group ^ (2 - core), 2 - core, ((1, 0), (1, HD)), 0),
            ],
            [got, near(got)],
            part,
        )
        got_d, dq = lax.optimization_barrier((got_d, part[0]))
        sums = exchange((dq, *part[1:]))
        last_sums = exchange(
            heads(
                "heads_far",
                lambda core, group: [(group ^ 3, 0, ((0, 0), (1, 0)), core)],
                [got_d, near(got_d)],
            )
        )
        ab = lambda core, group: [group, group ^ 1, group ^ 2]
        last = lambda core, group: [group ^ 3]
        old = finish("finish_first", ab, [sums], queries.shape)
        return finish("finish_last", last, [last_sums], queries.shape, old)
    full = lax.all_gather(w_out, "fsdp", axis=0, tiled=True)
    halo = kv, near(kv), far(kv)
    order = lambda core, group: list(range(n_chunks))
    steps = lambda core, group: [
        (i, i, ((0, i * PAIR), (0, i * PAIR + HD)), 0) for i in range(n_chunks)
    ]
    return finish("finish", order, [exchange(heads("heads_all", steps, [full]))], queries.shape)


def solution(mesh):
    rows = P("fsdp", "seq", None)
    in_specs = (rows, rows, rows, rows, P("fsdp", None), P(), P("fsdp", None))
    return jax.shard_map(
        body, mesh=mesh, in_specs=in_specs, out_specs=(rows,) * 3, check_vma=False
    )
```

```python
import functools

import jax
import jax.numpy as jnp
from jax import lax
from jax.experimental import pallas as pl
from jax.experimental.pallas import tpu as pltpu
from jax.sharding import PartitionSpec as P

HD = 128
PAIR = 2 * HD
EXTRA = 16
PIECE = 64
BRIEF = pl.CostEstimate(flops=1, bytes_accessed=1, transcendentals=0)
F32 = jnp.float32
BF16 = jnp.bfloat16
NT = (((1,), (1,)), ((), ()))
NN = (((1,), (0,)), ((), ()))
TN = (((0,), (0,)), ((), ()))
HBM = pl.BlockSpec(memory_space=pltpu.HBM)
ANY = pl.BlockSpec(memory_space=pl.ANY)
VMEM = pl.BlockSpec(memory_space=pltpu.VMEM)
SMEM = pl.BlockSpec(memory_space=pltpu.SMEM)
PARAMS = pltpu.CompilerParams(vmem_limit_bytes=40 * 2**20)
WIDE = pltpu.CompilerParams(vmem_limit_bytes=58 * 2**20)
SCALE = HD ** (-0.5)


def dot(a, b, dims):
    return lax.dot_general(a, b, dims, preferred_element_type=F32)


def swap(n, offset):
    pairs = []
    for i in range(offset, n - 1, 2):
        pairs += [(i, i + 1), (i + 1, i)]
    return pairs


def place():
    return lax.rem(lax.axis_index("seq"), 2), lax.axis_index("fsdp")


def columns(chunk):
    return pl.ds(pl.multiple_of(chunk * PAIR, PAIR), PAIR)


def call(kernel, name, out_shape, in_specs, out_specs, scratch, *args):
    return pl.pallas_call(
        kernel,
        out_shape=out_shape,
        in_specs=in_specs,
        out_specs=out_specs,
        scratch_shapes=scratch,
        cost_estimate=BRIEF,
        compiler_params=PARAMS,
        name=name,
    )(*args)


def key_limits(pat_ref, val_ref):
    shard = lax.axis_index("seq")
    count = val_ref.shape[1]
    odd = lax.rem(shard, 2)
    blocks = (shard, shard + 1 - 2 * odd, shard - 1 + 2 * odd)
    limits = []
    for row, block in [(shard, block) for block in blocks] + [(block, shard) for block in blocks[1:]]:
        held = jnp.clip(row, 0, count - 1)
        listed = pat_ref[held, 0] == block
        for entry in range(1, pat_ref.shape[1]):
            listed = jnp.logical_or(listed, pat_ref[held, entry] == block)
        inside = jnp.logical_and(row == held, jnp.logical_and(block >= 0, block < count))
        keys = val_ref[0, jnp.clip(block, 0, count - 1)]
        limits.append(jnp.where(jnp.logical_and(listed, inside), keys, 0))
    return limits


def pack_kernel(last, pat_ref, val_ref, dy_ref, q_ref, limit_ref, both_ref):
    core, group = place()
    depth = dy_ref.shape[2]
    limit_ref[...] = jnp.zeros_like(limit_ref)
    for row, limit in enumerate(key_limits(pat_ref, val_ref)):
        limit_ref[row : row + 1, :] = jnp.full((1, PAIR), limit, jnp.int32)
    both_ref[:, :depth] = dy_ref[0]
    both_ref[:, depth:] = q_ref[0, :, columns(last(core, group))]


def pack(last, pattern, valid, d_out, queries):
    tok, depth = d_out.shape[1:]
    return call(
        functools.partial(pack_kernel, last),
        "pack",
        (
            jax.ShapeDtypeStruct((8, PAIR), jnp.int32),
            jax.ShapeDtypeStruct((tok, depth + PAIR), BF16),
        ),
        [SMEM] * 2 + [VMEM] * 2,
        (VMEM,) * 2,
        [],
        pattern,
        valid,
        d_out,
        queries,
    )


def join_kernel(k_ref, v_ref, kv_ref, buffer, sems):
    arrivals, moves = [], []
    for side, ref in enumerate((k_ref, v_ref)):
        for row in range(0, ref.shape[1], PIECE):
            rows = pl.ds(row, PIECE)
            held, i = buffer.at[side, rows, :], len(moves)
            arrivals.append(pltpu.make_async_copy(ref.at[0, rows, :], held, sems.at[0, i]))
            moves.append(pltpu.make_async_copy(held, kv_ref.at[side, rows, :], sems.at[1, i]))
    for copy in arrivals:
        copy.start()
    for arrival, move in zip(arrivals, moves):
        arrival.wait()
        move.start()
    for move in moves:
        move.wait()


def join(keys, values):
    shape = (2,) + keys.shape[1:]
    copies = 2 * (shape[1] // PIECE)
    return pl.pallas_call(
        join_kernel,
        out_shape=jax.ShapeDtypeStruct(shape, BF16),
        in_specs=[HBM] * 2,
        out_specs=ANY,
        scratch_shapes=[pltpu.VMEM(shape, BF16), pltpu.SemaphoreType.DMA((2, copies))],
        cost_estimate=BRIEF,
        compiler_params=WIDE,
        name="join",
    )(keys, values)


def onward_kernel(w_ref, *out_refs):
    core, _ = place()
    half = w_ref.shape[0] // 2
    start = pl.multiple_of(core * half, half)
    for i, ref in enumerate(out_refs[:2]):
        rows = ref.shape[0]
        ref[...] = w_ref[pl.ds(start + i * rows, rows), :]
    for ref, first in zip(out_refs[2:], (start, half - start)):
        ref[...] = w_ref[pl.ds(pl.multiple_of(first, half), half), :]


def onward(got):
    rows, depth = got.shape
    shapes = [jax.ShapeDtypeStruct((rows // part, depth), BF16) for part in (4, 4, 2, 2)]
    return call(onward_kernel, "onward", tuple(shapes), [VMEM], (VMEM,) * 4, [], got)


def diagonal(x):
    zero = jnp.zeros((x.shape[0], HD), x.dtype)
    return jnp.concatenate(
        [
            jnp.concatenate([x[:, :HD], zero], axis=1),
            jnp.concatenate([zero, x[:, HD:]], axis=1),
        ],
        axis=0,
    )


def diagonal_turned(one, two):
    zero = jnp.zeros_like(one)
    return jnp.concatenate(
        [jnp.concatenate([one, zero], axis=1), jnp.concatenate([zero, two], axis=1)], axis=0
    )


def in_order(rows, lead):
    one, two = rows[:HD], rows[HD:]
    if isinstance(lead, int):
        return (one, two) if lead == 0 else (two, one)
    return jnp.where(lead == 0, one, two), jnp.where(lead == 0, two, one)


def key_mask(limit_ref, rows, first, count):
    index = lax.broadcasted_iota(jnp.int32, (rows, PAIR), 0)
    return jnp.concatenate(
        [index < limit_ref[i : i + 1, :] for i in range(first, first + count)], axis=0
    )


def softmax(k, qd, open_keys):
    score = jnp.where(open_keys, dot(k, qd, NT) * SCALE, -jnp.inf)
    top = jnp.max(score, axis=0, keepdims=True)
    raised = jnp.exp(score - top)
    total = jnp.sum(raised, axis=0, keepdims=True)
    return raised * (1.0 / total), top, total


def stacked(refs, side, cols):
    return jnp.concatenate([ref[side, :, cols] for ref in refs], axis=0)


def heads_kernel(steps, last, dy_ref, q_ref, limit_ref, *refs):
    core, group = place()
    kv_refs, w_refs = refs[:3], refs[3:-4]
    dq_ref, own_ref, to_core_ref, to_far_ref = refs[-4:]
    tok = q_ref.shape[1]
    open_keys = key_mask(limit_ref, tok, 0, 3)
    todo = steps(core, group)
    for chunk, slot, pieces, lead in todo:
        cols, dest = columns(chunk), columns(slot)
        w = jnp.concatenate([w_refs[i][row : row + rows, :] for i, row, rows in pieces], axis=0)
        d = diagonal_turned(*in_order(dot(w, dy_ref[0], NT).astype(BF16), lead))
        qd = diagonal(q_ref[0, :, cols])
        k, v = stacked(kv_refs, 0, cols), stacked(kv_refs, 1, cols)
        prob, _, _ = softmax(k, qd, open_keys)
        prob_b = prob.astype(BF16)
        d_prob = dot(v, d, NN)
        delta = jnp.sum(prob_b.astype(F32) * d_prob, axis=0, keepdims=True)
        d_score = (prob * (d_prob - delta)).astype(BF16)
        both = dot(d_score, k, TN) * SCALE
        dq_ref[:, dest] = jnp.concatenate([both[:tok, :HD], both[tok:, HD:]], axis=1).astype(BF16)
        for side, grad in enumerate((dot(d_score, qd, NN) * SCALE, dot(prob_b, d, NT))):
            own_ref[side, :, dest] = grad[:tok]
            to_core_ref[side, :tok, dest] = grad[tok : 2 * tok].astype(BF16)
            to_far_ref[side, :tok, dest] = grad[2 * tok :].astype(BF16)
    for ref in (to_core_ref, to_far_ref):
        ref[:, tok:, : len(todo) * PAIR] = jnp.zeros((2, EXTRA, len(todo) * PAIR), BF16)
    if last is not None:
        cols = columns(last(core, group))
        prob, top, total = softmax(stacked(kv_refs, 0, cols), diagonal(q_ref[0, :, cols]), open_keys)
        out = dot(stacked(kv_refs, 1, cols), prob.astype(BF16), TN)
        lse = top + jnp.log(total)
        place_ = slice(len(todo) * PAIR, len(todo) * PAIR + HD)
        for head in range(2):
            span = slice(head * HD, (head + 1) * HD)
            rest = lse[:, span]
            terms = []
            for _ in range(3):
                terms.append(rest.astype(BF16))
                rest = rest - terms[-1].astype(F32)
            terms.append(jnp.zeros((EXTRA - 3, HD), BF16))
            tail = jnp.concatenate(terms, axis=0)
            for ref in (to_core_ref, to_far_ref):
                ref[head, :tok, place_] = out[span, span].astype(BF16)
                ref[head, tok:, place_] = tail


def heads(name, steps, last, weights, d_out, q, limits, blocks):
    tok = q.shape[1]
    width = len(steps(0, 0)) * PAIR
    message = (2, tok + EXTRA, width if last is None else width + HD)
    return call(
        functools.partial(heads_kernel, steps, last),
        name,
        (
            jax.ShapeDtypeStruct((tok, width), BF16),
            jax.ShapeDtypeStruct((2, tok, width), F32),
            jax.ShapeDtypeStruct(message, BF16),
            jax.ShapeDtypeStruct(message, BF16),
        ),
        [VMEM] * (6 + len(weights)),
        (VMEM,) * 4,
        [],
        d_out,
        q,
        limits,
        *blocks,
        *weights,
    )


def last_kernel(last, dy_ref, q_ref, limit_ref, *refs):
    core, group = place()
    kv_refs = refs[:3]
    near_dy, far_dy, near_message, far_message, *w_refs, dq_ref, dk_ref, dv_ref = refs[3:]
    tok, depth = q_ref.shape[1], dy_ref.shape[2]
    cols = columns(last(core, group))
    w = jnp.concatenate([ref[...] for ref in w_refs], axis=0)
    dy = jnp.concatenate([dy_ref[0], near_dy[:, :depth], far_dy[:, :depth]], axis=0)
    turned = in_order(dot(w, dy, NT).astype(BF16), core)

    def of(block):
        span = slice(block * tok, (block + 1) * tok)
        return [half[:, span] for half in turned]

    k, v = stacked(kv_refs, 0, cols), stacked(kv_refs, 1, cols)
    qd = diagonal(q_ref[0, :, cols])
    d = diagonal_turned(*of(0))
    prob, _, _ = softmax(k, qd, key_mask(limit_ref, tok, 0, 3))
    prob_b = prob.astype(BF16)
    d_prob = dot(v, d, NN)
    delta = jnp.sum(prob_b.astype(F32) * d_prob, axis=0, keepdims=True)
    d_score = (prob * (d_prob - delta)).astype(BF16)
    both = dot(d_score, k, TN) * SCALE
    dq_ref[...] = jnp.concatenate([both[:tok, :HD], both[tok:, HD:]], axis=1).astype(BF16)
    scores, probs, queries, cotangents = [d_score[:tok]], [prob_b[:tok]], [qd], [d]
    for block, (dy_far, message) in enumerate(((near_dy, near_message), (far_dy, far_message)), 1):
        qd = diagonal(dy_far[:, depth:])
        one, two = of(block)
        d = diagonal_turned(one, two)
        at = slice(message.shape[2] - HD, message.shape[2])
        lse = jnp.concatenate(
            [
                sum(message[head, tok + term : tok + term + 1, at].astype(F32) for term in range(3))
                for head in range(2)
            ],
            axis=1,
        )
        delta = jnp.concatenate(
            [
                jnp.sum(t.astype(F32) * message[head, :tok, at].astype(F32), axis=0, keepdims=True)
                for head, t in enumerate((one, two))
            ],
            axis=1,
        )
        score = dot(k[:tok], qd, NT) * SCALE
        score = jnp.where(key_mask(limit_ref, tok, 2 + block, 1), score, -jnp.inf)
        prob = jnp.exp(score - lse)
        scores.append((prob * (dot(v[:tok], d, NN) - delta)).astype(BF16))
        probs.append(prob.astype(BF16))
        queries.append(qd)
        cotangents.append(d)
    scores, probs = jnp.concatenate(scores, axis=1), jnp.concatenate(probs, axis=1)
    dk_ref[...] = (dot(scores, jnp.concatenate(queries, axis=0), NN) * SCALE).astype(BF16)
    dv_ref[...] = dot(probs, jnp.concatenate(cotangents, axis=1), NT).astype(BF16)


def last_heads(last, d_out, q, limits, blocks, halo, messages, weights):
    tok = q.shape[1]
    return call(
        functools.partial(last_kernel, last),
        "heads_last",
        (jax.ShapeDtypeStruct((tok, PAIR), BF16),) * 3,
        [VMEM] * (10 + len(weights)),
        (VMEM,) * 3,
        [],
        d_out,
        q,
        limits,
        *blocks,
        *halo,
        *messages,
        *weights,
    )


def finish_kernel(chunks, widths, *refs):
    core, group = place()
    outs, stage, sems = refs[-5:-2], refs[-2], refs[-1]
    tok = stage.shape[1]
    copies = []
    slot = at = 0
    for width, summed in widths:
        part = refs[at : at + (3 if summed else 4)]
        at += len(part)
        for step in range(width // PAIR):
            cols = slice(step * PAIR, (step + 1) * PAIR)
            dest = columns(chunks(core, group)[slot])
            stage[3 * slot] = part[0][:, cols]
            for side in range(2):
                if summed:
                    total = part[1 + side][:, cols]
                else:
                    _, own, near, far = part
                    total = own[side, :, cols] + near[side, :tok, cols].astype(F32)
                    total = (total + far[side, :tok, cols].astype(F32)).astype(BF16)
                stage[3 * slot + 1 + side] = total
            for index in range(3):
                copy = pltpu.make_async_copy(
                    stage.at[3 * slot + index], outs[index].at[0, :, dest], sems.at[3 * slot + index]
                )
                copy.start()
                copies.append(copy)
            slot += 1
    for copy in copies:
        copy.wait()


def finish(chunks, parts, shape):
    count = len(chunks(0, 0))
    ins = [x for part in parts for x in part]
    widths = tuple((part[0].shape[1], len(part) == 3) for part in parts)
    return call(
        functools.partial(finish_kernel, chunks, widths),
        "finish",
        (jax.ShapeDtypeStruct(shape, BF16),) * 3,
        [VMEM] * len(ins),
        (ANY,) * 3,
        [
            pltpu.VMEM((3 * count, shape[1], PAIR), BF16),
            pltpu.SemaphoreType.DMA((3 * count,)),
        ],
        *ins,
    )


def body(queries, keys, values, d_out, w_out, pattern, valid):
    n_seq, n_fsdp = lax.axis_size("seq"), lax.axis_size("fsdp")
    n_chunks = queries.shape[2] // PAIR
    near = functools.partial(lax.ppermute, axis_name="seq", perm=swap(n_seq, 0))
    far = functools.partial(lax.ppermute, axis_name="seq", perm=swap(n_seq, 1))

    def cross(x, bits):
        pairs = [
            (s * n_fsdp + g, s * n_fsdp + (g ^ bits[s % 2]))
            for s in range(n_seq)
            for g in range(n_fsdp)
        ]
        return lax.ppermute(x, ("seq", "fsdp"), pairs)

    def exchange(part):
        dq, own, to_core, to_far = part
        back = far(to_far)
        return dq, own, near(to_core), back

    kv = join(keys, values)
    far_kv, near_kv = far(kv), near(kv)
    if n_fsdp == 4 and n_chunks == 4 and w_out.shape[0] == PAIR:
        last = lambda core, group: group ^ 3
        got = cross(w_out, (1, 2))
        limits, both = pack(last, pattern, valid, d_out, queries)
        far_both, near_both = far(both), near(both)
        ours = d_out, queries, limits, (kv, near_kv, far_kv)
        own = heads(
            "heads_own",
            lambda core, group: [(group, 0, ((0, 0, PAIR),), 0)],
            last,
            [w_out],
            *ours,
        )
        got, dq, near_both = lax.optimization_barrier((got, own[0], near_both))
        own = exchange((dq, *own[1:]))
        *pieces, mine, other = onward(got)
        got_d = [cross(piece, (2, 1)) for piece in pieces]
        far_both, near_got = lax.optimization_barrier((far_both, (near(mine), near(other))))
        side = heads(
            "heads_side",
            lambda core, group: [
                (group ^ (1 + core), core, ((0, 0, HD), (0, HD, HD)), 0),
                (
                    group ^ (2 - core),
                    1 - core,
                    ((1, 0, HD), (2, 0, HD)),
                    1 - core,
                ),
            ],
            None,
            [got, *near_got],
            *ours,
        )
        got_d, dq, messages = lax.optimization_barrier((got_d, side[0], own[2:]))
        own = (*own[:2], *messages)
        side = exchange((dq, *side[1:]))
        third = last_heads(last, *ours, (near_both, far_both), messages, (*got_d, *[near(x) for x in got_d]))
        order = lambda core, group: [group, group ^ 1, group ^ 2, group ^ 3]
        return finish(order, [own, side, third], queries.shape)
    full = lax.all_gather(w_out, "fsdp", axis=0, tiled=True)
    limits, _ = pack(lambda core, group: 0, pattern, valid, d_out, queries)
    steps = lambda core, group: [
        (i, i, ((0, i * PAIR, PAIR),), 0) for i in range(n_chunks)
    ]
    ours = d_out, queries, limits, (kv, near_kv, far_kv)
    part = exchange(heads("heads_all", steps, None, [full], *ours))
    return finish(lambda core, group: list(range(n_chunks)), [part], queries.shape)


def solution(mesh):
    rows = P("fsdp", "seq", None)
    in_specs = (rows, rows, rows, rows, P("fsdp", None), P(), P("fsdp", None))
    return jax.shard_map(
        body, mesh=mesh, in_specs=in_specs, out_specs=(rows,) * 3, check_vma=False
    )
```

```python
import functools

import jax
import jax.numpy as jnp
from jax import lax
from jax.experimental import pallas as pl
from jax.experimental.pallas import tpu as pltpu
from jax.sharding import PartitionSpec as P

HD = 128
PAIR = 2 * HD
PIECE = 64
BRIEF = pl.CostEstimate(flops=1, bytes_accessed=1, transcendentals=0)
F32 = jnp.float32
BF16 = jnp.bfloat16
NT = (((1,), (1,)), ((), ()))
NN = (((1,), (0,)), ((), ()))
TN = (((0,), (0,)), ((), ()))
HBM = pl.BlockSpec(memory_space=pltpu.HBM)
ANY = pl.BlockSpec(memory_space=pl.ANY)
VMEM = pl.BlockSpec(memory_space=pltpu.VMEM)
SMEM = pl.BlockSpec(memory_space=pltpu.SMEM)
PARAMS = pltpu.CompilerParams(vmem_limit_bytes=40 * 2**20)
WIDE = pltpu.CompilerParams(vmem_limit_bytes=58 * 2**20)
SCALE = HD ** (-0.5)


def dot(a, b, dims):
    return lax.dot_general(a, b, dims, preferred_element_type=F32)


def swap(n, offset):
    pairs = []
    for i in range(offset, n - 1, 2):
        pairs += [(i, i + 1), (i + 1, i)]
    return pairs


def place():
    return lax.rem(lax.axis_index("seq"), 2), lax.axis_index("fsdp")


def columns(chunk):
    return pl.ds(pl.multiple_of(chunk * PAIR, PAIR), PAIR)


def call(kernel, name, out_shape, in_specs, out_specs, scratch, *args):
    return pl.pallas_call(
        kernel,
        out_shape=out_shape,
        in_specs=in_specs,
        out_specs=out_specs,
        scratch_shapes=scratch,
        cost_estimate=BRIEF,
        compiler_params=PARAMS,
        name=name,
    )(*args)


def key_limits(pat_ref, val_ref):
    shard = lax.axis_index("seq")
    count = val_ref.shape[1]

    def pair(block):
        return block + 1 - 2 * lax.rem(block + 2, 2)

    def far(block):
        return block - 1 + 2 * lax.rem(block + 2, 2)

    wanted = [(shard, block) for block in (shard, pair(shard), far(shard))]
    for row, other in ((pair(shard), far(pair(shard))), (far(shard), pair(far(shard)))):
        wanted += [(row, block) for block in (row, shard, other)]
    limits = []
    for row, block in wanted:
        held = jnp.clip(row, 0, count - 1)
        listed = pat_ref[held, 0] == block
        for entry in range(1, pat_ref.shape[1]):
            listed = jnp.logical_or(listed, pat_ref[held, entry] == block)
        inside = jnp.logical_and(row == held, jnp.logical_and(block >= 0, block < count))
        keys = val_ref[0, jnp.clip(block, 0, count - 1)]
        limits.append(jnp.where(jnp.logical_and(listed, inside), keys, 0))
    return limits


def limits_kernel(pat_ref, val_ref, limit_ref):
    limit_ref[...] = jnp.zeros_like(limit_ref)
    for row, limit in enumerate(key_limits(pat_ref, val_ref)):
        limit_ref[row : row + 1, :] = jnp.full((1, PAIR), limit, jnp.int32)


def limits_of(pattern, valid):
    shape = jax.ShapeDtypeStruct((16, PAIR), jnp.int32)
    return call(limits_kernel, "limits", shape, [SMEM] * 2, VMEM, [], pattern, valid)


def join_kernel(last, k_ref, v_ref, dy_ref, q_ref, kv_ref, both_ref, kv, both, sems):
    core, group = place()
    tok, depth = dy_ref.shape[1:]
    width = k_ref.shape[2]
    steps = []
    for sources, held, target in (
        (((k_ref, slice(None), width), (v_ref, slice(None), width)), kv, kv_ref),
        (
            ((dy_ref, slice(None), depth), (q_ref, columns(last(core, group)), PAIR)),
            both,
            both_ref,
        ),
    ):
        for row in range(0, tok, PIECE):
            rows = pl.ds(row, PIECE)
            to = 0
            for source, cols, size in sources:
                at = (rows, pl.ds(to, size))
                steps.append((source.at[0, rows, cols], held.at[at], target.at[at]))
                to += size
    arrivals, moves = [], []
    for i, (source, held, target) in enumerate(steps):
        arrivals.append(pltpu.make_async_copy(source, held, sems.at[0, i]))
        moves.append(pltpu.make_async_copy(held, target, sems.at[1, i]))
    for copy in arrivals:
        copy.start()
    for arrival, move in zip(arrivals, moves):
        arrival.wait()
        move.start()
    for move in moves:
        move.wait()


def join(last, keys, values, d_out, queries):
    tok, depth = d_out.shape[1:]
    kv, both = (tok, 2 * keys.shape[2]), (tok, depth + PAIR)
    return pl.pallas_call(
        functools.partial(join_kernel, last),
        out_shape=(jax.ShapeDtypeStruct(kv, BF16), jax.ShapeDtypeStruct(both, BF16)),
        in_specs=[HBM] * 4,
        out_specs=(ANY,) * 2,
        scratch_shapes=[
            pltpu.VMEM(kv, BF16),
            pltpu.VMEM(both, BF16),
            pltpu.SemaphoreType.DMA((2, 4 * (tok // PIECE))),
        ],
        cost_estimate=BRIEF,
        compiler_params=WIDE,
        name="join",
    )(keys, values, d_out, queries)


def hand_on_kernel(last, *refs):
    core, group = place()
    *before, kv_ref, out_ref = refs
    chunk = last(core, group)
    cols = [columns(chunk), columns(chunk + kv_ref.shape[1] // (2 * PAIR))]
    to = 0
    for piece in [ref[...] for ref in before] + [kv_ref[:, at] for at in cols]:
        out_ref[:, to : to + piece.shape[1]] = piece
        to += piece.shape[1]


def hand_on(name, last, kv, *before):
    width = sum(x.shape[1] for x in before) + 2 * PAIR
    shape = jax.ShapeDtypeStruct((kv.shape[0], width), BF16)
    kernel = functools.partial(hand_on_kernel, last)
    return call(kernel, name, shape, [VMEM] * (len(before) + 1), VMEM, [], *before, kv)


def onward_kernel(w_ref, *out_refs):
    core, _ = place()
    half = w_ref.shape[0] // 2
    start = pl.multiple_of(core * half, half)
    for i, ref in enumerate(out_refs[:2]):
        rows = ref.shape[0]
        ref[...] = w_ref[pl.ds(start + i * rows, rows), :]
    for ref, first in zip(out_refs[2:], (start, half - start)):
        ref[...] = w_ref[pl.ds(pl.multiple_of(first, half), half), :]


def onward(got):
    rows, depth = got.shape
    shapes = [jax.ShapeDtypeStruct((rows // part, depth), BF16) for part in (4, 4, 2, 2)]
    return call(onward_kernel, "onward", tuple(shapes), [VMEM], (VMEM,) * 4, [], got)


def diagonal(x):
    zero = jnp.zeros((x.shape[0], HD), x.dtype)
    return jnp.concatenate(
        [
            jnp.concatenate([x[:, :HD], zero], axis=1),
            jnp.concatenate([zero, x[:, HD:]], axis=1),
        ],
        axis=0,
    )


def diagonal_turned(one, two):
    zero = jnp.zeros_like(one)
    return jnp.concatenate(
        [jnp.concatenate([one, zero], axis=1), jnp.concatenate([zero, two], axis=1)], axis=0
    )


def in_order(rows, lead):
    one, two = rows[:HD], rows[HD:]
    if isinstance(lead, int):
        return (one, two) if lead == 0 else (two, one)
    return jnp.where(lead == 0, one, two), jnp.where(lead == 0, two, one)


def key_mask(limit_ref, rows, first, count):
    index = lax.broadcasted_iota(jnp.int32, (rows, PAIR), 0)
    return jnp.concatenate(
        [index < limit_ref[i : i + 1, :] for i in range(first, first + count)], axis=0
    )


def scores_of(k, v, qd, d, open_keys):
    score = jnp.where(open_keys, dot(k, qd, NT) * SCALE, -jnp.inf)
    top = jnp.maximum(jnp.max(score, axis=0, keepdims=True), -1e30)
    raised = jnp.exp(score - top)
    total = jnp.maximum(jnp.sum(raised, axis=0, keepdims=True), 1.0)
    prob = raised * (1.0 / total)
    prob_b = prob.astype(BF16)
    d_prob = dot(v, d, NN)
    delta = jnp.sum(prob_b.astype(F32) * d_prob, axis=0, keepdims=True)
    return prob_b, (prob * (d_prob - delta)).astype(BF16)


def query_grad(d_score, k, tok):
    both = dot(d_score, k, TN) * SCALE
    return jnp.concatenate([both[:tok, :HD], both[tok:, HD:]], axis=1).astype(BF16)


def stacked(refs, cols):
    return jnp.concatenate([ref[:, cols] for ref in refs], axis=0)


def heads_kernel(steps, carried, dy_ref, q_ref, limit_ref, *refs):
    core, group = place()
    kv_refs, w_refs = refs[:3], refs[3 : -4 - carried]
    earlier, outs = refs[-4 - carried : -4], refs[-4:]
    dq_ref, own_ref, to_core_ref, to_far_ref = outs
    for old, out in zip(earlier, outs):
        out[..., : old.shape[-1]] = old[...]
    tok = q_ref.shape[1]
    values_at = kv_refs[0].shape[1] // (2 * PAIR)
    open_keys = key_mask(limit_ref, tok, 0, 3)
    for chunk, slot, pieces, lead in steps(core, group):
        cols, dest = columns(chunk), columns(slot)
        w = jnp.concatenate([w_refs[i][row : row + rows, :] for i, row, rows in pieces], axis=0)
        d = diagonal_turned(*in_order(dot(w, dy_ref[0], NT).astype(BF16), lead))
        qd = diagonal(q_ref[0, :, cols])
        k, v = stacked(kv_refs, cols), stacked(kv_refs, columns(chunk + values_at))
        prob_b, d_score = scores_of(k, v, qd, d, open_keys)
        dq_ref[:, dest] = query_grad(d_score, k, tok)
        for side, grad in enumerate((dot(d_score, qd, NN) * SCALE, dot(prob_b, d, NT))):
            own_ref[side, :, dest] = grad[:tok]
            to_core_ref[side, :, dest] = grad[tok : 2 * tok].astype(BF16)
            to_far_ref[side, :, dest] = grad[2 * tok :].astype(BF16)


def heads(name, steps, weights, earlier, d_out, q, limits, blocks):
    tok = q.shape[1]
    width = len(steps(0, 0)) * PAIR + (earlier[0].shape[1] if earlier else 0)
    return call(
        functools.partial(heads_kernel, steps, len(earlier)),
        name,
        (
            jax.ShapeDtypeStruct((tok, width), BF16),
            jax.ShapeDtypeStruct((2, tok, width), F32),
            jax.ShapeDtypeStruct((2, tok, width), BF16),
            jax.ShapeDtypeStruct((2, tok, width), BF16),
        ),
        [VMEM] * (6 + len(weights) + len(earlier)),
        (VMEM,) * 4,
        [],
        d_out,
        q,
        limits,
        *blocks,
        *weights,
        *earlier,
    )


def last_kernel(last, dy_ref, q_ref, limit_ref, *refs):
    core, group = place()
    kv_refs = refs[:3]
    near_both, far_both, near_next, *w_refs, dq_ref, dk_ref, dv_ref = refs[3:]
    tok, depth = q_ref.shape[1], dy_ref.shape[2]
    chunk = last(core, group)
    cols = columns(chunk)
    value_cols = columns(chunk + kv_refs[0].shape[1] // (2 * PAIR))
    w = jnp.concatenate([ref[...] for ref in w_refs], axis=0)
    dy = jnp.concatenate([dy_ref[0], near_both[:, :depth], far_both[:, :depth]], axis=0)
    turned = in_order(dot(w, dy, NT).astype(BF16), core)
    own, near, far = ([ref[:, at] for at in (cols, value_cols)] for ref in kv_refs)
    past_near = [near_next[:, :PAIR], near_next[:, PAIR:]]
    past_far = [far_both[:, depth + PAIR : depth + 2 * PAIR], far_both[:, depth + 2 * PAIR :]]
    at_queries = slice(depth, depth + PAIR)
    probs, scores, queries, cotangents = [], [], [], []
    for block, (q, parts) in enumerate(
        (
            (q_ref[0, :, cols], (own, near, far)),
            (near_both[:, at_queries], (near, own, past_near)),
            (far_both[:, at_queries], (far, own, past_far)),
        )
    ):
        k, v = (jnp.concatenate([part[side] for part in parts], axis=0) for side in range(2))
        qd = diagonal(q)
        d = diagonal_turned(*[half[:, block * tok : (block + 1) * tok] for half in turned])
        prob_b, d_score = scores_of(k, v, qd, d, key_mask(limit_ref, tok, 3 * block, 3))
        if block == 0:
            dq_ref[...] = query_grad(d_score, k, tok)
        mine = slice(0, tok) if block == 0 else slice(tok, 2 * tok)
        probs.append(prob_b[mine])
        scores.append(d_score[mine])
        queries.append(qd)
        cotangents.append(d)
    scores, probs = jnp.concatenate(scores, axis=1), jnp.concatenate(probs, axis=1)
    dk_ref[...] = (dot(scores, jnp.concatenate(queries, axis=0), NN) * SCALE).astype(BF16)
    dv_ref[...] = dot(probs, jnp.concatenate(cotangents, axis=1), NT).astype(BF16)


def last_heads(last, d_out, q, limits, blocks, halo, weights):
    tok = q.shape[1]
    return call(
        functools.partial(last_kernel, last),
        "heads_last",
        (jax.ShapeDtypeStruct((tok, PAIR), BF16),) * 3,
        [VMEM] * (9 + len(weights)),
        (VMEM,) * 3,
        [],
        d_out,
        q,
        limits,
        *blocks,
        *halo,
        *weights,
    )


def finish_kernel(chunks, widths, *refs):
    core, group = place()
    outs, stage, sems = refs[-5:-2], refs[-2], refs[-1]
    tok = stage.shape[1]
    copies = []
    slot = at = 0
    for width, summed in widths:
        part = refs[at : at + (3 if summed else 4)]
        at += len(part)
        for step in range(width // PAIR):
            cols = slice(step * PAIR, (step + 1) * PAIR)
            dest = columns(chunks(core, group)[slot])
            stage[3 * slot] = part[0][:, cols]
            for side in range(2):
                if summed:
                    total = part[1 + side][:, cols]
                else:
                    _, own, near, far = part
                    total = own[side, :, cols] + near[side, :, cols].astype(F32)
                    total = (total + far[side, :, cols].astype(F32)).astype(BF16)
                stage[3 * slot + 1 + side] = total
            for index in range(3):
                copy = pltpu.make_async_copy(
                    stage.at[3 * slot + index], outs[index].at[0, :, dest], sems.at[3 * slot + index]
                )
                copy.start()
                copies.append(copy)
            slot += 1
    for copy in copies:
        copy.wait()


def finish(chunks, parts, shape):
    count = len(chunks(0, 0))
    ins = [x for part in parts for x in part]
    widths = tuple((part[0].shape[1], len(part) == 3) for part in parts)
    return call(
        functools.partial(finish_kernel, chunks, widths),
        "finish",
        (jax.ShapeDtypeStruct(shape, BF16),) * 3,
        [VMEM] * len(ins),
        (ANY,) * 3,
        [
            pltpu.VMEM((3 * count, shape[1], PAIR), BF16),
            pltpu.SemaphoreType.DMA((3 * count,)),
        ],
        *ins,
    )


def body(queries, keys, values, d_out, w_out, pattern, valid):
    n_seq, n_fsdp = lax.axis_size("seq"), lax.axis_size("fsdp")
    n_chunks = queries.shape[2] // PAIR
    near = functools.partial(lax.ppermute, axis_name="seq", perm=swap(n_seq, 0))
    far = functools.partial(lax.ppermute, axis_name="seq", perm=swap(n_seq, 1))

    def cross(x, bits):
        pairs = [
            (s * n_fsdp + g, s * n_fsdp + (g ^ bits[s % 2]))
            for s in range(n_seq)
            for g in range(n_fsdp)
        ]
        return lax.ppermute(x, ("seq", "fsdp"), pairs)

    def exchange(part):
        dq, own, to_core, to_far = part
        back = far(to_far)
        return dq, own, near(to_core), back

    last = lambda core, group: group ^ 3 if n_fsdp == 4 else 0
    kv, both = join(last, keys, values, d_out, queries)
    limits = limits_of(pattern, valid)
    far_kv, near_kv = far(kv), near(kv)
    ours = d_out, queries, limits, (kv, near_kv, far_kv)
    if n_fsdp == 4 and n_chunks == 4 and w_out.shape[0] == PAIR:
        got = cross(w_out, (1, 2))
        near_both = near(both)
        far_both = far(hand_on("hand_far", last, near_kv, both))
        near_next = near(hand_on("hand_near", last, far_kv))
        own = heads("heads_own", lambda core, group: [(group, 0, ((0, 0, PAIR),), 0)], [w_out], (), *ours)
        got, dq, near_both, near_next = lax.optimization_barrier((got, own[0], near_both, near_next))
        *pieces, mine, other = onward(got)
        got_d = [cross(piece, (2, 1)) for piece in pieces]
        far_both, near_got = lax.optimization_barrier((far_both, (near(mine), near(other))))
        side = heads(
            "heads_side",
            lambda core, group: [
                (group ^ (1 + core), 1 + core, ((0, 0, HD), (0, HD, HD)), 0),
                (group ^ (2 - core), 2 - core, ((1, 0, HD), (2, 0, HD)), 1 - core),
            ],
            [got, *near_got],
            (dq, *own[1:]),
            *ours,
        )
        got_d, dq = lax.optimization_barrier((got_d, side[0]))
        sums = exchange((dq, *side[1:]))
        halo = near_both, far_both, near_next
        third = last_heads(last, *ours, halo, (*got_d, *[near(x) for x in got_d]))
        order = lambda core, group: [group, group ^ 1, group ^ 2, group ^ 3]
        return finish(order, [sums, third], queries.shape)
    full = lax.all_gather(w_out, "fsdp", axis=0, tiled=True)
    steps = lambda core, group: [
        (i, i, ((0, i * PAIR, PAIR),), 0) for i in range(n_chunks)
    ]
    part = exchange(heads("heads_all", steps, [full], (), *ours))
    return finish(lambda core, group: list(range(n_chunks)), [part], queries.shape)


def solution(mesh):
    rows = P("fsdp", "seq", None)
    in_specs = (rows, rows, rows, rows, P("fsdp", None), P(), P("fsdp", None))
    return jax.shard_map(
        body, mesh=mesh, in_specs=in_specs, out_specs=(rows,) * 3, check_vma=False
    )
```

```python
import functools

import jax
import jax.numpy as jnp
from jax import lax
from jax.experimental import pallas as pl
from jax.experimental.pallas import tpu as pltpu
from jax.sharding import PartitionSpec as P

HD = 128
PAIR = 2 * HD
PIECE = 64
BRIEF = pl.CostEstimate(flops=1, bytes_accessed=1, transcendentals=0)
F32 = jnp.float32
BF16 = jnp.bfloat16
NT = (((1,), (1,)), ((), ()))
NN = (((1,), (0,)), ((), ()))
TN = (((0,), (0,)), ((), ()))
HBM = pl.BlockSpec(memory_space=pltpu.HBM)
ANY = pl.BlockSpec(memory_space=pl.ANY)
VMEM = pl.BlockSpec(memory_space=pltpu.VMEM)
SMEM = pl.BlockSpec(memory_space=pltpu.SMEM)
PARAMS = pltpu.CompilerParams(vmem_limit_bytes=40 * 2**20)
WIDE = pltpu.CompilerParams(vmem_limit_bytes=58 * 2**20)
SCALE = HD ** (-0.5)


def dot(a, b, dims):
    return lax.dot_general(a, b, dims, preferred_element_type=F32)


def swap(n, offset):
    pairs = []
    for i in range(offset, n - 1, 2):
        pairs += [(i, i + 1), (i + 1, i)]
    return pairs


def place():
    return lax.rem(lax.axis_index("seq"), 2), lax.axis_index("fsdp")


def columns(chunk):
    return pl.ds(pl.multiple_of(chunk * PAIR, PAIR), PAIR)


def call(kernel, name, out_shape, in_specs, out_specs, scratch, *args):
    return pl.pallas_call(
        kernel,
        out_shape=out_shape,
        in_specs=in_specs,
        out_specs=out_specs,
        scratch_shapes=scratch,
        cost_estimate=BRIEF,
        compiler_params=PARAMS,
        name=name,
    )(*args)


def key_limits(pat_ref, val_ref):
    shard = lax.axis_index("seq")
    count = val_ref.shape[1]

    def pair(block):
        return block + 1 - 2 * lax.rem(block + 2, 2)

    def far(block):
        return block - 1 + 2 * lax.rem(block + 2, 2)

    wanted = [(shard, block) for block in (shard, pair(shard), far(shard))]
    for row, other in ((pair(shard), far(pair(shard))), (far(shard), pair(far(shard)))):
        wanted += [(row, block) for block in (row, shard, other)]
    limits = []
    for row, block in wanted:
        held = jnp.clip(row, 0, count - 1)
        listed = pat_ref[held, 0] == block
        for entry in range(1, pat_ref.shape[1]):
            listed = jnp.logical_or(listed, pat_ref[held, entry] == block)
        inside = jnp.logical_and(row == held, jnp.logical_and(block >= 0, block < count))
        keys = val_ref[0, jnp.clip(block, 0, count - 1)]
        limits.append(jnp.where(jnp.logical_and(listed, inside), keys, 0))
    return limits


def limits_kernel(pat_ref, val_ref, limit_ref):
    limit_ref[...] = jnp.zeros_like(limit_ref)
    for row, limit in enumerate(key_limits(pat_ref, val_ref)):
        limit_ref[row : row + 1, :] = jnp.full((1, PAIR), limit, jnp.int32)


def limits_of(pattern, valid):
    shape = jax.ShapeDtypeStruct((16, PAIR), jnp.int32)
    return call(limits_kernel, "limits", shape, [SMEM] * 2, VMEM, [], pattern, valid)


def join_kernel(last, k_ref, v_ref, dy_ref, q_ref, kv_ref, both_ref, kv, both, sems):
    core, group = place()
    tok, depth = dy_ref.shape[1:]
    width = k_ref.shape[2]
    steps = []
    for sources, held, target in (
        (((k_ref, slice(None), width), (v_ref, slice(None), width)), kv, kv_ref),
        (
            ((dy_ref, slice(None), depth), (q_ref, columns(last(core, group)), PAIR)),
            both,
            both_ref,
        ),
    ):
        for row in range(0, tok, PIECE):
            rows = pl.ds(row, PIECE)
            to = 0
            for source, cols, size in sources:
                at = (rows, pl.ds(to, size))
                steps.append((source.at[0, rows, cols], held.at[at], target.at[at]))
                to += size
    arrivals, moves = [], []
    for i, (source, held, target) in enumerate(steps):
        arrivals.append(pltpu.make_async_copy(source, held, sems.at[0, i]))
        moves.append(pltpu.make_async_copy(held, target, sems.at[1, i]))
    for copy in arrivals:
        copy.start()
    for arrival, move in zip(arrivals, moves):
        arrival.wait()
        move.start()
    for move in moves:
        move.wait()


def join(last, keys, values, d_out, queries):
    tok, depth = d_out.shape[1:]
    kv, both = (tok, 2 * keys.shape[2]), (tok, depth + PAIR)
    return pl.pallas_call(
        functools.partial(join_kernel, last),
        out_shape=(jax.ShapeDtypeStruct(kv, BF16), jax.ShapeDtypeStruct(both, BF16)),
        in_specs=[HBM] * 4,
        out_specs=(ANY,) * 2,
        scratch_shapes=[
            pltpu.VMEM(kv, BF16),
            pltpu.VMEM(both, BF16),
            pltpu.SemaphoreType.DMA((2, 4 * (tok // PIECE))),
        ],
        cost_estimate=BRIEF,
        compiler_params=WIDE,
        name="join",
    )(keys, values, d_out, queries)


def hand_on_kernel(last, *refs):
    core, group = place()
    *before, kv_ref, out_ref = refs
    chunk = last(core, group)
    cols = [columns(chunk), columns(chunk + kv_ref.shape[1] // (2 * PAIR))]
    to = 0
    for piece in [ref[...] for ref in before] + [kv_ref[:, at] for at in cols]:
        out_ref[:, to : to + piece.shape[1]] = piece
        to += piece.shape[1]


def hand_on(name, last, kv, *before):
    width = sum(x.shape[1] for x in before) + 2 * PAIR
    shape = jax.ShapeDtypeStruct((kv.shape[0], width), BF16)
    kernel = functools.partial(hand_on_kernel, last)
    return call(kernel, name, shape, [VMEM] * (len(before) + 1), VMEM, [], *before, kv)


def onward_kernel(w_ref, *out_refs):
    core, _ = place()
    half = w_ref.shape[0] // 2
    start = pl.multiple_of(core * half, half)
    for i, ref in enumerate(out_refs[:2]):
        rows = ref.shape[0]
        ref[...] = w_ref[pl.ds(start + i * rows, rows), :]
    for ref, first in zip(out_refs[2:], (start, half - start)):
        ref[...] = w_ref[pl.ds(pl.multiple_of(first, half), half), :]


def onward(got):
    rows, depth = got.shape
    shapes = [jax.ShapeDtypeStruct((rows // part, depth), BF16) for part in (4, 4, 2, 2)]
    return call(onward_kernel, "onward", tuple(shapes), [VMEM], (VMEM,) * 4, [], got)


def diagonal(x):
    zero = jnp.zeros((x.shape[0], HD), x.dtype)
    return jnp.concatenate(
        [
            jnp.concatenate([x[:, :HD], zero], axis=1),
            jnp.concatenate([zero, x[:, HD:]], axis=1),
        ],
        axis=0,
    )


def diagonal_turned(one, two):
    zero = jnp.zeros_like(one)
    return jnp.concatenate(
        [jnp.concatenate([one, zero], axis=1), jnp.concatenate([zero, two], axis=1)], axis=0
    )


def in_order(rows, lead):
    one, two = rows[:HD], rows[HD:]
    if isinstance(lead, int):
        return (one, two) if lead == 0 else (two, one)
    return jnp.where(lead == 0, one, two), jnp.where(lead == 0, two, one)


def key_mask(limit_ref, rows, first, count):
    index = lax.broadcasted_iota(jnp.int32, (rows, PAIR), 0)
    return jnp.concatenate(
        [index < limit_ref[i : i + 1, :] for i in range(first, first + count)], axis=0
    )


def prob_of(k, qd, open_keys):
    score = jnp.where(open_keys, dot(k, qd, NT) * SCALE, -jnp.inf)
    top = jnp.maximum(jnp.max(score, axis=0, keepdims=True), -1e30)
    raised = jnp.exp(score - top)
    total = jnp.maximum(jnp.sum(raised, axis=0, keepdims=True), 1.0)
    return raised * (1.0 / total)


def score_grad(prob, prob_b, v, d):
    d_prob = dot(v, d, NN)
    delta = jnp.sum(prob_b.astype(F32) * d_prob, axis=0, keepdims=True)
    return (prob * (d_prob - delta)).astype(BF16)


def query_grad(d_score, k, tok):
    both = dot(d_score, k, TN) * SCALE
    return jnp.concatenate([both[:tok, :HD], both[tok:, HD:]], axis=1).astype(BF16)


def stacked(refs, cols):
    return jnp.concatenate([ref[:, cols] for ref in refs], axis=0)


def heads_kernel(steps, carried, dy_ref, q_ref, limit_ref, *refs):
    core, group = place()
    kv_refs, w_refs = refs[:3], refs[3 : -4 - carried]
    earlier, outs = refs[-4 - carried : -4], refs[-4:]
    dq_ref, own_ref, to_core_ref, to_far_ref = outs
    for old, out in zip(earlier, outs):
        out[..., : old.shape[-1]] = old[...]
    tok = q_ref.shape[1]
    values_at = kv_refs[0].shape[1] // (2 * PAIR)
    open_keys = key_mask(limit_ref, tok, 0, 3)
    for chunk, slot, pieces, lead in steps(core, group):
        cols, dest = columns(chunk), columns(slot)
        w = jnp.concatenate([w_refs[i][row : row + rows, :] for i, row, rows in pieces], axis=0)
        d = diagonal_turned(*in_order(dot(w, dy_ref[0], NT).astype(BF16), lead))
        qd = diagonal(q_ref[0, :, cols])
        k, v = stacked(kv_refs, cols), stacked(kv_refs, columns(chunk + values_at))
        prob = prob_of(k, qd, open_keys)
        prob_b = prob.astype(BF16)
        d_score = score_grad(prob, prob_b, v, d)
        dq_ref[:, dest] = query_grad(d_score, k, tok)
        for side, grad in enumerate((dot(d_score, qd, NN) * SCALE, dot(prob_b, d, NT))):
            own_ref[side, :, dest] = grad[:tok]
            to_core_ref[side, :, dest] = grad[tok : 2 * tok].astype(BF16)
            to_far_ref[side, :, dest] = grad[2 * tok :].astype(BF16)


def heads(name, steps, weights, earlier, d_out, q, limits, blocks):
    tok = q.shape[1]
    width = len(steps(0, 0)) * PAIR + (earlier[0].shape[1] if earlier else 0)
    return call(
        functools.partial(heads_kernel, steps, len(earlier)),
        name,
        (
            jax.ShapeDtypeStruct((tok, width), BF16),
            jax.ShapeDtypeStruct((2, tok, width), F32),
            jax.ShapeDtypeStruct((2, tok, width), BF16),
            jax.ShapeDtypeStruct((2, tok, width), BF16),
        ),
        [VMEM] * (6 + len(weights) + len(earlier)),
        (VMEM,) * 4,
        [],
        d_out,
        q,
        limits,
        *blocks,
        *weights,
        *earlier,
    )


def last_parts(last, q_ref, near_both, far_both, near_next, kv_refs):
    cols = columns(last(*place()))
    value_cols = columns(last(*place()) + kv_refs[0].shape[1] // (2 * PAIR))
    depth = far_both.shape[1] - 3 * PAIR
    own, near, far = ([ref[:, at] for at in (cols, value_cols)] for ref in kv_refs)
    past_near = [near_next[:, :PAIR], near_next[:, PAIR:]]
    past_far = [far_both[:, depth + PAIR : depth + 2 * PAIR], far_both[:, depth + 2 * PAIR :]]
    at_queries = slice(depth, depth + PAIR)
    return (
        (q_ref[0, :, cols], (own, near, far)),
        (near_both[:, at_queries], (near, own, past_near)),
        (far_both[:, at_queries], (far, own, past_far)),
    )


def joined(parts, side):
    return jnp.concatenate([part[side] for part in parts], axis=0)


def probs_kernel(last, q_ref, limit_ref, *refs):
    *kv_refs, near_both, far_both, near_next, prob_ref = refs
    tok = q_ref.shape[1]
    blocks = last_parts(last, q_ref, near_both, far_both, near_next, kv_refs)
    for block, (q, parts) in enumerate(blocks):
        open_keys = key_mask(limit_ref, tok, 3 * block, 3)
        prob_ref[block] = prob_of(joined(parts, 0), diagonal(q), open_keys)


def turn_kernel(dy_ref, near_both, far_both, *refs):
    *w_refs, out_ref = refs
    depth = dy_ref.shape[2]
    w = jnp.concatenate([ref[...] for ref in w_refs], axis=0)
    dy = jnp.concatenate([dy_ref[0], near_both[:, :depth], far_both[:, :depth]], axis=0)
    out_ref[...] = dot(w, dy, NT).astype(BF16)


def last_kernel(last, dy_ref, q_ref, prob_ref, mine_ref, *refs):
    core, _ = place()
    kv_refs = refs[:3]
    near_both, far_both, near_next, *w_refs, dq_ref, dk_ref, dv_ref = refs[3:]
    tok, depth = q_ref.shape[1], dy_ref.shape[2]
    w = jnp.concatenate([ref[...] for ref in w_refs], axis=0)
    dy = jnp.concatenate([dy_ref[0], near_both[:, :depth], far_both[:, :depth]], axis=0)
    other = dot(w, dy, NT).astype(BF16)
    turned = in_order(jnp.concatenate([mine_ref[...], other], axis=0), core)
    probs, scores, queries, cotangents = [], [], [], []
    blocks = last_parts(last, q_ref, near_both, far_both, near_next, kv_refs)
    for block, (q, parts) in enumerate(blocks):
        qd = diagonal(q)
        d = diagonal_turned(*[half[:, block * tok : (block + 1) * tok] for half in turned])
        prob = prob_ref[block]
        prob_b = prob.astype(BF16)
        d_score = score_grad(prob, prob_b, joined(parts, 1), d)
        if block == 0:
            dq_ref[...] = query_grad(d_score, joined(parts, 0), tok)
        mine = slice(0, tok) if block == 0 else slice(tok, 2 * tok)
        probs.append(prob_b[mine])
        scores.append(d_score[mine])
        queries.append(qd)
        cotangents.append(d)
    scores, probs = jnp.concatenate(scores, axis=1), jnp.concatenate(probs, axis=1)
    dk_ref[...] = (dot(scores, jnp.concatenate(queries, axis=0), NN) * SCALE).astype(BF16)
    dv_ref[...] = dot(probs, jnp.concatenate(cotangents, axis=1), NT).astype(BF16)


def last_heads(last, d_out, q, limits, blocks, halo, mine, other):
    tok = q.shape[1]
    prob = call(
        functools.partial(probs_kernel, last),
        "probs_last",
        jax.ShapeDtypeStruct((3, 3 * tok, PAIR), F32),
        [VMEM] * 8,
        VMEM,
        [],
        q,
        limits,
        *blocks,
        *halo,
    )
    turned = call(
        turn_kernel,
        "turn",
        jax.ShapeDtypeStruct((HD, 3 * tok), BF16),
        [VMEM] * (3 + len(mine)),
        VMEM,
        [],
        d_out,
        *halo[:2],
        *mine,
    )
    return call(
        functools.partial(last_kernel, last),
        "heads_last",
        (jax.ShapeDtypeStruct((tok, PAIR), BF16),) * 3,
        [VMEM] * (10 + len(other)),
        (VMEM,) * 3,
        [],
        d_out,
        q,
        prob,
        turned,
        *blocks,
        *halo,
        *other,
    )


def finish_kernel(chunks, widths, *refs):
    core, group = place()
    outs, stage, sems = refs[-5:-2], refs[-2], refs[-1]
    tok = stage.shape[1]
    copies = []
    slot = at = 0
    for width, summed in widths:
        part = refs[at : at + (3 if summed else 4)]
        at += len(part)
        for step in range(width // PAIR):
            cols = slice(step * PAIR, (step + 1) * PAIR)
            dest = columns(chunks(core, group)[slot])
            stage[3 * slot] = part[0][:, cols]
            for side in range(2):
                if summed:
                    total = part[1 + side][:, cols]
                else:
                    _, own, near, far = part
                    total = own[side, :, cols] + near[side, :, cols].astype(F32)
                    total = (total + far[side, :, cols].astype(F32)).astype(BF16)
                stage[3 * slot + 1 + side] = total
            for index in range(3):
                copy = pltpu.make_async_copy(
                    stage.at[3 * slot + index], outs[index].at[0, :, dest], sems.at[3 * slot + index]
                )
                copy.start()
                copies.append(copy)
            slot += 1
    for copy in copies:
        copy.wait()


def finish(chunks, parts, shape):
    count = len(chunks(0, 0))
    ins = [x for part in parts for x in part]
    widths = tuple((part[0].shape[1], len(part) == 3) for part in parts)
    return call(
        functools.partial(finish_kernel, chunks, widths),
        "finish",
        (jax.ShapeDtypeStruct(shape, BF16),) * 3,
        [VMEM] * len(ins),
        (ANY,) * 3,
        [
            pltpu.VMEM((3 * count, shape[1], PAIR), BF16),
            pltpu.SemaphoreType.DMA((3 * count,)),
        ],
        *ins,
    )


def body(queries, keys, values, d_out, w_out, pattern, valid):
    n_seq, n_fsdp = lax.axis_size("seq"), lax.axis_size("fsdp")
    n_chunks = queries.shape[2] // PAIR
    near = functools.partial(lax.ppermute, axis_name="seq", perm=swap(n_seq, 0))
    far = functools.partial(lax.ppermute, axis_name="seq", perm=swap(n_seq, 1))

    def cross(x, bits):
        pairs = [
            (s * n_fsdp + g, s * n_fsdp + (g ^ bits[s % 2]))
            for s in range(n_seq)
            for g in range(n_fsdp)
        ]
        return lax.ppermute(x, ("seq", "fsdp"), pairs)

    def exchange(part):
        dq, own, to_core, to_far = part
        back = far(to_far)
        return dq, own, near(to_core), back

    last = lambda core, group: group ^ 3 if n_fsdp == 4 else 0
    kv, both = join(last, keys, values, d_out, queries)
    limits = limits_of(pattern, valid)
    far_kv, near_kv = far(kv), near(kv)
    if n_fsdp == 4 and n_chunks == 4 and w_out.shape[0] == PAIR:
        got = cross(w_out, (1, 2))
        near_both = near(both)
        far_both = far(hand_on("hand_far", last, near_kv, both))
        early = got, near_kv, far_kv, limits
        got, near_kv, far_kv, limits = lax.optimization_barrier(early)
        *pieces, mine, other = onward(got)
        got_d = [cross(piece, (2, 1)) for piece in pieces]
        near_next = near(hand_on("hand_near", last, far_kv))
        ours = d_out, queries, limits, (kv, near_kv, far_kv)
        own = heads("heads_own", lambda core, group: [(group, 0, ((0, 0, PAIR),), 0)], [w_out], (), *ours)
        near_got = near(mine), near(other)
        far_both, near_both, near_got = lax.optimization_barrier((far_both, near_both, near_got))
        side = heads(
            "heads_side",
            lambda core, group: [
                (group ^ (1 + core), 1 + core, ((0, 0, HD), (0, HD, HD)), 0),
                (group ^ (2 - core), 2 - core, ((1, 0, HD), (2, 0, HD)), 1 - core),
            ],
            [got, *near_got],
            own,
            *ours,
        )
        got_d, near_next, dq = lax.optimization_barrier((got_d, near_next, side[0]))
        sums = exchange((dq, *side[1:]))
        halo = near_both, far_both, near_next
        third = last_heads(last, *ours, halo, got_d, [near(x) for x in got_d])
        order = lambda core, group: [group, group ^ 1, group ^ 2, group ^ 3]
        return finish(order, [sums, third], queries.shape)
    full = lax.all_gather(w_out, "fsdp", axis=0, tiled=True)
    ours = d_out, queries, limits, (kv, near_kv, far_kv)
    steps = lambda core, group: [
        (i, i, ((0, i * PAIR, PAIR),), 0) for i in range(n_chunks)
    ]
    part = exchange(heads("heads_all", steps, [full], (), *ours))
    return finish(lambda core, group: list(range(n_chunks)), [part], queries.shape)


def solution(mesh):
    rows = P("fsdp", "seq", None)
    in_specs = (rows, rows, rows, rows, P("fsdp", None), P(), P("fsdp", None))
    return jax.shard_map(
        body, mesh=mesh, in_specs=in_specs, out_specs=(rows,) * 3, check_vma=False
    )
```

```python
import functools

import jax
import jax.numpy as jnp
from jax import lax
from jax.experimental import pallas as pl
from jax.experimental.pallas import tpu as pltpu
from jax.sharding import PartitionSpec as P

HD = 128
PAIR = 2 * HD
PIECE = 64
BRIEF = pl.CostEstimate(flops=1, bytes_accessed=1, transcendentals=0)
F32 = jnp.float32
BF16 = jnp.bfloat16
NT = (((1,), (1,)), ((), ()))
NN = (((1,), (0,)), ((), ()))
TN = (((0,), (0,)), ((), ()))
HBM = pl.BlockSpec(memory_space=pltpu.HBM)
ANY = pl.BlockSpec(memory_space=pl.ANY)
VMEM = pl.BlockSpec(memory_space=pltpu.VMEM)
SMEM = pl.BlockSpec(memory_space=pltpu.SMEM)
PARAMS = pltpu.CompilerParams(vmem_limit_bytes=40 * 2**20)
WIDE = pltpu.CompilerParams(vmem_limit_bytes=58 * 2**20)
SCALE = HD ** (-0.5)


def dot(a, b, dims):
    return lax.dot_general(a, b, dims, preferred_element_type=F32)


def swap(n, offset):
    pairs = []
    for i in range(offset, n - 1, 2):
        pairs += [(i, i + 1), (i + 1, i)]
    return pairs


def place():
    return lax.rem(lax.axis_index("seq"), 2), lax.axis_index("fsdp")


def columns(chunk):
    return pl.ds(pl.multiple_of(chunk * PAIR, PAIR), PAIR)


def call(kernel, name, out_shape, in_specs, out_specs, scratch, *args):
    return pl.pallas_call(
        kernel,
        out_shape=out_shape,
        in_specs=in_specs,
        out_specs=out_specs,
        scratch_shapes=scratch,
        cost_estimate=BRIEF,
        compiler_params=PARAMS,
        name=name,
    )(*args)


def key_limits(pat_ref, val_ref):
    shard = lax.axis_index("seq")
    count = val_ref.shape[1]

    def pair(block):
        return block + 1 - 2 * lax.rem(block + 2, 2)

    def far(block):
        return block - 1 + 2 * lax.rem(block + 2, 2)

    wanted = [(shard, block) for block in (shard, pair(shard), far(shard))]
    for row, other in ((pair(shard), far(pair(shard))), (far(shard), pair(far(shard)))):
        wanted += [(row, block) for block in (row, shard, other)]
    limits = []
    for row, block in wanted:
        held = jnp.clip(row, 0, count - 1)
        listed = pat_ref[0, held] == block
        for entry in range(1, pat_ref.shape[0]):
            listed = jnp.logical_or(listed, pat_ref[entry, held] == block)
        inside = jnp.logical_and(row == held, jnp.logical_and(block >= 0, block < count))
        keys = val_ref[0, jnp.clip(block, 0, count - 1)]
        limits.append(jnp.where(jnp.logical_and(listed, inside), keys, 0))
    return limits


def limits_kernel(pat_ref, val_ref, limit_ref):
    limit_ref[...] = jnp.zeros_like(limit_ref)
    for row, limit in enumerate(key_limits(pat_ref, val_ref)):
        limit_ref[row : row + 1, :] = jnp.full((1, PAIR), limit, jnp.int32)


def limits_of(pattern, valid):
    shape = jax.ShapeDtypeStruct((16, PAIR), jnp.int32)
    return call(limits_kernel, "limits", shape, [SMEM] * 2, VMEM, [], pattern.T, valid)


def join_kernel(last, k_ref, v_ref, dy_ref, q_ref, kv_ref, both_ref, kv, both, sems):
    core, group = place()
    tok, depth = dy_ref.shape[1:]
    width = k_ref.shape[2]
    steps = []
    for sources, held, target in (
        (((k_ref, slice(None), width), (v_ref, slice(None), width)), kv, kv_ref),
        (
            ((dy_ref, slice(None), depth), (q_ref, columns(last(core, group)), PAIR)),
            both,
            both_ref,
        ),
    ):
        for row in range(0, tok, PIECE):
            rows = pl.ds(row, PIECE)
            to = 0
            for source, cols, size in sources:
                at = (rows, pl.ds(to, size))
                steps.append((source.at[0, rows, cols], held.at[at], target.at[at]))
                to += size
    arrivals, moves = [], []
    for i, (source, held, target) in enumerate(steps):
        arrivals.append(pltpu.make_async_copy(source, held, sems.at[0, i]))
        moves.append(pltpu.make_async_copy(held, target, sems.at[1, i]))
    for copy in arrivals:
        copy.start()
    for arrival, move in zip(arrivals, moves):
        arrival.wait()
        move.start()
    for move in moves:
        move.wait()


def join(last, keys, values, d_out, queries):
    tok, depth = d_out.shape[1:]
    kv, both = (tok, 2 * keys.shape[2]), (tok, depth + PAIR)
    return pl.pallas_call(
        functools.partial(join_kernel, last),
        out_shape=(jax.ShapeDtypeStruct(kv, BF16), jax.ShapeDtypeStruct(both, BF16)),
        in_specs=[HBM] * 4,
        out_specs=(ANY,) * 2,
        scratch_shapes=[
            pltpu.VMEM(kv, BF16),
            pltpu.VMEM(both, BF16),
            pltpu.SemaphoreType.DMA((2, 4 * (tok // PIECE))),
        ],
        cost_estimate=BRIEF,
        compiler_params=WIDE,
        name="join",
    )(keys, values, d_out, queries)


def hand_on_kernel(last, *refs):
    core, group = place()
    *before, kv_ref, out_ref = refs
    chunk = last(core, group)
    cols = [columns(chunk), columns(chunk + kv_ref.shape[1] // (2 * PAIR))]
    to = 0
    for piece in [ref[...] for ref in before] + [kv_ref[:, at] for at in cols]:
        out_ref[:, to : to + piece.shape[1]] = piece
        to += piece.shape[1]


def hand_on(name, last, kv, *before):
    width = sum(x.shape[1] for x in before) + 2 * PAIR
    shape = jax.ShapeDtypeStruct((kv.shape[0], width), BF16)
    kernel = functools.partial(hand_on_kernel, last)
    return call(kernel, name, shape, [VMEM] * (len(before) + 1), VMEM, [], *before, kv)


def onward_kernel(w_ref, *out_refs):
    core, _ = place()
    half = w_ref.shape[0] // 2
    start = pl.multiple_of(core * half, half)
    for i, ref in enumerate(out_refs[:2]):
        rows = ref.shape[0]
        ref[...] = w_ref[pl.ds(start + i * rows, rows), :]
    for ref, first in zip(out_refs[2:], (start, half - start)):
        ref[...] = w_ref[pl.ds(pl.multiple_of(first, half), half), :]


def onward(got):
    rows, depth = got.shape
    shapes = [jax.ShapeDtypeStruct((rows // part, depth), BF16) for part in (4, 4, 2, 2)]
    return call(onward_kernel, "onward", tuple(shapes), [VMEM], (VMEM,) * 4, [], got)


def diagonal(x):
    zero = jnp.zeros((x.shape[0], HD), x.dtype)
    return jnp.concatenate(
        [
            jnp.concatenate([x[:, :HD], zero], axis=1),
            jnp.concatenate([zero, x[:, HD:]], axis=1),
        ],
        axis=0,
    )


def diagonal_turned(one, two):
    zero = jnp.zeros_like(one)
    return jnp.concatenate(
        [jnp.concatenate([one, zero], axis=1), jnp.concatenate([zero, two], axis=1)], axis=0
    )


def in_order(rows, lead):
    one, two = rows[:HD], rows[HD:]
    if isinstance(lead, int):
        return (one, two) if lead == 0 else (two, one)
    return jnp.where(lead == 0, one, two), jnp.where(lead == 0, two, one)


def key_mask(limit_ref, rows, first, count):
    index = lax.broadcasted_iota(jnp.int32, (rows, PAIR), 0)
    return jnp.concatenate(
        [index < limit_ref[i : i + 1, :] for i in range(first, first + count)], axis=0
    )


def prob_of(k, qd, open_keys):
    score = jnp.where(open_keys, dot(k, qd, NT) * SCALE, -jnp.inf)
    top = jnp.maximum(jnp.max(score, axis=0, keepdims=True), -1e30)
    raised = jnp.exp(score - top)
    total = jnp.maximum(jnp.sum(raised, axis=0, keepdims=True), 1.0)
    return raised * (1.0 / total)


def score_grad(prob, prob_b, v, d):
    d_prob = dot(v, d, NN)
    delta = jnp.sum(prob_b.astype(F32) * d_prob, axis=0, keepdims=True)
    return (prob * (d_prob - delta)).astype(BF16)


def query_grad(d_score, k, tok):
    both = dot(d_score, k, TN) * SCALE
    return jnp.concatenate([both[:tok, :HD], both[tok:, HD:]], axis=1).astype(BF16)


def stacked(refs, cols):
    return jnp.concatenate([ref[:, cols] for ref in refs], axis=0)


def heads_kernel(steps, carried, dy_ref, q_ref, limit_ref, *refs):
    core, group = place()
    kv_refs, w_refs = refs[:3], refs[3 : -4 - carried]
    earlier, outs = refs[-4 - carried : -4], refs[-4:]
    dq_ref, own_ref, to_core_ref, to_far_ref = outs
    for old, out in zip(earlier, outs):
        out[..., : old.shape[-1]] = old[...]
    tok = q_ref.shape[1]
    values_at = kv_refs[0].shape[1] // (2 * PAIR)
    open_keys = key_mask(limit_ref, tok, 0, 3)
    for chunk, slot, pieces, lead in steps(core, group):
        cols, dest = columns(chunk), columns(slot)
        w = jnp.concatenate([w_refs[i][row : row + rows, :] for i, row, rows in pieces], axis=0)
        d = diagonal_turned(*in_order(dot(w, dy_ref[0], NT).astype(BF16), lead))
        qd = diagonal(q_ref[0, :, cols])
        k, v = stacked(kv_refs, cols), stacked(kv_refs, columns(chunk + values_at))
        prob = prob_of(k, qd, open_keys)
        prob_b = prob.astype(BF16)
        d_score = score_grad(prob, prob_b, v, d)
        dq_ref[:, dest] = query_grad(d_score, k, tok)
        for side, grad in enumerate((dot(d_score, qd, NN) * SCALE, dot(prob_b, d, NT))):
            own_ref[side, :, dest] = grad[:tok]
            to_core_ref[side, :, dest] = grad[tok : 2 * tok].astype(BF16)
            to_far_ref[side, :, dest] = grad[2 * tok :].astype(BF16)


def heads(name, steps, weights, earlier, d_out, q, limits, blocks):
    tok = q.shape[1]
    width = len(steps(0, 0)) * PAIR + (earlier[0].shape[1] if earlier else 0)
    return call(
        functools.partial(heads_kernel, steps, len(earlier)),
        name,
        (
            jax.ShapeDtypeStruct((tok, width), BF16),
            jax.ShapeDtypeStruct((2, tok, width), F32),
            jax.ShapeDtypeStruct((2, tok, width), BF16),
            jax.ShapeDtypeStruct((2, tok, width), BF16),
        ),
        [VMEM] * (6 + len(weights) + len(earlier)),
        (VMEM,) * 4,
        [],
        d_out,
        q,
        limits,
        *blocks,
        *weights,
        *earlier,
    )


def last_parts(last, q_ref, near_both, far_both, near_next, kv_refs):
    cols = columns(last(*place()))
    value_cols = columns(last(*place()) + kv_refs[0].shape[1] // (2 * PAIR))
    depth = far_both.shape[1] - 3 * PAIR
    own, near, far = ([ref[:, at] for at in (cols, value_cols)] for ref in kv_refs)
    past_near = [near_next[:, :PAIR], near_next[:, PAIR:]]
    past_far = [far_both[:, depth + PAIR : depth + 2 * PAIR], far_both[:, depth + 2 * PAIR :]]
    at_queries = slice(depth, depth + PAIR)
    return (
        (q_ref[0, :, cols], (own, near, far)),
        (near_both[:, at_queries], (near, own, past_near)),
        (far_both[:, at_queries], (far, own, past_far)),
    )


def joined(parts, side):
    return jnp.concatenate([part[side] for part in parts], axis=0)


def probs_kernel(last, q_ref, limit_ref, *refs):
    *kv_refs, near_both, far_both, near_next, prob_ref = refs
    tok = q_ref.shape[1]
    blocks = last_parts(last, q_ref, near_both, far_both, near_next, kv_refs)
    for block, (q, parts) in enumerate(blocks):
        open_keys = key_mask(limit_ref, tok, 3 * block, 3)
        prob_ref[block] = prob_of(joined(parts, 0), diagonal(q), open_keys)


def turn_kernel(dy_ref, near_both, far_both, *refs):
    *w_refs, out_ref = refs
    depth = dy_ref.shape[2]
    w = jnp.concatenate([ref[...] for ref in w_refs], axis=0)
    dy = jnp.concatenate([dy_ref[0], near_both[:, :depth], far_both[:, :depth]], axis=0)
    out_ref[...] = dot(w, dy, NT).astype(BF16)


def last_kernel(last, dy_ref, q_ref, prob_ref, mine_ref, *refs):
    core, _ = place()
    kv_refs = refs[:3]
    near_both, far_both, near_next, *w_refs, dq_ref, dk_ref, dv_ref = refs[3:]
    tok, depth = q_ref.shape[1], dy_ref.shape[2]
    w = jnp.concatenate([ref[...] for ref in w_refs], axis=0)
    dy = jnp.concatenate([dy_ref[0], near_both[:, :depth], far_both[:, :depth]], axis=0)
    other = dot(w, dy, NT).astype(BF16)
    turned = in_order(jnp.concatenate([mine_ref[...], other], axis=0), core)
    probs, scores, queries, cotangents = [], [], [], []
    blocks = last_parts(last, q_ref, near_both, far_both, near_next, kv_refs)
    for block, (q, parts) in enumerate(blocks):
        qd = diagonal(q)
        d = diagonal_turned(*[half[:, block * tok : (block + 1) * tok] for half in turned])
        prob = prob_ref[block]
        prob_b = prob.astype(BF16)
        d_score = score_grad(prob, prob_b, joined(parts, 1), d)
        if block == 0:
            dq_ref[...] = query_grad(d_score, joined(parts, 0), tok)
        mine = slice(0, tok) if block == 0 else slice(tok, 2 * tok)
        probs.append(prob_b[mine])
        scores.append(d_score[mine])
        queries.append(qd)
        cotangents.append(d)
    scores, probs = jnp.concatenate(scores, axis=1), jnp.concatenate(probs, axis=1)
    dk_ref[...] = (dot(scores, jnp.concatenate(queries, axis=0), NN) * SCALE).astype(BF16)
    dv_ref[...] = dot(probs, jnp.concatenate(cotangents, axis=1), NT).astype(BF16)


def last_heads(last, d_out, q, limits, blocks, halo, mine, other):
    tok = q.shape[1]
    prob = call(
        functools.partial(probs_kernel, last),
        "probs_last",
        jax.ShapeDtypeStruct((3, 3 * tok, PAIR), F32),
        [VMEM] * 8,
        VMEM,
        [],
        q,
        limits,
        *blocks,
        *halo,
    )
    turned = call(
        turn_kernel,
        "turn",
        jax.ShapeDtypeStruct((HD, 3 * tok), BF16),
        [VMEM] * (3 + len(mine)),
        VMEM,
        [],
        d_out,
        *halo[:2],
        *mine,
    )
    return call(
        functools.partial(last_kernel, last),
        "heads_last",
        (jax.ShapeDtypeStruct((tok, PAIR), BF16),) * 3,
        [VMEM] * (10 + len(other)),
        (VMEM,) * 3,
        [],
        d_out,
        q,
        prob,
        turned,
        *blocks,
        *halo,
        *other,
    )


def finish_kernel(chunks, widths, *refs):
    core, group = place()
    outs, stage, sems = refs[-5:-2], refs[-2], refs[-1]
    tok = stage.shape[1]
    copies = []
    slot = at = 0
    for width, summed in widths:
        part = refs[at : at + (3 if summed else 4)]
        at += len(part)
        for step in range(width // PAIR):
            cols = slice(step * PAIR, (step + 1) * PAIR)
            dest = columns(chunks(core, group)[slot])
            stage[3 * slot] = part[0][:, cols]
            for side in range(2):
                if summed:
                    total = part[1 + side][:, cols]
                else:
                    _, own, near, far = part
                    total = own[side, :, cols] + near[side, :, cols].astype(F32)
                    total = (total + far[side, :, cols].astype(F32)).astype(BF16)
                stage[3 * slot + 1 + side] = total
            for index in range(3):
                copy = pltpu.make_async_copy(
                    stage.at[3 * slot + index], outs[index].at[0, :, dest], sems.at[3 * slot + index]
                )
                copy.start()
                copies.append(copy)
            slot += 1
    for copy in copies:
        copy.wait()


def finish(chunks, parts, shape):
    count = len(chunks(0, 0))
    ins = [x for part in parts for x in part]
    widths = tuple((part[0].shape[1], len(part) == 3) for part in parts)
    return call(
        functools.partial(finish_kernel, chunks, widths),
        "finish",
        (jax.ShapeDtypeStruct(shape, BF16),) * 3,
        [VMEM] * len(ins),
        (ANY,) * 3,
        [
            pltpu.VMEM((3 * count, shape[1], PAIR), BF16),
            pltpu.SemaphoreType.DMA((3 * count,)),
        ],
        *ins,
    )


def body(queries, keys, values, d_out, w_out, pattern, valid):
    n_seq, n_fsdp = lax.axis_size("seq"), lax.axis_size("fsdp")
    n_chunks = queries.shape[2] // PAIR
    near = functools.partial(lax.ppermute, axis_name="seq", perm=swap(n_seq, 0))
    far = functools.partial(lax.ppermute, axis_name="seq", perm=swap(n_seq, 1))

    def cross(x, bits):
        pairs = [
            (s * n_fsdp + g, s * n_fsdp + (g ^ bits[s % 2]))
            for s in range(n_seq)
            for g in range(n_fsdp)
        ]
        return lax.ppermute(x, ("seq", "fsdp"), pairs)

    def exchange(part):
        dq, own, to_core, to_far = part
        back = far(to_far)
        return dq, own, near(to_core), back

    last = lambda core, group: group ^ 3 if n_fsdp == 4 else 0
    kv, both = join(last, keys, values, d_out, queries)
    limits = limits_of(pattern, valid)
    far_kv, near_kv = far(kv), near(kv)
    if n_fsdp == 4 and n_chunks == 4 and w_out.shape[0] == PAIR:
        got = cross(w_out, (1, 2))
        near_both = near(both)
        far_both = far(hand_on("hand_far", last, near_kv, both))
        early = got, near_kv, far_kv, limits
        got, near_kv, far_kv, limits = lax.optimization_barrier(early)
        *pieces, mine, other = onward(got)
        got_d = [cross(piece, (2, 1)) for piece in pieces]
        near_next = near(hand_on("hand_near", last, far_kv))
        ours = d_out, queries, limits, (kv, near_kv, far_kv)
        own = heads("heads_own", lambda core, group: [(group, 0, ((0, 0, PAIR),), 0)], [w_out], (), *ours)
        near_got = near(mine), near(other)
        near_both, near_got = lax.optimization_barrier((near_both, near_got))
        side = heads(
            "heads_side",
            lambda core, group: [
                (group ^ (1 + core), 1 + core, ((0, 0, HD), (0, HD, HD)), 0),
                (group ^ (2 - core), 2 - core, ((1, 0, HD), (2, 0, HD)), 1 - core),
            ],
            [got, *near_got],
            own,
            *ours,
        )
        got_d, near_next, dq = lax.optimization_barrier((got_d, near_next, side[0]))
        far_both, messages = lax.optimization_barrier((far_both, side[2:]))
        sums = exchange((dq, side[1], *messages))
        halo = near_both, far_both, near_next
        third = last_heads(last, *ours, halo, got_d, [near(x) for x in got_d])
        order = lambda core, group: [group, group ^ 1, group ^ 2, group ^ 3]
        return finish(order, [sums, third], queries.shape)
    full = lax.all_gather(w_out, "fsdp", axis=0, tiled=True)
    ours = d_out, queries, limits, (kv, near_kv, far_kv)
    steps = lambda core, group: [
        (i, i, ((0, i * PAIR, PAIR),), 0) for i in range(n_chunks)
    ]
    part = exchange(heads("heads_all", steps, [full], (), *ours))
    return finish(lambda core, group: list(range(n_chunks)), [part], queries.shape)


def solution(mesh):
    rows = P("fsdp", "seq", None)
    in_specs = (rows, rows, rows, rows, P("fsdp", None), P(), P("fsdp", None))
    return jax.shard_map(
        body, mesh=mesh, in_specs=in_specs, out_specs=(rows,) * 3, check_vma=False
    )
```

```python
import functools

import jax
import jax.numpy as jnp
from jax import lax
from jax.experimental import pallas as pl
from jax.experimental.pallas import tpu as pltpu
from jax.sharding import PartitionSpec as P

HD = 128
PAIR = 2 * HD
PIECE = 32
BRIEF = pl.CostEstimate(flops=1, bytes_accessed=1, transcendentals=0)
F32 = jnp.float32
BF16 = jnp.bfloat16
NT = (((1,), (1,)), ((), ()))
NN = (((1,), (0,)), ((), ()))
TN = (((0,), (0,)), ((), ()))
HBM = pl.BlockSpec(memory_space=pltpu.HBM)
ANY = pl.BlockSpec(memory_space=pl.ANY)
VMEM = pl.BlockSpec(memory_space=pltpu.VMEM)
SMEM = pl.BlockSpec(memory_space=pltpu.SMEM)
PARAMS = pltpu.CompilerParams(vmem_limit_bytes=40 * 2**20)
WIDE = pltpu.CompilerParams(vmem_limit_bytes=58 * 2**20)
SCALE = HD ** (-0.5)


def dot(a, b, dims):
    return lax.dot_general(a, b, dims, preferred_element_type=F32)


def swap(n, offset):
    pairs = []
    for i in range(offset, n - 1, 2):
        pairs += [(i, i + 1), (i + 1, i)]
    return pairs


def place():
    return lax.rem(lax.axis_index("seq"), 2), lax.axis_index("fsdp")


def columns(chunk):
    return pl.ds(pl.multiple_of(chunk * PAIR, PAIR), PAIR)


def call(kernel, name, out_shape, in_specs, out_specs, scratch, *args):
    return pl.pallas_call(
        kernel,
        out_shape=out_shape,
        in_specs=in_specs,
        out_specs=out_specs,
        scratch_shapes=scratch,
        cost_estimate=BRIEF,
        compiler_params=PARAMS,
        name=name,
    )(*args)


def key_limits(pat_ref, val_ref):
    shard = lax.axis_index("seq")
    count = val_ref.shape[1]

    def pair(block):
        return block + 1 - 2 * lax.rem(block + 2, 2)

    def far(block):
        return block - 1 + 2 * lax.rem(block + 2, 2)

    wanted = [(shard, block) for block in (shard, pair(shard), far(shard))]
    for row, other in ((pair(shard), far(pair(shard))), (far(shard), pair(far(shard)))):
        wanted += [(row, block) for block in (row, shard, other)]
    limits = []
    for row, block in wanted:
        held = jnp.clip(row, 0, count - 1)
        listed = pat_ref[0, held] == block
        for entry in range(1, pat_ref.shape[0]):
            listed = jnp.logical_or(listed, pat_ref[entry, held] == block)
        inside = jnp.logical_and(row == held, jnp.logical_and(block >= 0, block < count))
        keys = val_ref[0, jnp.clip(block, 0, count - 1)]
        limits.append(jnp.where(jnp.logical_and(listed, inside), keys, 0))
    return limits


def limits_kernel(pat_ref, val_ref, limit_ref):
    limit_ref[...] = jnp.zeros_like(limit_ref)
    for row, limit in enumerate(key_limits(pat_ref, val_ref)):
        limit_ref[row : row + 1, :] = jnp.full((1, PAIR), limit, jnp.int32)


def limits_of(pattern, valid):
    shape = jax.ShapeDtypeStruct((16, PAIR), jnp.int32)
    return call(limits_kernel, "limits", shape, [SMEM] * 2, VMEM, [], pattern.T, valid)


def join_kernel(k_ref, v_ref, kv_ref, kv, sems):
    tok, width = k_ref.shape[1:]
    arrivals, moves = [], []
    for side, ref in enumerate((k_ref, v_ref)):
        for row in range(0, tok, PIECE):
            rows, i = pl.ds(row, PIECE), len(moves)
            at = (rows, pl.ds(side * width, width))
            arrivals.append(pltpu.make_async_copy(ref.at[0, rows, :], kv.at[at], sems.at[0, i]))
            moves.append(pltpu.make_async_copy(kv.at[at], kv_ref.at[at], sems.at[1, i]))
    for copy in arrivals:
        copy.start()
    for arrival, move in zip(arrivals, moves):
        arrival.wait()
        move.start()
    for move in moves:
        move.wait()


def join(keys, values):
    tok, width = keys.shape[1:]
    kv = (tok, 2 * width)
    return pl.pallas_call(
        join_kernel,
        out_shape=jax.ShapeDtypeStruct(kv, BF16),
        in_specs=[HBM] * 2,
        out_specs=ANY,
        scratch_shapes=[
            pltpu.VMEM(kv, BF16),
            pltpu.SemaphoreType.DMA((2, 2 * (tok // PIECE))),
        ],
        cost_estimate=BRIEF,
        compiler_params=WIDE,
        name="join",
    )(keys, values)


def hand_on_kernel(last, n_whole, *refs):
    core, group = place()
    whole, cut, out_ref = refs[:n_whole], refs[n_whole:-1], refs[-1]
    chunk = last(core, group)
    pieces = [ref[0] for ref in whole]
    for ref in cut:
        if ref.ndim == 3:
            pieces.append(ref[0, :, columns(chunk)])
        else:
            pieces.append(ref[:, columns(chunk)])
            pieces.append(ref[:, columns(chunk + ref.shape[1] // (2 * PAIR))])
    to = 0
    for piece in pieces:
        out_ref[:, to : to + piece.shape[1]] = piece
        to += piece.shape[1]


def hand_on(name, last, whole, cut):
    width = sum(x.shape[2] for x in whole) + sum(PAIR * (1 if x.ndim == 3 else 2) for x in cut)
    shape = jax.ShapeDtypeStruct((cut[0].shape[-2], width), BF16)
    kernel = functools.partial(hand_on_kernel, last, len(whole))
    return call(kernel, name, shape, [VMEM] * (len(whole) + len(cut)), VMEM, [], *whole, *cut)


def onward_kernel(w_ref, *out_refs):
    core, _ = place()
    half = w_ref.shape[0] // 2
    start = pl.multiple_of(core * half, half)
    for ref, first in zip(out_refs, (start, half - start)):
        ref[...] = w_ref[pl.ds(pl.multiple_of(first, half), half), :]


def onward(got):
    rows, depth = got.shape
    shapes = [jax.ShapeDtypeStruct((rows // part, depth), BF16) for part in (2, 2)]
    return call(onward_kernel, "onward", tuple(shapes), [VMEM], (VMEM,) * 2, [], got)


def split_kernel(x_ref, *out_refs):
    for i, ref in enumerate(out_refs):
        ref[...] = x_ref[i * ref.shape[0] : (i + 1) * ref.shape[0], :]


def split(x):
    half = jax.ShapeDtypeStruct((x.shape[0] // 2, x.shape[1]), BF16)
    return call(split_kernel, "split", (half, half), [VMEM], (VMEM,) * 2, [], x)


def diagonal(x):
    zero = jnp.zeros((x.shape[0], HD), x.dtype)
    return jnp.concatenate(
        [
            jnp.concatenate([x[:, :HD], zero], axis=1),
            jnp.concatenate([zero, x[:, HD:]], axis=1),
        ],
        axis=0,
    )


def diagonal_turned(one, two):
    zero = jnp.zeros_like(one)
    return jnp.concatenate(
        [jnp.concatenate([one, zero], axis=1), jnp.concatenate([zero, two], axis=1)], axis=0
    )


def in_order(rows, lead):
    one, two = rows[:HD], rows[HD:]
    if isinstance(lead, int):
        return (one, two) if lead == 0 else (two, one)
    return jnp.where(lead == 0, one, two), jnp.where(lead == 0, two, one)


def key_mask(limit_ref, rows, first, count):
    index = lax.broadcasted_iota(jnp.int32, (rows, PAIR), 0)
    return jnp.concatenate(
        [index < limit_ref[i : i + 1, :] for i in range(first, first + count)], axis=0
    )


def prob_of(k, qd, open_keys):
    score = jnp.where(open_keys, dot(k, qd, NT) * SCALE, -jnp.inf)
    top = jnp.maximum(jnp.max(score, axis=0, keepdims=True), -1e30)
    raised = jnp.exp(score - top)
    total = jnp.maximum(jnp.sum(raised, axis=0, keepdims=True), 1.0)
    return raised * (1.0 / total)


def score_grad(prob, prob_b, v, d):
    d_prob = dot(v, d, NN)
    delta = jnp.sum(prob_b.astype(F32) * d_prob, axis=0, keepdims=True)
    return (prob * (d_prob - delta)).astype(BF16)


def query_grad(d_score, k, tok):
    both = dot(d_score, k, TN) * SCALE
    return jnp.concatenate([both[:tok, :HD], both[tok:, HD:]], axis=1).astype(BF16)


def stacked(refs, cols):
    return jnp.concatenate([ref[:, cols] for ref in refs], axis=0)


def heads_kernel(steps, carried, dy_ref, q_ref, limit_ref, *refs):
    core, group = place()
    kv_refs, w_refs = refs[:3], refs[3 : -4 - carried]
    earlier, outs = refs[-4 - carried : -4], refs[-4:]
    dq_ref, own_ref, to_core_ref, to_far_ref = outs
    for old, out in zip(earlier, outs):
        out[..., : old.shape[-1]] = old[...]
    tok = q_ref.shape[1]
    values_at = kv_refs[0].shape[1] // (2 * PAIR)
    open_keys = key_mask(limit_ref, tok, 0, 3)
    for chunk, slot, pieces, lead in steps(core, group):
        cols, dest = columns(chunk), columns(slot)
        w = jnp.concatenate([w_refs[i][row : row + rows, :] for i, row, rows in pieces], axis=0)
        d = diagonal_turned(*in_order(dot(w, dy_ref[0], NT).astype(BF16), lead))
        qd = diagonal(q_ref[0, :, cols])
        k, v = stacked(kv_refs, cols), stacked(kv_refs, columns(chunk + values_at))
        prob = prob_of(k, qd, open_keys)
        prob_b = prob.astype(BF16)
        d_score = score_grad(prob, prob_b, v, d)
        dq_ref[:, dest] = query_grad(d_score, k, tok)
        for side, grad in enumerate((dot(d_score, qd, NN) * SCALE, dot(prob_b, d, NT))):
            own_ref[side, :, dest] = grad[:tok]
            to_core_ref[side, :, dest] = grad[tok : 2 * tok].astype(BF16)
            to_far_ref[side, :, dest] = grad[2 * tok :].astype(BF16)


def heads(name, steps, weights, earlier, d_out, q, limits, blocks):
    tok = q.shape[1]
    width = len(steps(0, 0)) * PAIR + (earlier[0].shape[1] if earlier else 0)
    return call(
        functools.partial(heads_kernel, steps, len(earlier)),
        name,
        (
            jax.ShapeDtypeStruct((tok, width), BF16),
            jax.ShapeDtypeStruct((2, tok, width), F32),
            jax.ShapeDtypeStruct((2, tok, width), BF16),
            jax.ShapeDtypeStruct((2, tok, width), BF16),
        ),
        [VMEM] * (6 + len(weights) + len(earlier)),
        (VMEM,) * 4,
        [],
        d_out,
        q,
        limits,
        *blocks,
        *weights,
        *earlier,
    )


def last_parts(last, q_ref, near_both, far_both, near_next, kv_refs):
    cols = columns(last(*place()))
    value_cols = columns(last(*place()) + kv_refs[0].shape[1] // (2 * PAIR))
    depth = far_both.shape[1] - 3 * PAIR
    own, near, far = ([ref[:, at] for at in (cols, value_cols)] for ref in kv_refs)
    past_near = [near_next[:, :PAIR], near_next[:, PAIR:]]
    past_far = [far_both[:, depth + PAIR : depth + 2 * PAIR], far_both[:, depth + 2 * PAIR :]]
    at_queries = slice(depth, depth + PAIR)
    return (
        (q_ref[0, :, cols], (own, near, far)),
        (near_both[:, at_queries], (near, own, past_near)),
        (far_both[:, at_queries], (far, own, past_far)),
    )


def joined(parts, side):
    return jnp.concatenate([part[side] for part in parts], axis=0)


def probs_kernel(last, q_ref, limit_ref, *refs):
    *kv_refs, near_both, far_both, near_next, prob_ref = refs
    tok = q_ref.shape[1]
    blocks = last_parts(last, q_ref, near_both, far_both, near_next, kv_refs)
    for block, (q, parts) in enumerate(blocks):
        open_keys = key_mask(limit_ref, tok, 3 * block, 3)
        prob_ref[block] = prob_of(joined(parts, 0), diagonal(q), open_keys)


def turn_kernel(dy_ref, near_both, far_both, *refs):
    *w_refs, out_ref = refs
    depth = dy_ref.shape[2]
    w = jnp.concatenate([ref[...] for ref in w_refs], axis=0)
    dy = jnp.concatenate([dy_ref[0], near_both[:, :depth], far_both[:, :depth]], axis=0)
    out_ref[...] = dot(w, dy, NT).astype(BF16)


def last_kernel(last, dy_ref, q_ref, prob_ref, mine_ref, *refs):
    core, _ = place()
    kv_refs = refs[:3]
    near_both, far_both, near_next, *w_refs, dq_ref, dk_ref, dv_ref = refs[3:]
    tok, depth = q_ref.shape[1], dy_ref.shape[2]
    w = jnp.concatenate([ref[...] for ref in w_refs], axis=0)
    dy = jnp.concatenate([dy_ref[0], near_both[:, :depth], far_both[:, :depth]], axis=0)
    other = dot(w, dy, NT).astype(BF16)
    turned = in_order(jnp.concatenate([mine_ref[...], other], axis=0), core)
    probs, scores, queries, cotangents = [], [], [], []
    blocks = last_parts(last, q_ref, near_both, far_both, near_next, kv_refs)
    for block, (q, parts) in enumerate(blocks):
        qd = diagonal(q)
        d = diagonal_turned(*[half[:, block * tok : (block + 1) * tok] for half in turned])
        prob = prob_ref[block]
        prob_b = prob.astype(BF16)
        d_score = score_grad(prob, prob_b, joined(parts, 1), d)
        if block == 0:
            dq_ref[...] = query_grad(d_score, joined(parts, 0), tok)
        mine = slice(0, tok) if block == 0 else slice(tok, 2 * tok)
        probs.append(prob_b[mine])
        scores.append(d_score[mine])
        queries.append(qd)
        cotangents.append(d)
    scores, probs = jnp.concatenate(scores, axis=1), jnp.concatenate(probs, axis=1)
    dk_ref[...] = (dot(scores, jnp.concatenate(queries, axis=0), NN) * SCALE).astype(BF16)
    dv_ref[...] = dot(probs, jnp.concatenate(cotangents, axis=1), NT).astype(BF16)


def last_heads(last, d_out, q, limits, blocks, halo, mine, other):
    tok = q.shape[1]
    prob = call(
        functools.partial(probs_kernel, last),
        "probs_last",
        jax.ShapeDtypeStruct((3, 3 * tok, PAIR), F32),
        [VMEM] * 8,
        VMEM,
        [],
        q,
        limits,
        *blocks,
        *halo,
    )
    turned = call(
        turn_kernel,
        "turn",
        jax.ShapeDtypeStruct((HD, 3 * tok), BF16),
        [VMEM] * (3 + len(mine)),
        VMEM,
        [],
        d_out,
        *halo[:2],
        *mine,
    )
    return call(
        functools.partial(last_kernel, last),
        "heads_last",
        (jax.ShapeDtypeStruct((tok, PAIR), BF16),) * 3,
        [VMEM] * (10 + len(other)),
        (VMEM,) * 3,
        [],
        d_out,
        q,
        prob,
        turned,
        *blocks,
        *halo,
        *other,
    )


def finish_kernel(chunks, widths, *refs):
    core, group = place()
    outs, stage, sems = refs[-5:-2], refs[-2], refs[-1]
    tok = stage.shape[1]
    copies = []
    slot = at = 0
    for width, summed in widths:
        part = refs[at : at + (3 if summed else 4)]
        at += len(part)
        for step in range(width // PAIR):
            cols = slice(step * PAIR, (step + 1) * PAIR)
            dest = columns(chunks(core, group)[slot])
            stage[3 * slot] = part[0][:, cols]
            for side in range(2):
                if summed:
                    total = part[1 + side][:, cols]
                else:
                    _, own, near, far = part
                    total = own[side, :, cols] + near[side, :, cols].astype(F32)
                    total = (total + far[side, :, cols].astype(F32)).astype(BF16)
                stage[3 * slot + 1 + side] = total
            for index in range(3):
                copy = pltpu.make_async_copy(
                    stage.at[3 * slot + index], outs[index].at[0, :, dest], sems.at[3 * slot + index]
                )
                copy.start()
                copies.append(copy)
            slot += 1
    for copy in copies:
        copy.wait()


def finish(chunks, parts, shape):
    count = len(chunks(0, 0))
    ins = [x for part in parts for x in part]
    widths = tuple((part[0].shape[1], len(part) == 3) for part in parts)
    return call(
        functools.partial(finish_kernel, chunks, widths),
        "finish",
        (jax.ShapeDtypeStruct(shape, BF16),) * 3,
        [VMEM] * len(ins),
        (ANY,) * 3,
        [
            pltpu.VMEM((3 * count, shape[1], PAIR), BF16),
            pltpu.SemaphoreType.DMA((3 * count,)),
        ],
        *ins,
    )


def body(queries, keys, values, d_out, w_out, pattern, valid):
    n_seq, n_fsdp = lax.axis_size("seq"), lax.axis_size("fsdp")
    n_chunks = queries.shape[2] // PAIR
    near = functools.partial(lax.ppermute, axis_name="seq", perm=swap(n_seq, 0))
    far = functools.partial(lax.ppermute, axis_name="seq", perm=swap(n_seq, 1))

    def cross(x, bits):
        pairs = [
            (s * n_fsdp + g, s * n_fsdp + (g ^ bits[s % 2]))
            for s in range(n_seq)
            for g in range(n_fsdp)
        ]
        return lax.ppermute(x, ("seq", "fsdp"), pairs)

    def exchange(part):
        dq, own, to_core, to_far = part
        back = far(to_far)
        return dq, own, near(to_core), back

    last = lambda core, group: group ^ 3 if n_fsdp == 4 else 0
    kv = join(keys, values)
    limits = limits_of(pattern, valid)
    far_kv, near_kv = far(kv), near(kv)
    if n_fsdp == 4 and n_chunks == 4 and w_out.shape[0] == PAIR:
        got = cross(w_out, (1, 2))
        message = hand_on("hand_far", last, [d_out], [queries, near_kv])
        far_both, near_both = far(message), near(message)
        early = got, near_kv, far_kv, limits
        got, near_kv, far_kv, limits = lax.optimization_barrier(early)
        mine, other = onward(got)
        got_d = cross(mine, (2, 1))
        near_next = near(hand_on("hand_near", last, [], [far_kv]))
        ours = d_out, queries, limits, (kv, near_kv, far_kv)
        own = heads("heads_own", lambda core, group: [(group, 0, ((0, 0, PAIR),), 0)], [w_out], (), *ours)
        near_got = near(mine), near(other)
        near_both, near_got = lax.optimization_barrier((near_both, near_got))
        side = heads(
            "heads_side",
            lambda core, group: [
                (group ^ (1 + core), 1 + core, ((0, 0, HD), (0, HD, HD)), 0),
                (group ^ (2 - core), 2 - core, ((1, 0, HD), (2, 0, HD)), 1 - core),
            ],
            [got, *near_got],
            own,
            *ours,
        )
        got_d, near_next, far_both, dq = lax.optimization_barrier(
            (got_d, near_next, far_both, side[0])
        )
        sums = exchange((dq, *side[1:]))
        halo = near_both, far_both, near_next
        third = last_heads(last, *ours, halo, [got_d], [near(x) for x in split(got_d)])
        order = lambda core, group: [group, group ^ 1, group ^ 2, group ^ 3]
        return finish(order, [sums, third], queries.shape)
    full = lax.all_gather(w_out, "fsdp", axis=0, tiled=True)
    ours = d_out, queries, limits, (kv, near_kv, far_kv)
    steps = lambda core, group: [
        (i, i, ((0, i * PAIR, PAIR),), 0) for i in range(n_chunks)
    ]
    part = exchange(heads("heads_all", steps, [full], (), *ours))
    return finish(lambda core, group: list(range(n_chunks)), [part], queries.shape)


def solution(mesh):
    rows = P("fsdp", "seq", None)
    in_specs = (rows, rows, rows, rows, P("fsdp", None), P(), P("fsdp", None))
    return jax.shard_map(
        body, mesh=mesh, in_specs=in_specs, out_specs=(rows,) * 3, check_vma=False
    )
```

```python
import functools

import jax
import jax.numpy as jnp
from jax import lax
from jax.experimental import pallas as pl
from jax.experimental.pallas import tpu as pltpu
from jax.sharding import PartitionSpec as P

HD = 128
PAIR = 2 * HD
PIECE = 32
BRIEF = pl.CostEstimate(flops=1, bytes_accessed=1, transcendentals=0)
F32 = jnp.float32
BF16 = jnp.bfloat16
NT = (((1,), (1,)), ((), ()))
NN = (((1,), (0,)), ((), ()))
TN = (((0,), (0,)), ((), ()))
HBM = pl.BlockSpec(memory_space=pltpu.HBM)
ANY = pl.BlockSpec(memory_space=pl.ANY)
VMEM = pl.BlockSpec(memory_space=pltpu.VMEM)
SMEM = pl.BlockSpec(memory_space=pltpu.SMEM)
PARAMS = pltpu.CompilerParams(vmem_limit_bytes=40 * 2**20)
WIDE = pltpu.CompilerParams(vmem_limit_bytes=58 * 2**20)
SCALE = HD ** (-0.5)


def dot(a, b, dims):
    return lax.dot_general(a, b, dims, preferred_element_type=F32)


def swap(n, offset):
    pairs = []
    for i in range(offset, n - 1, 2):
        pairs += [(i, i + 1), (i + 1, i)]
    return pairs


def place():
    return lax.rem(lax.axis_index("seq"), 2), lax.axis_index("fsdp")


def columns(chunk):
    return pl.ds(pl.multiple_of(chunk * PAIR, PAIR), PAIR)


def call(kernel, name, out_shape, in_specs, out_specs, scratch, *args):
    return pl.pallas_call(
        kernel,
        out_shape=out_shape,
        in_specs=in_specs,
        out_specs=out_specs,
        scratch_shapes=scratch,
        cost_estimate=BRIEF,
        compiler_params=PARAMS,
        name=name,
    )(*args)


def key_limits(pat_ref, val_ref):
    shard = lax.axis_index("seq")
    count = val_ref.shape[1]

    def pair(block):
        return block + 1 - 2 * lax.rem(block + 2, 2)

    def far(block):
        return block - 1 + 2 * lax.rem(block + 2, 2)

    wanted = [(shard, block) for block in (shard, pair(shard), far(shard))]
    for row, other in ((pair(shard), far(pair(shard))), (far(shard), pair(far(shard)))):
        wanted += [(row, block) for block in (row, shard, other)]
    limits = []
    for row, block in wanted:
        held = jnp.clip(row, 0, count - 1)
        listed = pat_ref[0, held] == block
        for entry in range(1, pat_ref.shape[0]):
            listed = jnp.logical_or(listed, pat_ref[entry, held] == block)
        inside = jnp.logical_and(row == held, jnp.logical_and(block >= 0, block < count))
        keys = val_ref[0, jnp.clip(block, 0, count - 1)]
        limits.append(jnp.where(jnp.logical_and(listed, inside), keys, 0))
    return limits


def limits_kernel(pat_ref, val_ref, limit_ref):
    limit_ref[...] = jnp.zeros_like(limit_ref)
    for row, limit in enumerate(key_limits(pat_ref, val_ref)):
        limit_ref[row : row + 1, :] = jnp.full((1, PAIR), limit, jnp.int32)


def limits_of(pattern, valid):
    shape = jax.ShapeDtypeStruct((16, PAIR), jnp.int32)
    return call(limits_kernel, "limits", shape, [SMEM] * 2, VMEM, [], pattern.T, valid)


def join_kernel(k_ref, v_ref, kv_ref, kv, sems):
    tok, width = k_ref.shape[1:]
    arrivals, moves = [], []
    for side, ref in enumerate((k_ref, v_ref)):
        for row in range(0, tok, PIECE):
            rows, i = pl.ds(row, PIECE), len(moves)
            at = (rows, pl.ds(side * width, width))
            arrivals.append(pltpu.make_async_copy(ref.at[0, rows, :], kv.at[at], sems.at[0, i]))
            moves.append(pltpu.make_async_copy(kv.at[at], kv_ref.at[at], sems.at[1, i]))
    for copy in arrivals:
        copy.start()
    for arrival, move in zip(arrivals, moves):
        arrival.wait()
        move.start()
    for move in moves:
        move.wait()


def join(keys, values):
    tok, width = keys.shape[1:]
    kv = (tok, 2 * width)
    return pl.pallas_call(
        join_kernel,
        out_shape=jax.ShapeDtypeStruct(kv, BF16),
        in_specs=[HBM] * 2,
        out_specs=ANY,
        scratch_shapes=[
            pltpu.VMEM(kv, BF16),
            pltpu.SemaphoreType.DMA((2, 2 * (tok // PIECE))),
        ],
        cost_estimate=BRIEF,
        compiler_params=WIDE,
        name="join",
    )(keys, values)


def hand_on_kernel(last, n_whole, *refs):
    core, group = place()
    whole, cut, out_ref = refs[:n_whole], refs[n_whole:-1], refs[-1]
    chunk = last(core, group)
    pieces = [ref[0] for ref in whole]
    for ref in cut:
        if ref.ndim == 3:
            pieces.append(ref[0, :, columns(chunk)])
        else:
            pieces.append(ref[:, columns(chunk)])
            pieces.append(ref[:, columns(chunk + ref.shape[1] // (2 * PAIR))])
    to = 0
    for piece in pieces:
        out_ref[:, to : to + piece.shape[1]] = piece
        to += piece.shape[1]


def hand_on(name, last, whole, cut):
    width = sum(x.shape[2] for x in whole) + sum(PAIR * (1 if x.ndim == 3 else 2) for x in cut)
    shape = jax.ShapeDtypeStruct((cut[0].shape[-2], width), BF16)
    kernel = functools.partial(hand_on_kernel, last, len(whole))
    return call(kernel, name, shape, [VMEM] * (len(whole) + len(cut)), VMEM, [], *whole, *cut)


def onward_kernel(last, w_ref, kv_ref, mine_ref, *both_refs):
    core, group = place()
    half, depth = mine_ref.shape
    chunk = last(core, group)
    mine_ref[...] = w_ref[pl.ds(pl.multiple_of(core * half, half), half), :]
    for side, (ref, which) in enumerate(zip(both_refs, (core, 1 - core))):
        ref[:, :depth] = w_ref[pl.ds(pl.multiple_of(which * half, half), half), :]
        ref[:, depth:] = kv_ref[:, columns(chunk + side * (kv_ref.shape[1] // (2 * PAIR)))]


def onward(last, got, kv):
    rows, depth = got.shape
    half, wide = (rows // 2, depth), (rows // 2, depth + PAIR)
    shapes = tuple(jax.ShapeDtypeStruct(shape, BF16) for shape in (half, wide, wide))
    kernel = functools.partial(onward_kernel, last)
    return call(kernel, "onward", shapes, [VMEM] * 2, (VMEM,) * 3, [], got, kv)


def split_kernel(x_ref, *out_refs):
    for i, ref in enumerate(out_refs):
        ref[...] = x_ref[i * ref.shape[0] : (i + 1) * ref.shape[0], :]


def split(x):
    half = jax.ShapeDtypeStruct((x.shape[0] // 2, x.shape[1]), BF16)
    return call(split_kernel, "split", (half, half), [VMEM], (VMEM,) * 2, [], x)


def diagonal(x):
    zero = jnp.zeros((x.shape[0], HD), x.dtype)
    return jnp.concatenate(
        [
            jnp.concatenate([x[:, :HD], zero], axis=1),
            jnp.concatenate([zero, x[:, HD:]], axis=1),
        ],
        axis=0,
    )


def diagonal_turned(one, two):
    zero = jnp.zeros_like(one)
    return jnp.concatenate(
        [jnp.concatenate([one, zero], axis=1), jnp.concatenate([zero, two], axis=1)], axis=0
    )


def in_order(rows, lead):
    one, two = rows[:HD], rows[HD:]
    if isinstance(lead, int):
        return (one, two) if lead == 0 else (two, one)
    return jnp.where(lead == 0, one, two), jnp.where(lead == 0, two, one)


def key_mask(limit_ref, rows, first, count):
    index = lax.broadcasted_iota(jnp.int32, (rows, PAIR), 0)
    return jnp.concatenate(
        [index < limit_ref[i : i + 1, :] for i in range(first, first + count)], axis=0
    )


def prob_of(k, qd, open_keys):
    score = jnp.where(open_keys, dot(k, qd, NT) * SCALE, -jnp.inf)
    top = jnp.maximum(jnp.max(score, axis=0, keepdims=True), -1e30)
    raised = jnp.exp(score - top)
    total = jnp.maximum(jnp.sum(raised, axis=0, keepdims=True), 1.0)
    return raised * (1.0 / total)


def score_grad(prob, prob_b, v, d):
    d_prob = dot(v, d, NN)
    delta = jnp.sum(prob_b.astype(F32) * d_prob, axis=0, keepdims=True)
    return (prob * (d_prob - delta)).astype(BF16)


def query_grad(d_score, k, tok):
    both = dot(d_score, k, TN) * SCALE
    return jnp.concatenate([both[:tok, :HD], both[tok:, HD:]], axis=1).astype(BF16)


def stacked(refs, cols):
    return jnp.concatenate([ref[:, cols] for ref in refs], axis=0)


def heads_kernel(steps, messages, dy_ref, q_ref, limit_ref, *refs):
    core, group = place()
    k_refs, w_refs = refs[:3], refs[3 : -4 - messages]
    earlier, (dq_ref, own_ref, *message_refs) = refs[-4 - messages : -4], refs[-4:]
    for old, out in zip(earlier, message_refs):
        out[...] = old[...]
    tok, depth = q_ref.shape[1], dy_ref.shape[2]
    values_at = k_refs[0].shape[1] // (2 * PAIR)
    open_keys = key_mask(limit_ref, tok, 0, 3)
    for chunk, slot, message_slot, pieces, lead in steps(core, group):
        cols, dest, message_dest = columns(chunk), columns(slot), columns(message_slot)
        w = jnp.concatenate([w_refs[i][row : row + rows, :depth] for i, row, rows in pieces], axis=0)
        d = diagonal_turned(*in_order(dot(w, dy_ref[0], NT).astype(BF16), lead))
        qd = diagonal(q_ref[0, :, cols])
        k, v = stacked(k_refs, cols), stacked(k_refs, columns(chunk + values_at))
        prob = prob_of(k, qd, open_keys)
        prob_b = prob.astype(BF16)
        d_score = score_grad(prob, prob_b, v, d)
        dq_ref[:, dest] = query_grad(d_score, k, tok)
        for side, grad in enumerate((dot(d_score, qd, NN) * SCALE, dot(prob_b, d, NT))):
            own_ref[side, :, dest] = grad[:tok]
            for i, ref in enumerate(message_refs, 1):
                ref[side, :, message_dest] = grad[i * tok : (i + 1) * tok].astype(BF16)


def heads(name, steps, places, weights, earlier, d_out, q, limits, blocks):
    tok = q.shape[1]
    width = len(steps(0, 0)) * PAIR
    message = jax.ShapeDtypeStruct((2, tok, places * PAIR), BF16)
    return call(
        functools.partial(heads_kernel, steps, len(earlier)),
        name,
        (
            jax.ShapeDtypeStruct((tok, width), BF16),
            jax.ShapeDtypeStruct((2, tok, width), F32),
            message,
            message,
        ),
        [VMEM] * (6 + len(weights) + len(earlier)),
        (VMEM,) * 4,
        [],
        d_out,
        q,
        limits,
        *blocks,
        *weights,
        *earlier,
    )


def last_parts(last, q_ref, near_both, far_both, near_next, kv_refs):
    cols = columns(last(*place()))
    value_cols = columns(last(*place()) + kv_refs[0].shape[1] // (2 * PAIR))
    depth = far_both.shape[1] - 3 * PAIR
    own, near, far = ([ref[:, at] for at in (cols, value_cols)] for ref in kv_refs)
    past_near = [ref[:, depth:] for ref in near_next]
    past_far = [far_both[:, depth + PAIR : depth + 2 * PAIR], far_both[:, depth + 2 * PAIR :]]
    at_queries = slice(depth, depth + PAIR)
    return (
        (q_ref[0, :, cols], (own, near, far)),
        (near_both[:, at_queries], (near, own, past_near)),
        (far_both[:, at_queries], (far, own, past_far)),
    )


def joined(parts, side):
    return jnp.concatenate([part[side] for part in parts], axis=0)


def probs_kernel(last, q_ref, limit_ref, *refs):
    *kv_refs, near_both, far_both = refs[:5]
    near_next, prob_ref = refs[5:7], refs[7]
    tok = q_ref.shape[1]
    blocks = last_parts(last, q_ref, near_both, far_both, near_next, kv_refs)
    for block, (q, parts) in enumerate(blocks):
        open_keys = key_mask(limit_ref, tok, 3 * block, 3)
        prob_ref[block] = prob_of(joined(parts, 0), diagonal(q), open_keys)


def turn_kernel(dy_ref, near_both, far_both, *refs):
    *w_refs, out_ref = refs
    depth = dy_ref.shape[2]
    w = jnp.concatenate([ref[...] for ref in w_refs], axis=0)
    dy = jnp.concatenate([dy_ref[0], near_both[:, :depth], far_both[:, :depth]], axis=0)
    out_ref[...] = dot(w, dy, NT).astype(BF16)


def last_kernel(last, dy_ref, q_ref, prob_ref, mine_ref, *refs):
    core, _ = place()
    kv_refs = refs[:3]
    near_both, far_both, *near_next = refs[3:7]
    *w_refs, dq_ref, dk_ref, dv_ref = refs[7:]
    tok, depth = q_ref.shape[1], dy_ref.shape[2]
    w = jnp.concatenate([ref[...] for ref in w_refs], axis=0)
    dy = jnp.concatenate([dy_ref[0], near_both[:, :depth], far_both[:, :depth]], axis=0)
    other = dot(w, dy, NT).astype(BF16)
    turned = in_order(jnp.concatenate([mine_ref[...], other], axis=0), core)
    probs, scores, queries, cotangents = [], [], [], []
    blocks = last_parts(last, q_ref, near_both, far_both, near_next, kv_refs)
    for block, (q, parts) in enumerate(blocks):
        qd = diagonal(q)
        d = diagonal_turned(*[half[:, block * tok : (block + 1) * tok] for half in turned])
        prob = prob_ref[block]
        prob_b = prob.astype(BF16)
        d_score = score_grad(prob, prob_b, joined(parts, 1), d)
        if block == 0:
            dq_ref[...] = query_grad(d_score, joined(parts, 0), tok)
        mine = slice(0, tok) if block == 0 else slice(tok, 2 * tok)
        probs.append(prob_b[mine])
        scores.append(d_score[mine])
        queries.append(qd)
        cotangents.append(d)
    scores, probs = jnp.concatenate(scores, axis=1), jnp.concatenate(probs, axis=1)
    dk_ref[...] = (dot(scores, jnp.concatenate(queries, axis=0), NN) * SCALE).astype(BF16)
    dv_ref[...] = dot(probs, jnp.concatenate(cotangents, axis=1), NT).astype(BF16)


def last_probs(last, q, limits, blocks, halo):
    tok = q.shape[1]
    return call(
        functools.partial(probs_kernel, last),
        "probs_last",
        jax.ShapeDtypeStruct((3, 3 * tok, PAIR), F32),
        [VMEM] * 9,
        VMEM,
        [],
        q,
        limits,
        *blocks,
        *halo,
    )


def last_heads(last, prob, d_out, q, blocks, halo, mine, other):
    tok = q.shape[1]
    turned = call(
        turn_kernel,
        "turn",
        jax.ShapeDtypeStruct((HD, 3 * tok), BF16),
        [VMEM] * (3 + len(mine)),
        VMEM,
        [],
        d_out,
        *halo[:2],
        *mine,
    )
    return call(
        functools.partial(last_kernel, last),
        "heads_last",
        (jax.ShapeDtypeStruct((tok, PAIR), BF16),) * 3,
        [VMEM] * (11 + len(other)),
        (VMEM,) * 3,
        [],
        d_out,
        q,
        prob,
        turned,
        *blocks,
        *halo,
        *other,
    )


class Columns:
    def __init__(self, stage, sems):
        self.stage, self.sems, self.copies = stage, sems, []

    def put(self, out_ref, chunk, value):
        at = len(self.copies)
        self.stage[at] = value
        target = out_ref.at[0, :, columns(chunk)]
        copy = pltpu.make_async_copy(self.stage.at[at], target, self.sems.at[at])
        copy.start()
        self.copies.append(copy)

    def wait(self):
        for copy in self.copies:
            copy.wait()


def scratch_of(count, tok):
    return [pltpu.VMEM((count, tok, PAIR), BF16), pltpu.SemaphoreType.DMA((count,))]


def settle_kernel(order, widths, *refs):
    outs, to = refs[-5:-2], Columns(*refs[-2:])
    pairs = order(*place())
    for part, width in enumerate(widths):
        for step in range(width // PAIR):
            cols = slice(step * PAIR, (step + 1) * PAIR)
            to.put(outs[0], pairs[part][step][0], refs[part][:, cols])
    for out_ref, ref in zip(outs[1:], refs[len(widths) : -5]):
        to.put(out_ref, pairs[-1][0][0], ref[...])
    to.wait()


def settle(order, d_queries, last, shape):
    widths = tuple(x.shape[1] for x in d_queries)
    count = sum(widths) // PAIR + len(last)
    ins = [*d_queries, *last]
    return call(
        functools.partial(settle_kernel, order, widths),
        "settle",
        (jax.ShapeDtypeStruct(shape, BF16),) * 3,
        [VMEM] * len(ins),
        (ANY,) * 3,
        scratch_of(count, shape[1]),
        *ins,
    )


def finish_kernel(order, widths, far, near, *refs):
    outs, to = refs[-4:-2], Columns(*refs[-2:])
    pairs = order(*place())
    for part, width in enumerate(widths):
        own = refs[part]
        for step in range(width // PAIR):
            cols = slice(step * PAIR, (step + 1) * PAIR)
            chunk, message_slot = pairs[part][step]
            at = columns(message_slot)
            for side, out_ref in enumerate(outs):
                total = own[side, :, cols] + near[side, :, at].astype(F32)
                to.put(out_ref, chunk, (total + far[side, :, at].astype(F32)).astype(BF16))
    to.wait()


def finish(order, far, near, parts, old):
    shape = old[0].shape
    widths = tuple(x.shape[2] for x in parts)
    ins = [far, near, *parts]
    return pl.pallas_call(
        functools.partial(finish_kernel, order, widths),
        out_shape=(jax.ShapeDtypeStruct(shape, BF16),) * 2,
        in_specs=[VMEM] * len(ins) + [ANY] * 2,
        out_specs=(ANY,) * 2,
        scratch_shapes=scratch_of(2 * sum(widths) // PAIR, shape[1]),
        input_output_aliases={len(ins): 0, len(ins) + 1: 1},
        cost_estimate=BRIEF,
        compiler_params=PARAMS,
        name="finish",
    )(*ins, *old)


def body(queries, keys, values, d_out, w_out, pattern, valid):
    n_seq, n_fsdp = lax.axis_size("seq"), lax.axis_size("fsdp")
    n_chunks = queries.shape[2] // PAIR
    near = functools.partial(lax.ppermute, axis_name="seq", perm=swap(n_seq, 0))
    far = functools.partial(lax.ppermute, axis_name="seq", perm=swap(n_seq, 1))

    def cross(x, bits):
        pairs = [
            (s * n_fsdp + g, s * n_fsdp + (g ^ bits[s % 2]))
            for s in range(n_seq)
            for g in range(n_fsdp)
        ]
        return lax.ppermute(x, ("seq", "fsdp"), pairs)

    last = lambda core, group: group ^ 3 if n_fsdp == 4 else 0
    kv = join(keys, values)
    limits = limits_of(pattern, valid)
    far_kv, near_kv = far(kv), near(kv)
    if n_fsdp == 4 and n_chunks == 4 and w_out.shape[0] == PAIR:
        got = cross(w_out, (1, 2))
        message = hand_on("hand_far", last, [d_out], [queries, near_kv])
        far_both, near_both = far(message), near(message)
        early = got, near_kv, far_kv, limits
        got, near_kv, far_kv, limits = lax.optimization_barrier(early)
        ours = d_out, queries, limits, (kv, near_kv, far_kv)
        mine, *both = onward(last, got, far_kv)
        got_d = cross(mine, (2, 1))
        near_got = [near(x) for x in both]
        first = heads(
            "heads_first",
            lambda core, group: [
                (group, 0, 0, ((0, 0, PAIR),), 0),
                (group ^ (1 + core), 1, 1 + core, ((1, 0, PAIR),), 0),
            ],
            3,
            [w_out, got],
            (),
            *ours,
        )
        near_both, near_got, dq = lax.optimization_barrier((near_both, near_got, first[0]))
        second = heads(
            "heads_second",
            lambda core, group: [(group ^ (2 - core), 0, 2 - core, ((0, 0, HD), (1, 0, HD)), 1 - core)],
            3,
            near_got,
            first[2:],
            *ours,
        )
        halo = near_both, far_both, *near_got
        prob = last_probs(last, *ours[1:], halo)
        got_d, halo, prob, second_dq = lax.optimization_barrier((got_d, halo, prob, second[0]))
        sums = far(second[3]), near(second[2])
        third = last_heads(last, prob, *ours[:2], ours[3], halo, [got_d], [near(x) for x in split(got_d)])
        order = lambda core, group: [
            [(group, 0), (group ^ (1 + core), 1 + core)],
            [(group ^ (2 - core), 2 - core)],
            [(group ^ 3, 0)],
        ]
        d_queries, *old = settle(order, (dq, second_dq, third[0]), third[1:], queries.shape)
        return d_queries, *finish(order, *sums, (first[1], second[1]), old)
    full = lax.all_gather(w_out, "fsdp", axis=0, tiled=True)
    ours = d_out, queries, limits, (kv, near_kv, far_kv)
    steps = lambda core, group: [
        (i, i, i, ((0, i * PAIR, PAIR),), 0) for i in range(n_chunks)
    ]
    dq, own, to_core, to_far = heads("heads_all", steps, n_chunks, [full], (), *ours)
    order = lambda core, group: [[(i, i) for i in range(n_chunks)]]
    d_queries, *old = settle(order, (dq,), (), queries.shape)
    return d_queries, *finish(order, far(to_far), near(to_core), (own,), old)


def solution(mesh):
    rows = P("fsdp", "seq", None)
    in_specs = (rows, rows, rows, rows, P("fsdp", None), P(), P("fsdp", None))
    return jax.shard_map(
        body, mesh=mesh, in_specs=in_specs, out_specs=(rows,) * 3, check_vma=False
    )
```

```python
import functools

import jax
import jax.numpy as jnp
from jax import lax
from jax.experimental import pallas as pl
from jax.experimental.pallas import tpu as pltpu
from jax.sharding import PartitionSpec as P

HD = 128
PAIR = 2 * HD
PIECE = 32
BRIEF = pl.CostEstimate(flops=1, bytes_accessed=1, transcendentals=0)
F32 = jnp.float32
BF16 = jnp.bfloat16
NT = (((1,), (1,)), ((), ()))
NN = (((1,), (0,)), ((), ()))
TN = (((0,), (0,)), ((), ()))
HBM = pl.BlockSpec(memory_space=pltpu.HBM)
ANY = pl.BlockSpec(memory_space=pl.ANY)
VMEM = pl.BlockSpec(memory_space=pltpu.VMEM)
SMEM = pl.BlockSpec(memory_space=pltpu.SMEM)
PARAMS = pltpu.CompilerParams(vmem_limit_bytes=40 * 2**20)
WIDE = pltpu.CompilerParams(vmem_limit_bytes=58 * 2**20)
SCALE = HD ** (-0.5)


def dot(a, b, dims):
    return lax.dot_general(a, b, dims, preferred_element_type=F32)


def swap(n, offset):
    pairs = []
    for i in range(offset, n - 1, 2):
        pairs += [(i, i + 1), (i + 1, i)]
    return pairs


def place():
    return lax.rem(lax.axis_index("seq"), 2), lax.axis_index("fsdp")


def columns(chunk):
    return pl.ds(pl.multiple_of(chunk * PAIR, PAIR), PAIR)


def call(kernel, name, out_shape, in_specs, out_specs, scratch, *args):
    return pl.pallas_call(
        kernel,
        out_shape=out_shape,
        in_specs=in_specs,
        out_specs=out_specs,
        scratch_shapes=scratch,
        cost_estimate=BRIEF,
        compiler_params=PARAMS,
        name=name,
    )(*args)


def key_limits(pat_ref, val_ref):
    shard = lax.axis_index("seq")
    count = val_ref.shape[1]

    def pair(block):
        return block + 1 - 2 * lax.rem(block + 2, 2)

    def far(block):
        return block - 1 + 2 * lax.rem(block + 2, 2)

    wanted = [(shard, block) for block in (shard, pair(shard), far(shard))]
    for row, other in ((pair(shard), far(pair(shard))), (far(shard), pair(far(shard)))):
        wanted += [(row, block) for block in (row, shard, other)]
    limits = []
    for row, block in wanted:
        held = jnp.clip(row, 0, count - 1)
        listed = pat_ref[0, held] == block
        for entry in range(1, pat_ref.shape[0]):
            listed = jnp.logical_or(listed, pat_ref[entry, held] == block)
        inside = jnp.logical_and(row == held, jnp.logical_and(block >= 0, block < count))
        keys = val_ref[0, jnp.clip(block, 0, count - 1)]
        limits.append(jnp.where(jnp.logical_and(listed, inside), keys, 0))
    return limits


def limits_kernel(pat_ref, val_ref, limit_ref):
    limit_ref[...] = jnp.zeros_like(limit_ref)
    for row, limit in enumerate(key_limits(pat_ref, val_ref)):
        limit_ref[row : row + 1, :] = jnp.full((1, PAIR), limit, jnp.int32)


def limits_of(pattern, valid):
    shape = jax.ShapeDtypeStruct((16, PAIR), jnp.int32)
    return call(limits_kernel, "limits", shape, [SMEM] * 2, VMEM, [], pattern.T, valid)


def join_kernel(k_ref, v_ref, kv_ref, kv, sems):
    tok, width = k_ref.shape[1:]
    arrivals, moves = [], []
    for side, ref in enumerate((k_ref, v_ref)):
        for row in range(0, tok, PIECE):
            rows, i = pl.ds(row, PIECE), len(moves)
            at = (rows, pl.ds(side * width, width))
            arrivals.append(pltpu.make_async_copy(ref.at[0, rows, :], kv.at[at], sems.at[0, i]))
            moves.append(pltpu.make_async_copy(kv.at[at], kv_ref.at[at], sems.at[1, i]))
    for copy in arrivals:
        copy.start()
    for arrival, move in zip(arrivals, moves):
        arrival.wait()
        move.start()
    for move in moves:
        move.wait()


def join(keys, values):
    tok, width = keys.shape[1:]
    kv = (tok, 2 * width)
    return pl.pallas_call(
        join_kernel,
        out_shape=jax.ShapeDtypeStruct(kv, BF16),
        in_specs=[HBM] * 2,
        out_specs=ANY,
        scratch_shapes=[
            pltpu.VMEM(kv, BF16),
            pltpu.SemaphoreType.DMA((2, 2 * (tok // PIECE))),
        ],
        cost_estimate=BRIEF,
        compiler_params=WIDE,
        name="join",
    )(keys, values)


def hand_on_kernel(last, n_whole, *refs):
    core, group = place()
    whole, cut, out_ref = refs[:n_whole], refs[n_whole:-1], refs[-1]
    chunk = last(core, group)
    pieces = [ref[0] for ref in whole]
    for ref in cut:
        if ref.ndim == 3:
            pieces.append(ref[0, :, columns(chunk)])
        else:
            pieces.append(ref[:, columns(chunk)])
            pieces.append(ref[:, columns(chunk + ref.shape[1] // (2 * PAIR))])
    to = 0
    for piece in pieces:
        out_ref[:, to : to + piece.shape[1]] = piece
        to += piece.shape[1]


def hand_on(name, last, whole, cut):
    width = sum(x.shape[2] for x in whole) + sum(PAIR * (1 if x.ndim == 3 else 2) for x in cut)
    shape = jax.ShapeDtypeStruct((cut[0].shape[-2], width), BF16)
    kernel = functools.partial(hand_on_kernel, last, len(whole))
    return call(kernel, name, shape, [VMEM] * (len(whole) + len(cut)), VMEM, [], *whole, *cut)


def turned_kernel(dy_ref, out_ref):
    out_ref[...] = dy_ref[0].T


def turned_rows(d_out):
    shape = jax.ShapeDtypeStruct(d_out.shape[:0:-1], BF16)
    return call(turned_kernel, "turned", shape, [VMEM], VMEM, [], d_out)


def onward_kernel(last, w_ref, kv_ref, mine_ref, *both_refs):
    core, group = place()
    half, depth = mine_ref.shape
    chunk = last(core, group)
    mine_ref[...] = w_ref[pl.ds(pl.multiple_of(core * half, half), half), :]
    for side, (ref, which) in enumerate(zip(both_refs, (core, 1 - core))):
        ref[:, :depth] = w_ref[pl.ds(pl.multiple_of(which * half, half), half), :]
        ref[:, depth:] = kv_ref[:, columns(chunk + side * (kv_ref.shape[1] // (2 * PAIR)))]


def onward(last, got, kv):
    rows, depth = got.shape
    half, wide = (rows // 2, depth), (rows // 2, depth + PAIR)
    shapes = tuple(jax.ShapeDtypeStruct(shape, BF16) for shape in (half, wide, wide))
    kernel = functools.partial(onward_kernel, last)
    return call(kernel, "onward", shapes, [VMEM] * 2, (VMEM,) * 3, [], got, kv)


def split_kernel(x_ref, *out_refs):
    for i, ref in enumerate(out_refs):
        ref[...] = x_ref[i * ref.shape[0] : (i + 1) * ref.shape[0], :]


def split(x):
    half = jax.ShapeDtypeStruct((x.shape[0] // 2, x.shape[1]), BF16)
    return call(split_kernel, "split", (half, half), [VMEM], (VMEM,) * 2, [], x)


def diagonal(x):
    zero = jnp.zeros((x.shape[0], HD), x.dtype)
    return jnp.concatenate(
        [
            jnp.concatenate([x[:, :HD], zero], axis=1),
            jnp.concatenate([zero, x[:, HD:]], axis=1),
        ],
        axis=0,
    )


def diagonal_turned(one, two):
    zero = jnp.zeros_like(one)
    return jnp.concatenate(
        [jnp.concatenate([one, zero], axis=1), jnp.concatenate([zero, two], axis=1)], axis=0
    )


def in_order(rows, lead):
    one, two = rows[:HD], rows[HD:]
    if isinstance(lead, int):
        return (one, two) if lead == 0 else (two, one)
    return jnp.where(lead == 0, one, two), jnp.where(lead == 0, two, one)


def key_mask(limit_ref, rows, first, count):
    index = lax.broadcasted_iota(jnp.int32, (rows, PAIR), 0)
    return jnp.concatenate(
        [index < limit_ref[i : i + 1, :] for i in range(first, first + count)], axis=0
    )


def prob_of(k, qd, open_keys):
    score = jnp.where(open_keys, dot(k, qd, NT) * SCALE, -jnp.inf)
    top = jnp.maximum(jnp.max(score, axis=0, keepdims=True), -1e30)
    raised = jnp.exp(score - top)
    total = jnp.maximum(jnp.sum(raised, axis=0, keepdims=True), 1.0)
    return raised * (1.0 / total)


def score_grad(prob, prob_b, v, d):
    d_prob = dot(v, d, NN)
    delta = jnp.sum(prob_b.astype(F32) * d_prob, axis=0, keepdims=True)
    return (prob * (d_prob - delta)).astype(BF16)


def query_grad(d_score, k, tok):
    both = dot(d_score, k, TN) * SCALE
    return jnp.concatenate([both[:tok, :HD], both[tok:, HD:]], axis=1).astype(BF16)


def stacked(refs, cols):
    return jnp.concatenate([ref[:, cols] for ref in refs], axis=0)


def heads_kernel(steps, messages, dy_ref, q_ref, limit_ref, *refs):
    core, group = place()
    k_refs, w_refs = refs[:3], refs[3 : -4 - messages]
    earlier, (dq_ref, own_ref, *message_refs) = refs[-4 - messages : -4], refs[-4:]
    for old, out in zip(earlier, message_refs):
        out[...] = old[...]
    tok, depth = q_ref.shape[1], dy_ref.shape[0]
    values_at = k_refs[0].shape[1] // (2 * PAIR)
    open_keys = key_mask(limit_ref, tok, 0, 3)
    for chunk, slot, message_slot, pieces, lead in steps(core, group):
        cols, dest, message_dest = columns(chunk), columns(slot), columns(message_slot)
        w = jnp.concatenate([w_refs[i][row : row + rows, :depth] for i, row, rows in pieces], axis=0)
        d = diagonal_turned(*in_order(dot(w, dy_ref[...], NN).astype(BF16), lead))
        qd = diagonal(q_ref[0, :, cols])
        k, v = stacked(k_refs, cols), stacked(k_refs, columns(chunk + values_at))
        prob = prob_of(k, qd, open_keys)
        prob_b = prob.astype(BF16)
        d_score = score_grad(prob, prob_b, v, d)
        dq_ref[:, dest] = query_grad(d_score, k, tok)
        for side, grad in enumerate((dot(d_score, qd, NN) * SCALE, dot(prob_b, d, NT))):
            own_ref[side, :, dest] = grad[:tok]
            for i, ref in enumerate(message_refs, 1):
                ref[side, :, message_dest] = grad[i * tok : (i + 1) * tok].astype(BF16)


def heads(name, steps, places, weights, earlier, d_out, q, limits, blocks):
    tok = q.shape[1]
    width = len(steps(0, 0)) * PAIR
    message = jax.ShapeDtypeStruct((2, tok, places * PAIR), BF16)
    return call(
        functools.partial(heads_kernel, steps, len(earlier)),
        name,
        (
            jax.ShapeDtypeStruct((tok, width), BF16),
            jax.ShapeDtypeStruct((2, tok, width), F32),
            message,
            message,
        ),
        [VMEM] * (6 + len(weights) + len(earlier)),
        (VMEM,) * 4,
        [],
        d_out,
        q,
        limits,
        *blocks,
        *weights,
        *earlier,
    )


def last_parts(last, q_ref, near_both, far_both, near_next, kv_refs):
    cols = columns(last(*place()))
    value_cols = columns(last(*place()) + kv_refs[0].shape[1] // (2 * PAIR))
    depth = far_both.shape[1] - 3 * PAIR
    own, near, far = ([ref[:, at] for at in (cols, value_cols)] for ref in kv_refs)
    past_near = [ref[:, depth:] for ref in near_next]
    past_far = [far_both[:, depth + PAIR : depth + 2 * PAIR], far_both[:, depth + 2 * PAIR :]]
    at_queries = slice(depth, depth + PAIR)
    return (
        (q_ref[0, :, cols], (own, near, far)),
        (near_both[:, at_queries], (near, own, past_near)),
        (far_both[:, at_queries], (far, own, past_far)),
    )


def joined(parts, side):
    return jnp.concatenate([part[side] for part in parts], axis=0)


def probs_kernel(last, q_ref, limit_ref, *refs):
    *kv_refs, near_both, far_both = refs[:5]
    near_next, prob_ref, turned_ref = refs[5:7], refs[7], refs[8]
    tok = q_ref.shape[1]
    depth = turned_ref.shape[0]
    turned_ref[:, :tok] = near_both[:, :depth].T
    turned_ref[:, tok:] = far_both[:, :depth].T
    blocks = last_parts(last, q_ref, near_both, far_both, near_next, kv_refs)
    for block, (q, parts) in enumerate(blocks):
        open_keys = key_mask(limit_ref, tok, 3 * block, 3)
        prob_ref[block] = prob_of(joined(parts, 0), diagonal(q), open_keys)


def turn_kernel(rows_ref, far_ref, *refs):
    *w_refs, out_ref = refs
    w = jnp.concatenate([ref[...] for ref in w_refs], axis=0)
    out_ref[...] = three_blocks(w, rows_ref, far_ref)


def three_blocks(w, rows_ref, far_ref):
    parts = [dot(w, ref[...], NN).astype(BF16) for ref in (rows_ref, far_ref)]
    return jnp.concatenate(parts, axis=1)


def last_kernel(last, rows_ref, far_rows_ref, q_ref, prob_ref, mine_ref, *refs):
    core, _ = place()
    kv_refs = refs[:3]
    near_both, far_both, *near_next = refs[3:7]
    *w_refs, dq_ref, dk_ref, dv_ref = refs[7:]
    tok = q_ref.shape[1]
    w = jnp.concatenate([ref[...] for ref in w_refs], axis=0)
    other = three_blocks(w, rows_ref, far_rows_ref)
    turned = in_order(jnp.concatenate([mine_ref[...], other], axis=0), core)
    probs, scores, queries, cotangents = [], [], [], []
    blocks = last_parts(last, q_ref, near_both, far_both, near_next, kv_refs)
    for block, (q, parts) in enumerate(blocks):
        qd = diagonal(q)
        d = diagonal_turned(*[half[:, block * tok : (block + 1) * tok] for half in turned])
        prob = prob_ref[block]
        prob_b = prob.astype(BF16)
        d_score = score_grad(prob, prob_b, joined(parts, 1), d)
        if block == 0:
            dq_ref[...] = query_grad(d_score, joined(parts, 0), tok)
        mine = slice(0, tok) if block == 0 else slice(tok, 2 * tok)
        probs.append(prob_b[mine])
        scores.append(d_score[mine])
        queries.append(qd)
        cotangents.append(d)
    scores, probs = jnp.concatenate(scores, axis=1), jnp.concatenate(probs, axis=1)
    dk_ref[...] = (dot(scores, jnp.concatenate(queries, axis=0), NN) * SCALE).astype(BF16)
    dv_ref[...] = dot(probs, jnp.concatenate(cotangents, axis=1), NT).astype(BF16)


def last_probs(last, q, limits, blocks, halo):
    tok = q.shape[1]
    depth = halo[1].shape[1] - 3 * PAIR
    return call(
        functools.partial(probs_kernel, last),
        "probs_last",
        (
            jax.ShapeDtypeStruct((3, 3 * tok, PAIR), F32),
            jax.ShapeDtypeStruct((depth, 2 * tok), BF16),
        ),
        [VMEM] * 9,
        (VMEM,) * 2,
        [],
        q,
        limits,
        *blocks,
        *halo,
    )


def last_heads(last, prob, far_rows, rows, q, blocks, halo, mine, other):
    tok = q.shape[1]
    turned = call(
        turn_kernel,
        "turn",
        jax.ShapeDtypeStruct((HD, 3 * tok), BF16),
        [VMEM] * (2 + len(mine)),
        VMEM,
        [],
        rows,
        far_rows,
        *mine,
    )
    return call(
        functools.partial(last_kernel, last),
        "heads_last",
        (jax.ShapeDtypeStruct((tok, PAIR), BF16),) * 3,
        [VMEM] * (12 + len(other)),
        (VMEM,) * 3,
        [],
        rows,
        far_rows,
        q,
        prob,
        turned,
        *blocks,
        *halo,
        *other,
    )


class Columns:
    def __init__(self, stage, sems):
        self.stage, self.sems, self.copies = stage, sems, []

    def put(self, out_ref, chunk, value):
        at = len(self.copies)
        self.stage[at] = value
        target = out_ref.at[0, :, columns(chunk)]
        copy = pltpu.make_async_copy(self.stage.at[at], target, self.sems.at[at])
        copy.start()
        self.copies.append(copy)

    def wait(self):
        for copy in self.copies:
            copy.wait()


def scratch_of(count, tok):
    return [pltpu.VMEM((count, tok, PAIR), BF16), pltpu.SemaphoreType.DMA((count,))]


def settle_kernel(order, widths, *refs):
    outs, to = refs[-5:-2], Columns(*refs[-2:])
    pairs = order(*place())
    for part, width in enumerate(widths):
        for step in range(width // PAIR):
            cols = slice(step * PAIR, (step + 1) * PAIR)
            to.put(outs[0], pairs[part][step][0], refs[part][:, cols])
    for out_ref, ref in zip(outs[1:], refs[len(widths) : -5]):
        to.put(out_ref, pairs[-1][0][0], ref[...])
    to.wait()


def settle(order, d_queries, last, shape):
    widths = tuple(x.shape[1] for x in d_queries)
    count = sum(widths) // PAIR + len(last)
    ins = [*d_queries, *last]
    return call(
        functools.partial(settle_kernel, order, widths),
        "settle",
        (jax.ShapeDtypeStruct(shape, BF16),) * 3,
        [VMEM] * len(ins),
        (ANY,) * 3,
        scratch_of(count, shape[1]),
        *ins,
    )


def finish_kernel(order, widths, far, near, *refs):
    outs, to = refs[-4:-2], Columns(*refs[-2:])
    pairs = order(*place())
    for part, width in enumerate(widths):
        own = refs[part]
        for step in range(width // PAIR):
            cols = slice(step * PAIR, (step + 1) * PAIR)
            chunk, message_slot = pairs[part][step]
            at = columns(message_slot)
            for side, out_ref in enumerate(outs):
                total = own[side, :, cols] + near[side, :, at].astype(F32)
                to.put(out_ref, chunk, (total + far[side, :, at].astype(F32)).astype(BF16))
    to.wait()


def finish(order, far, near, parts, old):
    shape = old[0].shape
    widths = tuple(x.shape[2] for x in parts)
    ins = [far, near, *parts]
    return pl.pallas_call(
        functools.partial(finish_kernel, order, widths),
        out_shape=(jax.ShapeDtypeStruct(shape, BF16),) * 2,
        in_specs=[VMEM] * len(ins) + [ANY] * 2,
        out_specs=(ANY,) * 2,
        scratch_shapes=scratch_of(2 * sum(widths) // PAIR, shape[1]),
        input_output_aliases={len(ins): 0, len(ins) + 1: 1},
        cost_estimate=BRIEF,
        compiler_params=PARAMS,
        name="finish",
    )(*ins, *old)


def body(queries, keys, values, d_out, w_out, pattern, valid):
    n_seq, n_fsdp = lax.axis_size("seq"), lax.axis_size("fsdp")
    n_chunks = queries.shape[2] // PAIR
    near = functools.partial(lax.ppermute, axis_name="seq", perm=swap(n_seq, 0))
    far = functools.partial(lax.ppermute, axis_name="seq", perm=swap(n_seq, 1))

    def cross(x, bits):
        pairs = [
            (s * n_fsdp + g, s * n_fsdp + (g ^ bits[s % 2]))
            for s in range(n_seq)
            for g in range(n_fsdp)
        ]
        return lax.ppermute(x, ("seq", "fsdp"), pairs)

    last = lambda core, group: group ^ 3 if n_fsdp == 4 else 0
    kv = join(keys, values)
    limits = limits_of(pattern, valid)
    far_kv, near_kv = far(kv), near(kv)
    if n_fsdp == 4 and n_chunks == 4 and w_out.shape[0] == PAIR:
        got = cross(w_out, (1, 2))
        message = hand_on("hand_far", last, [d_out], [queries, near_kv])
        far_both, near_both = far(message), near(message)
        early = got, near_kv, far_kv, limits, turned_rows(d_out)
        got, near_kv, far_kv, limits, rows = lax.optimization_barrier(early)
        ours = rows, queries, limits, (kv, near_kv, far_kv)
        mine, *both = onward(last, got, far_kv)
        got_d = cross(mine, (2, 1))
        near_got = [near(x) for x in both]
        first = heads(
            "heads_first",
            lambda core, group: [
                (group, 0, 0, ((0, 0, PAIR),), 0),
                (group ^ (1 + core), 1, 1 + core, ((1, 0, PAIR),), 0),
            ],
            3,
            [w_out, got],
            (),
            *ours,
        )
        near_both, near_got, dq = lax.optimization_barrier((near_both, near_got, first[0]))
        second = heads(
            "heads_second",
            lambda core, group: [(group ^ (2 - core), 0, 2 - core, ((0, 0, HD), (1, 0, HD)), 1 - core)],
            3,
            near_got,
            first[2:],
            *ours,
        )
        halo = near_both, far_both, *near_got
        prob, far_rows = last_probs(last, *ours[1:], halo)
        got_d, halo, prob, second_dq = lax.optimization_barrier((got_d, halo, prob, second[0]))
        sums = far(second[3]), near(second[2])
        third = last_heads(last, prob, far_rows, *ours[:2], ours[3], halo, [got_d], [near(x) for x in split(got_d)])
        order = lambda core, group: [
            [(group, 0), (group ^ (1 + core), 1 + core)],
            [(group ^ (2 - core), 2 - core)],
            [(group ^ 3, 0)],
        ]
        d_queries, *old = settle(order, (dq, second_dq, third[0]), third[1:], queries.shape)
        return d_queries, *finish(order, *sums, (first[1], second[1]), old)
    full = lax.all_gather(w_out, "fsdp", axis=0, tiled=True)
    ours = turned_rows(d_out), queries, limits, (kv, near_kv, far_kv)
    steps = lambda core, group: [
        (i, i, i, ((0, i * PAIR, PAIR),), 0) for i in range(n_chunks)
    ]
    dq, own, to_core, to_far = heads("heads_all", steps, n_chunks, [full], (), *ours)
    order = lambda core, group: [[(i, i) for i in range(n_chunks)]]
    d_queries, *old = settle(order, (dq,), (), queries.shape)
    return d_queries, *finish(order, far(to_far), near(to_core), (own,), old)


def solution(mesh):
    rows = P("fsdp", "seq", None)
    in_specs = (rows, rows, rows, rows, P("fsdp", None), P(), P("fsdp", None))
    return jax.shard_map(
        body, mesh=mesh, in_specs=in_specs, out_specs=(rows,) * 3, check_vma=False
    )
```

```python
import functools

import jax
import jax.numpy as jnp
from jax import lax
from jax.experimental import pallas as pl
from jax.experimental.pallas import tpu as pltpu
from jax.sharding import PartitionSpec as P

HD = 128
PAIR = 2 * HD
PIECE = 32
BRIEF = pl.CostEstimate(flops=1, bytes_accessed=1, transcendentals=0)
F32 = jnp.float32
BF16 = jnp.bfloat16
NT = (((1,), (1,)), ((), ()))
NN = (((1,), (0,)), ((), ()))
TN = (((0,), (0,)), ((), ()))
HBM = pl.BlockSpec(memory_space=pltpu.HBM)
ANY = pl.BlockSpec(memory_space=pl.ANY)
VMEM = pl.BlockSpec(memory_space=pltpu.VMEM)
SMEM = pl.BlockSpec(memory_space=pltpu.SMEM)
PARAMS = pltpu.CompilerParams(vmem_limit_bytes=40 * 2**20)
WIDE = pltpu.CompilerParams(vmem_limit_bytes=58 * 2**20)
SCALE = HD ** (-0.5)


def dot(a, b, dims):
    return lax.dot_general(a, b, dims, preferred_element_type=F32)


def swap(n, offset):
    pairs = []
    for i in range(offset, n - 1, 2):
        pairs += [(i, i + 1), (i + 1, i)]
    return pairs


def place():
    return lax.rem(lax.axis_index("seq"), 2), lax.axis_index("fsdp")


def columns(chunk):
    return pl.ds(pl.multiple_of(chunk * PAIR, PAIR), PAIR)


def head_columns(first, head):
    return pl.ds(pl.multiple_of(first + head * HD, HD), HD)


def call(kernel, name, out_shape, in_specs, out_specs, scratch, *args):
    return pl.pallas_call(
        kernel,
        out_shape=out_shape,
        in_specs=in_specs,
        out_specs=out_specs,
        scratch_shapes=scratch,
        cost_estimate=BRIEF,
        compiler_params=PARAMS,
        name=name,
    )(*args)


def key_limits(pat_ref, val_ref):
    shard = lax.axis_index("seq")
    count = val_ref.shape[1]

    def pair(block):
        return block + 1 - 2 * lax.rem(block + 2, 2)

    def far(block):
        return block - 1 + 2 * lax.rem(block + 2, 2)

    wanted = [(shard, block) for block in (shard, pair(shard), far(shard))]
    for row, other in ((pair(shard), far(pair(shard))), (far(shard), pair(far(shard)))):
        wanted += [(row, block) for block in (row, shard, other)]
    limits = []
    for row, block in wanted:
        held = jnp.clip(row, 0, count - 1)
        listed = pat_ref[0, held] == block
        for entry in range(1, pat_ref.shape[0]):
            listed = jnp.logical_or(listed, pat_ref[entry, held] == block)
        inside = jnp.logical_and(row == held, jnp.logical_and(block >= 0, block < count))
        keys = val_ref[0, jnp.clip(block, 0, count - 1)]
        limits.append(jnp.where(jnp.logical_and(listed, inside), keys, 0))
    return limits


def limits_kernel(pat_ref, val_ref, limit_ref):
    limit_ref[...] = jnp.zeros_like(limit_ref)
    for row, limit in enumerate(key_limits(pat_ref, val_ref)):
        limit_ref[row : row + 1, :] = jnp.full((1, PAIR), limit, jnp.int32)


def limits_of(pattern, valid):
    shape = jax.ShapeDtypeStruct((16, PAIR), jnp.int32)
    return call(limits_kernel, "limits", shape, [SMEM] * 2, VMEM, [], pattern.T, valid)


def join_kernel(k_ref, v_ref, kv_ref, kv, sems):
    tok, width = k_ref.shape[1:]
    arrivals, moves = [], []
    for side, ref in enumerate((k_ref, v_ref)):
        for row in range(0, tok, PIECE):
            rows, i = pl.ds(row, PIECE), len(moves)
            at = (rows, pl.ds(side * width, width))
            arrivals.append(pltpu.make_async_copy(ref.at[0, rows, :], kv.at[at], sems.at[0, i]))
            moves.append(pltpu.make_async_copy(kv.at[at], kv_ref.at[at], sems.at[1, i]))
    for copy in arrivals:
        copy.start()
    for arrival, move in zip(arrivals, moves):
        arrival.wait()
        move.start()
    for move in moves:
        move.wait()


def join(keys, values):
    tok, width = keys.shape[1:]
    kv = (tok, 2 * width)
    return pl.pallas_call(
        join_kernel,
        out_shape=jax.ShapeDtypeStruct(kv, BF16),
        in_specs=[HBM] * 2,
        out_specs=ANY,
        scratch_shapes=[
            pltpu.VMEM(kv, BF16),
            pltpu.SemaphoreType.DMA((2, 2 * (tok // PIECE))),
        ],
        cost_estimate=BRIEF,
        compiler_params=WIDE,
        name="join",
    )(keys, values)


def hand_on_kernel(last, n_whole, *refs):
    core, group = place()
    whole, cut, out_ref = refs[:n_whole], refs[n_whole:-1], refs[-1]
    chunk = last(core, group)
    pieces = [ref[0] for ref in whole]
    for ref in cut:
        if ref.ndim == 3:
            pieces.append(ref[0, :, columns(chunk)])
        else:
            pieces.append(ref[:, columns(chunk)])
            pieces.append(ref[:, columns(chunk + ref.shape[1] // (2 * PAIR))])
    to = 0
    for piece in pieces:
        out_ref[:, to : to + piece.shape[1]] = piece
        to += piece.shape[1]


def hand_on(name, last, whole, cut):
    width = sum(x.shape[2] for x in whole) + sum(PAIR * (1 if x.ndim == 3 else 2) for x in cut)
    shape = jax.ShapeDtypeStruct((cut[0].shape[-2], width), BF16)
    kernel = functools.partial(hand_on_kernel, last, len(whole))
    return call(kernel, name, shape, [VMEM] * (len(whole) + len(cut)), VMEM, [], *whole, *cut)


def turned_kernel(dy_ref, out_ref):
    out_ref[...] = dy_ref[0].T


def turned_rows(d_out):
    shape = jax.ShapeDtypeStruct(d_out.shape[:0:-1], BF16)
    return call(turned_kernel, "turned", shape, [VMEM], VMEM, [], d_out)


def onward_kernel(last, w_ref, kv_ref, mine_ref, *both_refs):
    core, group = place()
    half, depth = mine_ref.shape
    chunk = last(core, group)
    mine_ref[...] = w_ref[pl.ds(pl.multiple_of(core * half, half), half), :]
    for side, (ref, which) in enumerate(zip(both_refs, (core, 1 - core))):
        ref[:, :depth] = w_ref[pl.ds(pl.multiple_of(which * half, half), half), :]
        ref[:, depth:] = kv_ref[:, columns(chunk + side * (kv_ref.shape[1] // (2 * PAIR)))]


def onward(last, got, kv):
    rows, depth = got.shape
    half, wide = (rows // 2, depth), (rows // 2, depth + PAIR)
    shapes = tuple(jax.ShapeDtypeStruct(shape, BF16) for shape in (half, wide, wide))
    kernel = functools.partial(onward_kernel, last)
    return call(kernel, "onward", shapes, [VMEM] * 2, (VMEM,) * 3, [], got, kv)


def split_kernel(x_ref, *out_refs):
    for i, ref in enumerate(out_refs):
        ref[...] = x_ref[i * ref.shape[0] : (i + 1) * ref.shape[0], :]


def split(x):
    half = jax.ShapeDtypeStruct((x.shape[0] // 2, x.shape[1]), BF16)
    return call(split_kernel, "split", (half, half), [VMEM], (VMEM,) * 2, [], x)


def diagonal(x):
    zero = jnp.zeros((x.shape[0], HD), x.dtype)
    return jnp.concatenate(
        [
            jnp.concatenate([x[:, :HD], zero], axis=1),
            jnp.concatenate([zero, x[:, HD:]], axis=1),
        ],
        axis=0,
    )


def diagonal_turned(one, two):
    zero = jnp.zeros_like(one)
    return jnp.concatenate(
        [jnp.concatenate([one, zero], axis=1), jnp.concatenate([zero, two], axis=1)], axis=0
    )


def in_order(rows, lead):
    one, two = rows[:HD], rows[HD:]
    if isinstance(lead, int):
        return (one, two) if lead == 0 else (two, one)
    return jnp.where(lead == 0, one, two), jnp.where(lead == 0, two, one)


def key_mask(limit_ref, rows, first, count):
    index = lax.broadcasted_iota(jnp.int32, (rows, PAIR), 0)
    return jnp.concatenate(
        [index < limit_ref[i : i + 1, :] for i in range(first, first + count)], axis=0
    )


def prob_of(k, qd, open_keys):
    score = jnp.where(open_keys, dot(k, qd, NT) * SCALE, -jnp.inf)
    top = jnp.maximum(jnp.max(score, axis=0, keepdims=True), -1e30)
    raised = jnp.exp(score - top)
    total = jnp.maximum(jnp.sum(raised, axis=0, keepdims=True), 1.0)
    return raised * (1.0 / total)


def score_grad(prob, prob_b, v, d):
    d_prob = dot(v, d, NN)
    delta = jnp.sum(prob_b.astype(F32) * d_prob, axis=0, keepdims=True)
    return (prob * (d_prob - delta)).astype(BF16)


def query_grad(d_score, k, tok):
    both = dot(d_score, k, TN) * SCALE
    return jnp.concatenate([both[:tok, :HD], both[tok:, HD:]], axis=1).astype(BF16)


def stacked(refs, cols):
    return jnp.concatenate([ref[:, cols] for ref in refs], axis=0)


def heads_kernel(steps, messages, dy_ref, q_ref, limit_ref, *refs):
    core, group = place()
    k_refs, w_refs = refs[:3], refs[3 : -4 - messages]
    earlier, (dq_ref, own_ref, *message_refs) = refs[-4 - messages : -4], refs[-4:]
    for old, out in zip(earlier, message_refs):
        out[...] = old[...]
    tok, depth = q_ref.shape[1], dy_ref.shape[0]
    values_at = k_refs[0].shape[1] // (2 * PAIR)
    open_keys = key_mask(limit_ref, tok, 0, 3)
    for chunk, slot, message_slot, pieces, lead in steps(core, group):
        cols, dest, message_dest = columns(chunk), columns(slot), columns(message_slot)
        w = jnp.concatenate([w_refs[i][row : row + rows, :depth] for i, row, rows in pieces], axis=0)
        d = diagonal_turned(*in_order(dot(w, dy_ref[...], NN).astype(BF16), lead))
        qd = diagonal(q_ref[0, :, cols])
        k, v = stacked(k_refs, cols), stacked(k_refs, columns(chunk + values_at))
        prob = prob_of(k, qd, open_keys)
        prob_b = prob.astype(BF16)
        d_score = score_grad(prob, prob_b, v, d)
        dq_ref[:, dest] = query_grad(d_score, k, tok)
        for side, grad in enumerate((dot(d_score, qd, NN) * SCALE, dot(prob_b, d, NT))):
            own_ref[side, :, dest] = grad[:tok]
            for i, ref in enumerate(message_refs, 1):
                ref[side, :, message_dest] = grad[i * tok : (i + 1) * tok].astype(BF16)


def heads(name, steps, places, weights, earlier, d_out, q, limits, blocks):
    tok = q.shape[1]
    width = len(steps(0, 0)) * PAIR
    message = jax.ShapeDtypeStruct((2, tok, places * PAIR), BF16)
    return call(
        functools.partial(heads_kernel, steps, len(earlier)),
        name,
        (
            jax.ShapeDtypeStruct((tok, width), BF16),
            jax.ShapeDtypeStruct((2, tok, width), F32),
            message,
            message,
        ),
        [VMEM] * (6 + len(weights) + len(earlier)),
        (VMEM,) * 4,
        [],
        d_out,
        q,
        limits,
        *blocks,
        *weights,
        *earlier,
    )


def last_parts(last, q_ref, near_both, far_both, near_next, kv_refs):
    cols = columns(last(*place()))
    value_cols = columns(last(*place()) + kv_refs[0].shape[1] // (2 * PAIR))
    depth = far_both.shape[1] - 3 * PAIR
    own, near, far = ([ref[:, at] for at in (cols, value_cols)] for ref in kv_refs)
    past_near = [ref[:, depth:] for ref in near_next]
    past_far = [far_both[:, depth + PAIR : depth + 2 * PAIR], far_both[:, depth + 2 * PAIR :]]
    at_queries = slice(depth, depth + PAIR)
    return (
        (q_ref[0, :, cols], (own, near, far)),
        (near_both[:, at_queries], (near, own, past_near)),
        (far_both[:, at_queries], (far, own, past_far)),
    )


def joined(parts, side):
    return jnp.concatenate([part[side] for part in parts], axis=0)


def probs_kernel(last, q_ref, limit_ref, *refs):
    *kv_refs, near_both, far_both = refs[:5]
    near_next, prob_ref, turned_ref = refs[5:7], refs[7], refs[8]
    tok = q_ref.shape[1]
    depth = turned_ref.shape[0]
    turned_ref[:, :tok] = near_both[:, :depth].T
    turned_ref[:, tok:] = far_both[:, :depth].T
    blocks = last_parts(last, q_ref, near_both, far_both, near_next, kv_refs)
    for block, (q, parts) in enumerate(blocks):
        open_keys = key_mask(limit_ref, tok, 3 * block, 3)
        prob_ref[block] = prob_of(joined(parts, 0), diagonal(q), open_keys)


def last_probs(last, q, limits, blocks, halo):
    tok = q.shape[1]
    depth = halo[1].shape[1] - 3 * PAIR
    return call(
        functools.partial(probs_kernel, last),
        "probs_last",
        (
            jax.ShapeDtypeStruct((3, 3 * tok, PAIR), F32),
            jax.ShapeDtypeStruct((depth, 2 * tok), BF16),
        ),
        [VMEM] * 9,
        (VMEM,) * 2,
        [],
        q,
        limits,
        *blocks,
        *halo,
    )


def last_kernel(last, first, rows_ref, far_rows_ref, q_ref, prob_ref, *refs):
    core, group = place()
    head = core if first else 1 - core
    kv_refs, (near_both, far_both, *near_next) = refs[:3], refs[3:7]
    *w_refs, dq_ref, dk_ref, dv_ref = refs[7:]
    tok, depth = q_ref.shape[1], rows_ref.shape[0]
    w = jnp.concatenate([ref[...] for ref in w_refs], axis=0)
    turned = [dot(w, ref[...], NN).astype(BF16) for ref in (rows_ref, far_rows_ref)]
    turned = jnp.concatenate(turned, axis=1)
    start = last(core, group) * PAIR
    values_at = kv_refs[0].shape[1] // 2
    own, near, far = (
        [ref[:, head_columns(at, head)] for at in (start, start + values_at)] for ref in kv_refs
    )
    past_near = [ref[:, head_columns(depth, head)] for ref in near_next]
    past_far = [far_both[:, head_columns(depth + i * PAIR, head)] for i in (1, 2)]
    blocks = (
        (q_ref[0, :, head_columns(start, head)], (own, near, far)),
        (near_both[:, head_columns(depth, head)], (near, own, past_near)),
        (far_both[:, head_columns(depth, head)], (far, own, past_far)),
    )
    probs, scores, queries = [], [], []
    for block, (q, parts) in enumerate(blocks):
        prob = prob_ref[block, :, head_columns(0, head)]
        prob_b = prob.astype(BF16)
        d = turned[:, block * tok : (block + 1) * tok]
        d_score = score_grad(prob, prob_b, joined(parts, 1), d)
        if block == 0:
            dq_ref[...] = (dot(d_score, joined(parts, 0), TN) * SCALE).astype(BF16)
        mine = slice(0, tok) if block == 0 else slice(tok, 2 * tok)
        probs.append(prob_b[mine])
        scores.append(d_score[mine])
        queries.append(q)
    scores, probs = jnp.concatenate(scores, axis=1), jnp.concatenate(probs, axis=1)
    dk_ref[...] = (dot(scores, jnp.concatenate(queries, axis=0), NN) * SCALE).astype(BF16)
    dv_ref[...] = dot(probs, turned, NT).astype(BF16)


def last_head(last, first, prob, far_rows, rows, q, blocks, halo, w):
    tok = q.shape[1]
    return call(
        functools.partial(last_kernel, last, first),
        "heads_last" if first else "heads_end",
        (jax.ShapeDtypeStruct((tok, HD), BF16),) * 3,
        [VMEM] * (11 + len(w)),
        (VMEM,) * 3,
        [],
        rows,
        far_rows,
        q,
        prob,
        *blocks,
        *halo,
        *w,
    )


class Columns:
    def __init__(self, stage, sems):
        self.stage, self.sems, self.copies = stage, sems, []

    def put(self, out_ref, chunk, value, head=None):
        at = len(self.copies)
        if head is None:
            held, target = self.stage.at[at], out_ref.at[0, :, columns(chunk)]
        else:
            held = self.stage.at[at, :, pl.ds(0, HD)]
            target = out_ref.at[0, :, head_columns(chunk * PAIR, head)]
        held[...] = value
        copy = pltpu.make_async_copy(held, target, self.sems.at[at])
        copy.start()
        self.copies.append(copy)

    def wait(self):
        for copy in self.copies:
            copy.wait()


def scratch_of(count, tok):
    return [pltpu.VMEM((count, tok, PAIR), BF16), pltpu.SemaphoreType.DMA((count,))]


def settle_kernel(order, widths, *refs):
    out_ref, to = refs[-3], Columns(*refs[-2:])
    pairs = order(*place())
    for part, width in enumerate(widths):
        for step in range(width // PAIR):
            cols = slice(step * PAIR, (step + 1) * PAIR)
            to.put(out_ref, pairs[part][step][0], refs[part][:, cols])
    to.wait()


def settle(order, d_queries, shape):
    widths = tuple(x.shape[1] for x in d_queries)
    return call(
        functools.partial(settle_kernel, order, widths),
        "settle",
        jax.ShapeDtypeStruct(shape, BF16),
        [VMEM] * len(d_queries),
        ANY,
        scratch_of(sum(widths) // PAIR, shape[1]),
        *d_queries,
    )


def finish_kernel(order, last, widths, n_last, far, near, *refs):
    outs, to = refs[-5:-2], Columns(*refs[-2:])
    pairs = order(*place())
    core, group = place()
    for i, ref in enumerate(refs[len(widths) : len(widths) + n_last]):
        to.put(outs[i % 3], last(core, group), ref[...], core if i < 3 else 1 - core)
    for part, width in enumerate(widths):
        own = refs[part]
        for step in range(width // PAIR):
            cols = slice(step * PAIR, (step + 1) * PAIR)
            chunk, message_slot = pairs[part][step]
            at = columns(message_slot)
            for side, out_ref in enumerate(outs[1:]):
                total = own[side, :, cols] + near[side, :, at].astype(F32)
                to.put(out_ref, chunk, (total + far[side, :, at].astype(F32)).astype(BF16))
    to.wait()


def finish(order, last, far, near, parts, third, d_queries):
    shape = d_queries.shape
    widths = tuple(x.shape[2] for x in parts)
    ins = [far, near, *parts, *third]
    return pl.pallas_call(
        functools.partial(finish_kernel, order, last, widths, len(third)),
        out_shape=(jax.ShapeDtypeStruct(shape, BF16),) * 3,
        in_specs=[VMEM] * len(ins) + [ANY],
        out_specs=(ANY,) * 3,
        scratch_shapes=scratch_of(2 * sum(widths) // PAIR + len(third), shape[1]),
        input_output_aliases={len(ins): 0},
        cost_estimate=BRIEF,
        compiler_params=PARAMS,
        name="finish",
    )(*ins, d_queries)


def body(queries, keys, values, d_out, w_out, pattern, valid):
    n_seq, n_fsdp = lax.axis_size("seq"), lax.axis_size("fsdp")
    n_chunks = queries.shape[2] // PAIR
    near = functools.partial(lax.ppermute, axis_name="seq", perm=swap(n_seq, 0))
    far = functools.partial(lax.ppermute, axis_name="seq", perm=swap(n_seq, 1))

    def cross(x, bits):
        pairs = [
            (s * n_fsdp + g, s * n_fsdp + (g ^ bits[s % 2]))
            for s in range(n_seq)
            for g in range(n_fsdp)
        ]
        return lax.ppermute(x, ("seq", "fsdp"), pairs)

    last = lambda core, group: group ^ 3 if n_fsdp == 4 else 0
    kv = join(keys, values)
    limits = limits_of(pattern, valid)
    far_kv, near_kv = far(kv), near(kv)
    if n_fsdp == 4 and n_chunks == 4 and w_out.shape[0] == PAIR:
        got = cross(w_out, (1, 2))
        message = hand_on("hand_far", last, [d_out], [queries, near_kv])
        far_both, near_both = far(message), near(message)
        rows = turned_rows(d_out)
        ours = rows, queries, limits, (kv, near_kv, far_kv)
        own = heads("heads_own", lambda core, group: [(group, 0, 0, ((0, 0, PAIR),), 0)], 3, [w_out], (), *ours)
        early = got, near_kv, far_kv, limits, rows, own[0]
        got, near_kv, far_kv, limits, rows, own_dq = lax.optimization_barrier(early)
        ours = rows, queries, limits, (kv, near_kv, far_kv)
        mine, *both = onward(last, got, far_kv)
        got_d = cross(mine, (2, 1))
        near_got = [near(x) for x in both]
        first = heads(
            "heads_first",
            lambda core, group: [(group ^ (1 + core), 0, 1 + core, ((0, 0, PAIR),), 0)],
            3,
            [got],
            own[2:],
            *ours,
        )
        near_both, near_got, dq = lax.optimization_barrier((near_both, near_got, first[0]))
        second = heads(
            "heads_second",
            lambda core, group: [(group ^ (2 - core), 0, 2 - core, ((0, 0, HD), (1, 0, HD)), 1 - core)],
            3,
            near_got,
            first[2:],
            *ours,
        )
        halo = near_both, far_both, *near_got
        prob, far_rows = last_probs(last, *ours[1:], halo)
        order = lambda core, group: [
            [(group, 0)],
            [(group ^ (1 + core), 1 + core)],
            [(group ^ (2 - core), 2 - core)],
        ]
        placed = settle(order, (own_dq, dq, second[0]), queries.shape)
        got_d, halo, prob, placed = lax.optimization_barrier((got_d, halo, prob, placed))
        sums = far(second[3]), near(second[2])
        edge = [near(x) for x in split(got_d)]
        known = prob, far_rows, *ours[:2], ours[3], halo
        third = *last_head(last, True, *known, [got_d]), *last_head(last, False, *known, edge)
        return finish(order, last, *sums, (own[1], first[1], second[1]), third, placed)
    full = lax.all_gather(w_out, "fsdp", axis=0, tiled=True)
    ours = turned_rows(d_out), queries, limits, (kv, near_kv, far_kv)
    steps = lambda core, group: [
        (i, i, i, ((0, i * PAIR, PAIR),), 0) for i in range(n_chunks)
    ]
    dq, own, to_core, to_far = heads("heads_all", steps, n_chunks, [full], (), *ours)
    order = lambda core, group: [[(i, i) for i in range(n_chunks)]]
    placed = settle(order, (dq,), queries.shape)
    return finish(order, last, far(to_far), near(to_core), (own,), (), placed)


def solution(mesh):
    rows = P("fsdp", "seq", None)
    in_specs = (rows, rows, rows, rows, P("fsdp", None), P(), P("fsdp", None))
    return jax.shard_map(
        body, mesh=mesh, in_specs=in_specs, out_specs=(rows,) * 3, check_vma=False
    )
```

```python
import functools

import jax
import jax.numpy as jnp
from jax import lax
from jax.experimental import pallas as pl
from jax.experimental.pallas import tpu as pltpu
from jax.sharding import PartitionSpec as P

HD = 128
PAIR = 2 * HD
BRIEF = pl.CostEstimate(flops=1, bytes_accessed=1, transcendentals=0)
F32 = jnp.float32
BF16 = jnp.bfloat16
NT = (((1,), (1,)), ((), ()))
NN = (((1,), (0,)), ((), ()))
TN = (((0,), (0,)), ((), ()))
ANY = pl.BlockSpec(memory_space=pl.ANY)
VMEM = pl.BlockSpec(memory_space=pltpu.VMEM)
SMEM = pl.BlockSpec(memory_space=pltpu.SMEM)
PARAMS = pltpu.CompilerParams(vmem_limit_bytes=40 * 2**20)
SCALE = HD ** (-0.5)


def dot(a, b, dims):
    return lax.dot_general(a, b, dims, preferred_element_type=F32)


def swap(n, offset):
    pairs = []
    for i in range(offset, n - 1, 2):
        pairs += [(i, i + 1), (i + 1, i)]
    return pairs


def place():
    return lax.rem(lax.axis_index("seq"), 2), lax.axis_index("fsdp")


def columns(chunk):
    return pl.ds(pl.multiple_of(chunk * PAIR, PAIR), PAIR)


def head_columns(first, head):
    return pl.ds(pl.multiple_of(first + head * HD, HD), HD)


def call(kernel, name, out_shape, in_specs, out_specs, scratch, *args):
    return pl.pallas_call(
        kernel,
        out_shape=out_shape,
        in_specs=in_specs,
        out_specs=out_specs,
        scratch_shapes=scratch,
        cost_estimate=BRIEF,
        compiler_params=PARAMS,
        name=name,
    )(*args)


def key_limits(pat_ref, val_ref):
    shard = lax.axis_index("seq")
    count = val_ref.shape[1]

    def pair(block):
        return block + 1 - 2 * lax.rem(block + 2, 2)

    def far(block):
        return block - 1 + 2 * lax.rem(block + 2, 2)

    wanted = [(shard, block) for block in (shard, pair(shard), far(shard))]
    for row, other in ((pair(shard), far(pair(shard))), (far(shard), pair(far(shard)))):
        wanted += [(row, block) for block in (row, shard, other)]
    limits = []
    for row, block in wanted:
        held = jnp.clip(row, 0, count - 1)
        listed = pat_ref[0, held] == block
        for entry in range(1, pat_ref.shape[0]):
            listed = jnp.logical_or(listed, pat_ref[entry, held] == block)
        inside = jnp.logical_and(row == held, jnp.logical_and(block >= 0, block < count))
        keys = val_ref[0, jnp.clip(block, 0, count - 1)]
        limits.append(jnp.where(jnp.logical_and(listed, inside), keys, 0))
    return limits


def limits_kernel(pat_ref, val_ref, limit_ref):
    limit_ref[...] = jnp.zeros_like(limit_ref)
    for row, limit in enumerate(key_limits(pat_ref, val_ref)):
        limit_ref[row : row + 1, :] = jnp.full((1, PAIR), limit, jnp.int32)


def limits_of(pattern, valid):
    shape = jax.ShapeDtypeStruct((16, PAIR), jnp.int32)
    return call(limits_kernel, "limits", shape, [SMEM] * 2, VMEM, [], pattern.T, valid)


def join_kernel(k_ref, v_ref, kv_ref):
    width = k_ref.shape[2]
    kv_ref[:, :width] = k_ref[0]
    kv_ref[:, width:] = v_ref[0]


def join(keys, values):
    tok, width = keys.shape[1:]
    shape = jax.ShapeDtypeStruct((tok, 2 * width), BF16)
    return call(join_kernel, "join", shape, [VMEM] * 2, VMEM, [], keys, values)


def hand_on_kernel(last, n_whole, *refs):
    core, group = place()
    whole, cut, out_ref = refs[:n_whole], refs[n_whole:-1], refs[-1]
    chunk = last(core, group)
    pieces = [ref[0] for ref in whole]
    for ref in cut:
        if ref.ndim == 3:
            pieces.append(ref[0, :, columns(chunk)])
        else:
            pieces.append(ref[:, columns(chunk)])
            pieces.append(ref[:, columns(chunk + ref.shape[1] // (2 * PAIR))])
    to = 0
    for piece in pieces:
        out_ref[:, to : to + piece.shape[1]] = piece
        to += piece.shape[1]


def hand_on(name, last, whole, cut):
    width = sum(x.shape[2] for x in whole) + sum(PAIR * (1 if x.ndim == 3 else 2) for x in cut)
    shape = jax.ShapeDtypeStruct((cut[0].shape[-2], width), BF16)
    kernel = functools.partial(hand_on_kernel, last, len(whole))
    return call(kernel, name, shape, [VMEM] * (len(whole) + len(cut)), VMEM, [], *whole, *cut)


def turned_kernel(dy_ref, w_ref, out_ref, d_ref):
    out_ref[...] = dy_ref[0].T
    d_ref[...] = dot(w_ref[...], out_ref[...], NN).astype(BF16)


def turned_rows(d_out, w_out):
    depth, tok = d_out.shape[:0:-1]
    shapes = (depth, tok), (w_out.shape[0], tok)
    shapes = tuple(jax.ShapeDtypeStruct(shape, BF16) for shape in shapes)
    return call(turned_kernel, "turned", shapes, [VMEM] * 2, (VMEM,) * 2, [], d_out, w_out)


def onward_kernel(last, w_ref, kv_ref, mine_ref, *both_refs):
    core, group = place()
    half, depth = mine_ref.shape
    chunk = last(core, group)
    mine_ref[...] = w_ref[pl.ds(pl.multiple_of(core * half, half), half), :]
    for side, (ref, which) in enumerate(zip(both_refs, (core, 1 - core))):
        ref[:, :depth] = w_ref[pl.ds(pl.multiple_of(which * half, half), half), :]
        ref[:, depth:] = kv_ref[:, columns(chunk + side * (kv_ref.shape[1] // (2 * PAIR)))]


def onward(last, got, kv):
    rows, depth = got.shape
    half, wide = (rows // 2, depth), (rows // 2, depth + PAIR)
    shapes = tuple(jax.ShapeDtypeStruct(shape, BF16) for shape in (half, wide, wide))
    kernel = functools.partial(onward_kernel, last)
    return call(kernel, "onward", shapes, [VMEM] * 2, (VMEM,) * 3, [], got, kv)


def split_kernel(x_ref, *out_refs):
    for i, ref in enumerate(out_refs):
        ref[...] = x_ref[i * ref.shape[0] : (i + 1) * ref.shape[0], :]


def split(x):
    half = jax.ShapeDtypeStruct((x.shape[0] // 2, x.shape[1]), BF16)
    return call(split_kernel, "split", (half, half), [VMEM], (VMEM,) * 2, [], x)


def diagonal(x):
    zero = jnp.zeros((x.shape[0], HD), x.dtype)
    return jnp.concatenate(
        [
            jnp.concatenate([x[:, :HD], zero], axis=1),
            jnp.concatenate([zero, x[:, HD:]], axis=1),
        ],
        axis=0,
    )


def diagonal_turned(one, two):
    zero = jnp.zeros_like(one)
    return jnp.concatenate(
        [jnp.concatenate([one, zero], axis=1), jnp.concatenate([zero, two], axis=1)], axis=0
    )


def in_order(rows, lead):
    one, two = rows[:HD], rows[HD:]
    if isinstance(lead, int):
        return (one, two) if lead == 0 else (two, one)
    return jnp.where(lead == 0, one, two), jnp.where(lead == 0, two, one)


def key_mask(limit_ref, rows, first, count):
    index = lax.broadcasted_iota(jnp.int32, (rows, PAIR), 0)
    return jnp.concatenate(
        [index < limit_ref[i : i + 1, :] for i in range(first, first + count)], axis=0
    )


def prob_of(k, qd, open_keys):
    score = jnp.where(open_keys, dot(k, qd, NT) * SCALE, -jnp.inf)
    top = jnp.maximum(jnp.max(score, axis=0, keepdims=True), -1e30)
    raised = jnp.exp(score - top)
    total = jnp.maximum(jnp.sum(raised, axis=0, keepdims=True), 1.0)
    return raised * (1.0 / total)


def score_grad(prob, prob_b, v, d):
    d_prob = dot(v, d, NN)
    delta = jnp.sum(prob_b.astype(F32) * d_prob, axis=0, keepdims=True)
    return (prob * (d_prob - delta)).astype(BF16)


def query_grad(d_score, k, tok):
    both = dot(d_score, k, TN) * SCALE
    return jnp.concatenate([both[:tok, :HD], both[tok:, HD:]], axis=1).astype(BF16)


def stacked(refs, cols):
    return jnp.concatenate([ref[:, cols] for ref in refs], axis=0)


def heads_kernel(steps, messages, dy_ref, q_ref, limit_ref, *refs):
    core, group = place()
    k_refs, w_refs = refs[:3], refs[3 : -4 - messages]
    earlier, (dq_ref, own_ref, *message_refs) = refs[-4 - messages : -4], refs[-4:]
    for old, out in zip(earlier, message_refs):
        out[...] = old[...]
    tok, depth = q_ref.shape[1], dy_ref.shape[0]
    values_at = k_refs[0].shape[1] // (2 * PAIR)
    open_keys = key_mask(limit_ref, tok, 0, 3)
    for chunk, slot, message_slot, pieces, lead in steps(core, group):
        cols, dest, message_dest = columns(chunk), columns(slot), columns(message_slot)
        w = jnp.concatenate([w_refs[i][row : row + rows, :depth] for i, row, rows in pieces], axis=0)
        if w_refs[pieces[0][0]].shape[1] >= depth:
            w = dot(w, dy_ref[...], NN).astype(BF16)
        d = diagonal_turned(*in_order(w, lead))
        qd = diagonal(q_ref[0, :, cols])
        k, v = stacked(k_refs, cols), stacked(k_refs, columns(chunk + values_at))
        prob = prob_of(k, qd, open_keys)
        prob_b = prob.astype(BF16)
        d_score = score_grad(prob, prob_b, v, d)
        dq_ref[:, dest] = query_grad(d_score, k, tok)
        for side, grad in enumerate((dot(d_score, qd, NN) * SCALE, dot(prob_b, d, NT))):
            own_ref[side, :, dest] = grad[:tok]
            for i, ref in enumerate(message_refs, 1):
                ref[side, :, message_dest] = grad[i * tok : (i + 1) * tok].astype(BF16)


def heads(name, steps, places, weights, earlier, d_out, q, limits, blocks):
    tok = q.shape[1]
    width = len(steps(0, 0)) * PAIR
    message = jax.ShapeDtypeStruct((2, tok, places * PAIR), BF16)
    return call(
        functools.partial(heads_kernel, steps, len(earlier)),
        name,
        (
            jax.ShapeDtypeStruct((tok, width), BF16),
            jax.ShapeDtypeStruct((2, tok, width), F32),
            message,
            message,
        ),
        [VMEM] * (6 + len(weights) + len(earlier)),
        (VMEM,) * 4,
        [],
        d_out,
        q,
        limits,
        *blocks,
        *weights,
        *earlier,
    )


def last_parts(last, q_ref, near_both, far_both, near_next, kv_refs):
    cols = columns(last(*place()))
    value_cols = columns(last(*place()) + kv_refs[0].shape[1] // (2 * PAIR))
    depth = far_both.shape[1] - 3 * PAIR
    own, near, far = ([ref[:, at] for at in (cols, value_cols)] for ref in kv_refs)
    past_near = [ref[:, depth:] for ref in near_next]
    past_far = [far_both[:, depth + PAIR : depth + 2 * PAIR], far_both[:, depth + 2 * PAIR :]]
    at_queries = slice(depth, depth + PAIR)
    return (
        (q_ref[0, :, cols], (own, near, far)),
        (near_both[:, at_queries], (near, own, past_near)),
        (far_both[:, at_queries], (far, own, past_far)),
    )


def joined(parts, side):
    return jnp.concatenate([part[side] for part in parts], axis=0)


def probs_kernel(last, q_ref, limit_ref, *refs):
    *kv_refs, near_both, far_both = refs[:5]
    near_next, prob_ref, turned_ref = refs[5:7], refs[7], refs[8]
    tok = q_ref.shape[1]
    depth = turned_ref.shape[0]
    turned_ref[:, :tok] = near_both[:, :depth].T
    turned_ref[:, tok:] = far_both[:, :depth].T
    blocks = last_parts(last, q_ref, near_both, far_both, near_next, kv_refs)
    for block, (q, parts) in enumerate(blocks):
        open_keys = key_mask(limit_ref, tok, 3 * block, 3)
        prob_ref[block] = prob_of(joined(parts, 0), diagonal(q), open_keys)


def last_probs(last, q, limits, blocks, halo):
    tok = q.shape[1]
    depth = halo[1].shape[1] - 3 * PAIR
    return call(
        functools.partial(probs_kernel, last),
        "probs_last",
        (
            jax.ShapeDtypeStruct((3, 3 * tok, PAIR), F32),
            jax.ShapeDtypeStruct((depth, 2 * tok), BF16),
        ),
        [VMEM] * 9,
        (VMEM,) * 2,
        [],
        q,
        limits,
        *blocks,
        *halo,
    )


def last_kernel(last, first, rows_ref, far_rows_ref, q_ref, prob_ref, *refs):
    core, group = place()
    head = core if first else 1 - core
    kv_refs, (near_both, far_both, *near_next) = refs[:3], refs[3:7]
    *w_refs, dq_ref, dk_ref, dv_ref = refs[7:]
    tok, depth = q_ref.shape[1], rows_ref.shape[0]
    w = jnp.concatenate([ref[...] for ref in w_refs], axis=0)
    turned = [dot(w, ref[...], NN).astype(BF16) for ref in (rows_ref, far_rows_ref)]
    turned = jnp.concatenate(turned, axis=1)
    start = last(core, group) * PAIR
    values_at = kv_refs[0].shape[1] // 2
    own, near, far = (
        [ref[:, head_columns(at, head)] for at in (start, start + values_at)] for ref in kv_refs
    )
    past_near = [ref[:, head_columns(depth, head)] for ref in near_next]
    past_far = [far_both[:, head_columns(depth + i * PAIR, head)] for i in (1, 2)]
    blocks = (
        (q_ref[0, :, head_columns(start, head)], (own, near, far)),
        (near_both[:, head_columns(depth, head)], (near, own, past_near)),
        (far_both[:, head_columns(depth, head)], (far, own, past_far)),
    )
    probs, scores, queries = [], [], []
    for block, (q, parts) in enumerate(blocks):
        prob = prob_ref[block, :, head_columns(0, head)]
        prob_b = prob.astype(BF16)
        d = turned[:, block * tok : (block + 1) * tok]
        d_score = score_grad(prob, prob_b, joined(parts, 1), d)
        if block == 0:
            dq_ref[...] = (dot(d_score, joined(parts, 0), TN) * SCALE).astype(BF16)
        mine = slice(0, tok) if block == 0 else slice(tok, 2 * tok)
        probs.append(prob_b[mine])
        scores.append(d_score[mine])
        queries.append(q)
    scores, probs = jnp.concatenate(scores, axis=1), jnp.concatenate(probs, axis=1)
    dk_ref[...] = (dot(scores, jnp.concatenate(queries, axis=0), NN) * SCALE).astype(BF16)
    dv_ref[...] = dot(probs, turned, NT).astype(BF16)


def last_head(last, first, prob, far_rows, rows, q, blocks, halo, w):
    tok = q.shape[1]
    return call(
        functools.partial(last_kernel, last, first),
        "heads_last" if first else "heads_end",
        (jax.ShapeDtypeStruct((tok, HD), BF16),) * 3,
        [VMEM] * (11 + len(w)),
        (VMEM,) * 3,
        [],
        rows,
        far_rows,
        q,
        prob,
        *blocks,
        *halo,
        *w,
    )


class Columns:
    def __init__(self, stage, sems):
        self.stage, self.sems, self.copies = stage, sems, []

    def put(self, out_ref, chunk, value, head=None):
        at = len(self.copies)
        if head is None:
            held, target = self.stage.at[at], out_ref.at[0, :, columns(chunk)]
        else:
            held = self.stage.at[at, :, pl.ds(0, HD)]
            target = out_ref.at[0, :, head_columns(chunk * PAIR, head)]
        held[...] = value
        copy = pltpu.make_async_copy(held, target, self.sems.at[at])
        copy.start()
        self.copies.append(copy)

    def wait(self):
        for copy in self.copies:
            copy.wait()


def scratch_of(count, tok):
    return [pltpu.VMEM((count, tok, PAIR), BF16), pltpu.SemaphoreType.DMA((count,))]


def settle_kernel(order, widths, *refs):
    out_ref, to = refs[-3], Columns(*refs[-2:])
    pairs = order(*place())
    for part, width in enumerate(widths):
        for step in range(width // PAIR):
            cols = slice(step * PAIR, (step + 1) * PAIR)
            to.put(out_ref, pairs[part][step][0], refs[part][:, cols])
    to.wait()


def settle(order, d_queries, shape):
    widths = tuple(x.shape[1] for x in d_queries)
    return call(
        functools.partial(settle_kernel, order, widths),
        "settle",
        jax.ShapeDtypeStruct(shape, BF16),
        [VMEM] * len(d_queries),
        ANY,
        scratch_of(sum(widths) // PAIR, shape[1]),
        *d_queries,
    )


def finish_kernel(order, last, widths, n_last, far, near, *refs):
    outs, to = refs[-5:-2], Columns(*refs[-2:])
    pairs = order(*place())
    core, group = place()
    for i, ref in enumerate(refs[len(widths) : len(widths) + n_last]):
        to.put(outs[i % 3], last(core, group), ref[...], core if i < 3 else 1 - core)
    for part, width in enumerate(widths):
        own = refs[part]
        for step in range(width // PAIR):
            cols = slice(step * PAIR, (step + 1) * PAIR)
            chunk, message_slot = pairs[part][step]
            at = columns(message_slot)
            for side, out_ref in enumerate(outs[1:]):
                total = own[side, :, cols] + near[side, :, at].astype(F32)
                to.put(out_ref, chunk, (total + far[side, :, at].astype(F32)).astype(BF16))
    to.wait()


def finish(order, last, far, near, parts, third, d_queries):
    shape = d_queries.shape
    widths = tuple(x.shape[2] for x in parts)
    ins = [far, near, *parts, *third]
    return pl.pallas_call(
        functools.partial(finish_kernel, order, last, widths, len(third)),
        out_shape=(jax.ShapeDtypeStruct(shape, BF16),) * 3,
        in_specs=[VMEM] * len(ins) + [ANY],
        out_specs=(ANY,) * 3,
        scratch_shapes=scratch_of(2 * sum(widths) // PAIR + len(third), shape[1]),
        input_output_aliases={len(ins): 0},
        cost_estimate=BRIEF,
        compiler_params=PARAMS,
        name="finish",
    )(*ins, d_queries)


def body(queries, keys, values, d_out, w_out, pattern, valid):
    n_seq, n_fsdp = lax.axis_size("seq"), lax.axis_size("fsdp")
    n_chunks = queries.shape[2] // PAIR
    near = functools.partial(lax.ppermute, axis_name="seq", perm=swap(n_seq, 0))
    far = functools.partial(lax.ppermute, axis_name="seq", perm=swap(n_seq, 1))

    def cross(x, bits):
        pairs = [
            (s * n_fsdp + g, s * n_fsdp + (g ^ bits[s % 2]))
            for s in range(n_seq)
            for g in range(n_fsdp)
        ]
        return lax.ppermute(x, ("seq", "fsdp"), pairs)

    last = lambda core, group: group ^ 3 if n_fsdp == 4 else 0
    kv = join(keys, values)
    limits = limits_of(pattern, valid)
    far_kv, near_kv = far(kv), near(kv)
    if n_fsdp == 4 and n_chunks == 4 and w_out.shape[0] == PAIR:
        got = cross(w_out, (1, 2))
        message = hand_on("hand_far", last, [d_out], [queries, near_kv])
        far_both, near_both = far(message), near(message)
        rows, d_own = turned_rows(d_out, w_out)
        ours = rows, queries, limits, (kv, near_kv, far_kv)
        own = heads("heads_own", lambda core, group: [(group, 0, 0, ((0, 0, PAIR),), 0)], 3, [d_own], (), *ours)
        early = got, near_kv, far_kv, limits, rows, own[0]
        got, near_kv, far_kv, limits, rows, own_dq = lax.optimization_barrier(early)
        ours = rows, queries, limits, (kv, near_kv, far_kv)
        mine, *both = onward(last, got, far_kv)
        got_d = cross(mine, (2, 1))
        near_got = [near(x) for x in both]
        first = heads(
            "heads_first",
            lambda core, group: [(group ^ (1 + core), 0, 1 + core, ((0, 0, PAIR),), 0)],
            3,
            [got],
            own[2:],
            *ours,
        )
        near_both, near_got, dq = lax.optimization_barrier((near_both, near_got, first[0]))
        second = heads(
            "heads_second",
            lambda core, group: [(group ^ (2 - core), 0, 2 - core, ((0, 0, HD), (1, 0, HD)), 1 - core)],
            3,
            near_got,
            first[2:],
            *ours,
        )
        halo = near_both, far_both, *near_got
        prob, far_rows = last_probs(last, *ours[1:], halo)
        order = lambda core, group: [
            [(group, 0)],
            [(group ^ (1 + core), 1 + core)],
            [(group ^ (2 - core), 2 - core)],
        ]
        placed = settle(order, (own_dq, dq, second[0]), queries.shape)
        got_d, halo, prob, placed = lax.optimization_barrier((got_d, halo, prob, placed))
        sums = far(second[3]), near(second[2])
        edge = [near(x) for x in split(got_d)]
        known = prob, far_rows, *ours[:2], ours[3], halo
        third = *last_head(last, True, *known, [got_d]), *last_head(last, False, *known, edge)
        return finish(order, last, *sums, (own[1], first[1], second[1]), third, placed)
    full = lax.all_gather(w_out, "fsdp", axis=0, tiled=True)
    ours = turned_rows(d_out, w_out)[0], queries, limits, (kv, near_kv, far_kv)
    steps = lambda core, group: [
        (i, i, i, ((0, i * PAIR, PAIR),), 0) for i in range(n_chunks)
    ]
    dq, own, to_core, to_far = heads("heads_all", steps, n_chunks, [full], (), *ours)
    order = lambda core, group: [[(i, i) for i in range(n_chunks)]]
    placed = settle(order, (dq,), queries.shape)
    return finish(order, last, far(to_far), near(to_core), (own,), (), placed)


def solution(mesh):
    rows = P("fsdp", "seq", None)
    in_specs = (rows, rows, rows, rows, P("fsdp", None), P(), P("fsdp", None))
    return jax.shard_map(
        body, mesh=mesh, in_specs=in_specs, out_specs=(rows,) * 3, check_vma=False
    )
```

```python
import functools

import jax
import jax.numpy as jnp
from jax import lax
from jax.experimental import pallas as pl
from jax.experimental.pallas import tpu as pltpu
from jax.sharding import PartitionSpec as P

HD = 128
PAIR = 2 * HD
BRIEF = pl.CostEstimate(flops=1, bytes_accessed=1, transcendentals=0)
F32 = jnp.float32
BF16 = jnp.bfloat16
NT = (((1,), (1,)), ((), ()))
NN = (((1,), (0,)), ((), ()))
TN = (((0,), (0,)), ((), ()))
ANY = pl.BlockSpec(memory_space=pl.ANY)
VMEM = pl.BlockSpec(memory_space=pltpu.VMEM)
SMEM = pl.BlockSpec(memory_space=pltpu.SMEM)
PARAMS = pltpu.CompilerParams(vmem_limit_bytes=40 * 2**20)
SCALE = HD ** (-0.5)


def dot(a, b, dims):
    return lax.dot_general(a, b, dims, preferred_element_type=F32)


def swap(n, offset):
    pairs = []
    for i in range(offset, n - 1, 2):
        pairs += [(i, i + 1), (i + 1, i)]
    return pairs


def place():
    return lax.rem(lax.axis_index("seq"), 2), lax.axis_index("fsdp")


def columns(chunk):
    return pl.ds(pl.multiple_of(chunk * PAIR, PAIR), PAIR)


def head_columns(first, head):
    return pl.ds(pl.multiple_of(first + head * HD, HD), HD)


def call(kernel, name, out_shape, in_specs, out_specs, scratch, *args):
    return pl.pallas_call(
        kernel,
        out_shape=out_shape,
        in_specs=in_specs,
        out_specs=out_specs,
        scratch_shapes=scratch,
        cost_estimate=BRIEF,
        compiler_params=PARAMS,
        name=name,
    )(*args)


def key_limits(pat_ref, val_ref):
    shard = lax.axis_index("seq")
    count = val_ref.shape[1]

    def pair(block):
        return block + 1 - 2 * lax.rem(block + 2, 2)

    def far(block):
        return block - 1 + 2 * lax.rem(block + 2, 2)

    wanted = [(shard, block) for block in (shard, pair(shard), far(shard))]
    for row, other in ((pair(shard), far(pair(shard))), (far(shard), pair(far(shard)))):
        wanted += [(row, block) for block in (row, shard, other)]
    limits = []
    for row, block in wanted:
        held = jnp.clip(row, 0, count - 1)
        listed = pat_ref[0, held] == block
        for entry in range(1, pat_ref.shape[0]):
            listed = jnp.logical_or(listed, pat_ref[entry, held] == block)
        inside = jnp.logical_and(row == held, jnp.logical_and(block >= 0, block < count))
        keys = val_ref[0, jnp.clip(block, 0, count - 1)]
        limits.append(jnp.where(jnp.logical_and(listed, inside), keys, 0))
    return limits


def limits_kernel(pat_ref, val_ref, limit_ref):
    limit_ref[...] = jnp.zeros_like(limit_ref)
    for row, limit in enumerate(key_limits(pat_ref, val_ref)):
        limit_ref[row : row + 1, :] = jnp.full((1, PAIR), limit, jnp.int32)


def limits_of(pattern, valid):
    shape = jax.ShapeDtypeStruct((16, PAIR), jnp.int32)
    return call(limits_kernel, "limits", shape, [SMEM] * 2, VMEM, [], pattern.T, valid)


def join_kernel(k_ref, v_ref, kv_ref):
    width = k_ref.shape[2]
    kv_ref[:, :width] = k_ref[0]
    kv_ref[:, width:] = v_ref[0]


def join(keys, values):
    tok, width = keys.shape[1:]
    shape = jax.ShapeDtypeStruct((tok, 2 * width), BF16)
    return call(join_kernel, "join", shape, [VMEM] * 2, VMEM, [], keys, values)


def hand_on_kernel(last, n_whole, *refs):
    core, group = place()
    whole, cut, out_ref = refs[:n_whole], refs[n_whole:-1], refs[-1]
    chunk = last(core, group)
    pieces = [ref[0] for ref in whole]
    for ref in cut:
        if ref.ndim == 3:
            pieces.append(ref[0, :, columns(chunk)])
        else:
            pieces.append(ref[:, columns(chunk)])
            pieces.append(ref[:, columns(chunk + ref.shape[1] // (2 * PAIR))])
    to = 0
    for piece in pieces:
        out_ref[:, to : to + piece.shape[1]] = piece
        to += piece.shape[1]


def hand_on(name, last, whole, cut):
    width = sum(x.shape[2] for x in whole) + sum(PAIR * (1 if x.ndim == 3 else 2) for x in cut)
    shape = jax.ShapeDtypeStruct((cut[0].shape[-2], width), BF16)
    kernel = functools.partial(hand_on_kernel, last, len(whole))
    return call(kernel, name, shape, [VMEM] * (len(whole) + len(cut)), VMEM, [], *whole, *cut)


def turned_kernel(dy_ref, w_ref, out_ref, d_ref):
    out_ref[...] = dy_ref[0].T
    d_ref[...] = dot(w_ref[...], out_ref[...], NN).astype(BF16)


def turned_rows(d_out, w_out):
    depth, tok = d_out.shape[:0:-1]
    shapes = (depth, tok), (w_out.shape[0], tok)
    shapes = tuple(jax.ShapeDtypeStruct(shape, BF16) for shape in shapes)
    return call(turned_kernel, "turned", shapes, [VMEM] * 2, (VMEM,) * 2, [], d_out, w_out)


def onward_kernel(last, w_ref, kv_ref, mine_ref, *both_refs):
    core, group = place()
    half, depth = mine_ref.shape
    chunk = last(core, group)
    mine_ref[...] = w_ref[pl.ds(pl.multiple_of(core * half, half), half), :]
    for side, (ref, which) in enumerate(zip(both_refs, (core, 1 - core))):
        ref[:, :depth] = w_ref[pl.ds(pl.multiple_of(which * half, half), half), :]
        ref[:, depth:] = kv_ref[:, columns(chunk + side * (kv_ref.shape[1] // (2 * PAIR)))]


def onward(last, got, kv):
    rows, depth = got.shape
    half, wide = (rows // 2, depth), (rows // 2, depth + PAIR)
    shapes = tuple(jax.ShapeDtypeStruct(shape, BF16) for shape in (half, wide, wide))
    kernel = functools.partial(onward_kernel, last)
    return call(kernel, "onward", shapes, [VMEM] * 2, (VMEM,) * 3, [], got, kv)


def split_kernel(x_ref, *out_refs):
    for i, ref in enumerate(out_refs):
        ref[...] = x_ref[i * ref.shape[0] : (i + 1) * ref.shape[0], :]


def split(x):
    half = jax.ShapeDtypeStruct((x.shape[0] // 2, x.shape[1]), BF16)
    return call(split_kernel, "split", (half, half), [VMEM], (VMEM,) * 2, [], x)


def diagonal(x):
    zero = jnp.zeros((x.shape[0], HD), x.dtype)
    return jnp.concatenate(
        [
            jnp.concatenate([x[:, :HD], zero], axis=1),
            jnp.concatenate([zero, x[:, HD:]], axis=1),
        ],
        axis=0,
    )


def diagonal_turned(one, two):
    zero = jnp.zeros_like(one)
    return jnp.concatenate(
        [jnp.concatenate([one, zero], axis=1), jnp.concatenate([zero, two], axis=1)], axis=0
    )


def in_order(rows, lead):
    one, two = rows[:HD], rows[HD:]
    if isinstance(lead, int):
        return (one, two) if lead == 0 else (two, one)
    return jnp.where(lead == 0, one, two), jnp.where(lead == 0, two, one)


def key_mask(limit_ref, rows, first, count):
    index = lax.broadcasted_iota(jnp.int32, (rows, PAIR), 0)
    return jnp.concatenate(
        [index < limit_ref[i : i + 1, :] for i in range(first, first + count)], axis=0
    )


def prob_of(k, qd, open_keys):
    score = jnp.where(open_keys, dot(k, qd, NT) * SCALE, -jnp.inf)
    top = jnp.maximum(jnp.max(score, axis=0, keepdims=True), -1e30)
    raised = jnp.exp(score - top)
    total = jnp.maximum(jnp.sum(raised, axis=0, keepdims=True), 1.0)
    return raised * (1.0 / total)


def score_grad(prob, prob_b, v, d):
    d_prob = dot(v, d, NN)
    delta = jnp.sum(prob_b.astype(F32) * d_prob, axis=0, keepdims=True)
    return (prob * (d_prob - delta)).astype(BF16)


def query_grad(d_score, k, tok):
    both = dot(d_score, k, TN) * SCALE
    return jnp.concatenate([both[:tok, :HD], both[tok:, HD:]], axis=1).astype(BF16)


def stacked(refs, cols):
    return jnp.concatenate([ref[:, cols] for ref in refs], axis=0)


def heads_kernel(steps, messages, dy_ref, q_ref, limit_ref, *refs):
    core, group = place()
    k_refs, w_refs = refs[:3], refs[3 : -4 - messages]
    earlier, (dq_ref, own_ref, *message_refs) = refs[-4 - messages : -4], refs[-4:]
    for old, out in zip(earlier, message_refs):
        out[...] = old[...]
    tok, depth = q_ref.shape[1], dy_ref.shape[0]
    values_at = k_refs[0].shape[1] // (2 * PAIR)
    open_keys = key_mask(limit_ref, tok, 0, 3)
    for chunk, slot, message_slot, pieces, lead in steps(core, group):
        cols, dest, message_dest = columns(chunk), columns(slot), columns(message_slot)
        w = jnp.concatenate([w_refs[i][row : row + rows, :depth] for i, row, rows in pieces], axis=0)
        if w_refs[pieces[0][0]].shape[1] >= depth:
            w = dot(w, dy_ref[...], NN).astype(BF16)
        d = diagonal_turned(*in_order(w, lead))
        qd = diagonal(q_ref[0, :, cols])
        k, v = stacked(k_refs, cols), stacked(k_refs, columns(chunk + values_at))
        prob = prob_of(k, qd, open_keys)
        prob_b = prob.astype(BF16)
        d_score = score_grad(prob, prob_b, v, d)
        dq_ref[:, dest] = query_grad(d_score, k, tok)
        for side, grad in enumerate((dot(d_score, qd, NN) * SCALE, dot(prob_b, d, NT))):
            own_ref[side, :, dest] = grad[:tok]
            for i, ref in enumerate(message_refs, 1):
                ref[side, :, message_dest] = grad[i * tok : (i + 1) * tok].astype(BF16)


def heads(name, steps, places, weights, earlier, d_out, q, limits, blocks):
    tok = q.shape[1]
    width = len(steps(0, 0)) * PAIR
    message = jax.ShapeDtypeStruct((2, tok, places * PAIR), BF16)
    return call(
        functools.partial(heads_kernel, steps, len(earlier)),
        name,
        (
            jax.ShapeDtypeStruct((tok, width), BF16),
            jax.ShapeDtypeStruct((2, tok, width), F32),
            message,
            message,
        ),
        [VMEM] * (6 + len(weights) + len(earlier)),
        (VMEM,) * 4,
        [],
        d_out,
        q,
        limits,
        *blocks,
        *weights,
        *earlier,
    )


def last_parts(last, q_ref, near_both, far_both, near_next, kv_refs):
    cols = columns(last(*place()))
    value_cols = columns(last(*place()) + kv_refs[0].shape[1] // (2 * PAIR))
    depth = far_both.shape[1] - 3 * PAIR
    own, near, far = ([ref[:, at] for at in (cols, value_cols)] for ref in kv_refs)
    past_near = [ref[:, depth:] for ref in near_next]
    past_far = [far_both[:, depth + PAIR : depth + 2 * PAIR], far_both[:, depth + 2 * PAIR :]]
    at_queries = slice(depth, depth + PAIR)
    return (
        (q_ref[0, :, cols], (own, near, far)),
        (near_both[:, at_queries], (near, own, past_near)),
        (far_both[:, at_queries], (far, own, past_far)),
    )


def joined(parts, side):
    return jnp.concatenate([part[side] for part in parts], axis=0)


def probs_kernel(last, q_ref, limit_ref, *refs):
    *kv_refs, near_both, far_both = refs[:5]
    near_next, (prob_ref, attended_ref, turned_ref) = refs[5:7], refs[7:]
    tok = q_ref.shape[1]
    depth = turned_ref.shape[0]
    turned_ref[:, :tok] = near_both[:, :depth].T
    turned_ref[:, tok:] = far_both[:, :depth].T
    blocks = last_parts(last, q_ref, near_both, far_both, near_next, kv_refs)
    for block, (q, parts) in enumerate(blocks):
        open_keys = key_mask(limit_ref, tok, 3 * block, 3)
        prob = prob_of(joined(parts, 0), diagonal(q), open_keys)
        prob_ref[block] = prob
        out = dot(joined(parts, 1), prob.astype(BF16), TN)
        attended_ref[block] = jnp.concatenate([out[:HD, :tok], out[HD:, tok:]], axis=1)


def last_probs(last, q, limits, blocks, halo):
    tok = q.shape[1]
    depth = halo[1].shape[1] - 3 * PAIR
    return call(
        functools.partial(probs_kernel, last),
        "probs_last",
        (
            jax.ShapeDtypeStruct((3, 3 * tok, PAIR), F32),
            jax.ShapeDtypeStruct((3, HD, 2 * tok), F32),
            jax.ShapeDtypeStruct((depth, 2 * tok), BF16),
        ),
        [VMEM] * 9,
        (VMEM,) * 3,
        [],
        q,
        limits,
        *blocks,
        *halo,
    )


def last_kernel(last, first, rows_ref, far_rows_ref, q_ref, prob_ref, attended_ref, *refs):
    core, group = place()
    head = core if first else 1 - core
    kv_refs, (near_both, far_both, *near_next) = refs[:3], refs[3:7]
    *w_refs, dq_ref, dk_ref, dv_ref = refs[7:]
    tok, depth = q_ref.shape[1], rows_ref.shape[0]
    w = jnp.concatenate([ref[...] for ref in w_refs], axis=0)
    turned = [dot(w, ref[...], NN).astype(BF16) for ref in (rows_ref, far_rows_ref)]
    turned = jnp.concatenate(turned, axis=1)
    start = last(core, group) * PAIR
    values_at = kv_refs[0].shape[1] // 2
    own, near, far = (
        [ref[:, head_columns(at, head)] for at in (start, start + values_at)] for ref in kv_refs
    )
    past_near = [ref[:, head_columns(depth, head)] for ref in near_next]
    past_far = [far_both[:, head_columns(depth + i * PAIR, head)] for i in (1, 2)]
    blocks = (
        (q_ref[0, :, head_columns(start, head)], (own, near, far)),
        (near_both[:, head_columns(depth, head)], (near, own, past_near)),
        (far_both[:, head_columns(depth, head)], (far, own, past_far)),
    )
    probs, scores, queries = [], [], []
    for block, (q, parts) in enumerate(blocks):
        d = turned[:, block * tok : (block + 1) * tok]
        lanes = head_columns(0, head)
        delta = jnp.sum(d.astype(F32) * attended_ref[block, :, lanes], axis=0, keepdims=True)
        if block == 0:
            prob, v = prob_ref[block, :, lanes], joined(parts, 1)
        else:
            prob, v = prob_ref[block, tok : 2 * tok, lanes], parts[1][1]
        d_score = (prob * (dot(v, d, NN) - delta)).astype(BF16)
        if block == 0:
            dq_ref[...] = (dot(d_score, joined(parts, 0), TN) * SCALE).astype(BF16)
        probs.append(prob[:tok].astype(BF16))
        scores.append(d_score[:tok])
        queries.append(q)
    scores, probs = jnp.concatenate(scores, axis=1), jnp.concatenate(probs, axis=1)
    dk_ref[...] = (dot(scores, jnp.concatenate(queries, axis=0), NN) * SCALE).astype(BF16)
    dv_ref[...] = dot(probs, turned, NT).astype(BF16)


def last_head(last, first, prob, attended, far_rows, rows, q, blocks, halo, w):
    tok = q.shape[1]
    return call(
        functools.partial(last_kernel, last, first),
        "heads_last" if first else "heads_end",
        (jax.ShapeDtypeStruct((tok, HD), BF16),) * 3,
        [VMEM] * (12 + len(w)),
        (VMEM,) * 3,
        [],
        rows,
        far_rows,
        q,
        prob,
        attended,
        *blocks,
        *halo,
        *w,
    )


class Columns:
    def __init__(self, stage, sems):
        self.stage, self.sems, self.copies = stage, sems, []

    def put(self, out_ref, chunk, value, head=None):
        at = len(self.copies)
        if head is None:
            held, target = self.stage.at[at], out_ref.at[0, :, columns(chunk)]
        else:
            held = self.stage.at[at, :, pl.ds(0, HD)]
            target = out_ref.at[0, :, head_columns(chunk * PAIR, head)]
        held[...] = value
        copy = pltpu.make_async_copy(held, target, self.sems.at[at])
        copy.start()
        self.copies.append(copy)

    def wait(self):
        for copy in self.copies:
            copy.wait()


def scratch_of(count, tok):
    return [pltpu.VMEM((count, tok, PAIR), BF16), pltpu.SemaphoreType.DMA((count,))]


def settle_kernel(order, widths, *refs):
    out_ref, to = refs[-3], Columns(*refs[-2:])
    pairs = order(*place())
    for part, width in enumerate(widths):
        for step in range(width // PAIR):
            cols = slice(step * PAIR, (step + 1) * PAIR)
            to.put(out_ref, pairs[part][step][0], refs[part][:, cols])
    to.wait()


def settle(order, d_queries, shape):
    widths = tuple(x.shape[1] for x in d_queries)
    return call(
        functools.partial(settle_kernel, order, widths),
        "settle",
        jax.ShapeDtypeStruct(shape, BF16),
        [VMEM] * len(d_queries),
        ANY,
        scratch_of(sum(widths) // PAIR, shape[1]),
        *d_queries,
    )


def finish_kernel(order, last, widths, n_last, far, near, *refs):
    outs, to = refs[-5:-2], Columns(*refs[-2:])
    pairs = order(*place())
    core, group = place()
    for i, ref in enumerate(refs[len(widths) : len(widths) + n_last]):
        to.put(outs[i % 3], last(core, group), ref[...], core if i < 3 else 1 - core)
    for part, width in enumerate(widths):
        own = refs[part]
        for step in range(width // PAIR):
            cols = slice(step * PAIR, (step + 1) * PAIR)
            chunk, message_slot = pairs[part][step]
            at = columns(message_slot)
            for side, out_ref in enumerate(outs[1:]):
                total = own[side, :, cols] + near[side, :, at].astype(F32)
                to.put(out_ref, chunk, (total + far[side, :, at].astype(F32)).astype(BF16))
    to.wait()


def finish(order, last, far, near, parts, third, d_queries):
    shape = d_queries.shape
    widths = tuple(x.shape[2] for x in parts)
    ins = [far, near, *parts, *third]
    return pl.pallas_call(
        functools.partial(finish_kernel, order, last, widths, len(third)),
        out_shape=(jax.ShapeDtypeStruct(shape, BF16),) * 3,
        in_specs=[VMEM] * len(ins) + [ANY],
        out_specs=(ANY,) * 3,
        scratch_shapes=scratch_of(2 * sum(widths) // PAIR + len(third), shape[1]),
        input_output_aliases={len(ins): 0},
        cost_estimate=BRIEF,
        compiler_params=PARAMS,
        name="finish",
    )(*ins, d_queries)


def body(queries, keys, values, d_out, w_out, pattern, valid):
    n_seq, n_fsdp = lax.axis_size("seq"), lax.axis_size("fsdp")
    n_chunks = queries.shape[2] // PAIR
    near = functools.partial(lax.ppermute, axis_name="seq", perm=swap(n_seq, 0))
    far = functools.partial(lax.ppermute, axis_name="seq", perm=swap(n_seq, 1))

    def cross(x, bits):
        pairs = [
            (s * n_fsdp + g, s * n_fsdp + (g ^ bits[s % 2]))
            for s in range(n_seq)
            for g in range(n_fsdp)
        ]
        return lax.ppermute(x, ("seq", "fsdp"), pairs)

    last = lambda core, group: group ^ 3 if n_fsdp == 4 else 0
    kv = join(keys, values)
    limits = limits_of(pattern, valid)
    far_kv, near_kv = far(kv), near(kv)
    if n_fsdp == 4 and n_chunks == 4 and w_out.shape[0] == PAIR:
        got = cross(w_out, (1, 2))
        message = hand_on("hand_far", last, [d_out], [queries, near_kv])
        far_both, near_both = far(message), near(message)
        rows, d_own = turned_rows(d_out, w_out)
        ours = rows, queries, limits, (kv, near_kv, far_kv)
        own = heads("heads_own", lambda core, group: [(group, 0, 0, ((0, 0, PAIR),), 0)], 3, [d_own], (), *ours)
        early = got, near_kv, far_kv, limits, rows, own[0]
        got, near_kv, far_kv, limits, rows, own_dq = lax.optimization_barrier(early)
        ours = rows, queries, limits, (kv, near_kv, far_kv)
        mine, *both = onward(last, got, far_kv)
        got_d = cross(mine, (2, 1))
        near_got = [near(x) for x in both]
        first = heads(
            "heads_first",
            lambda core, group: [(group ^ (1 + core), 0, 1 + core, ((0, 0, PAIR),), 0)],
            3,
            [got],
            own[2:],
            *ours,
        )
        near_both, near_got, dq = lax.optimization_barrier((near_both, near_got, first[0]))
        second = heads(
            "heads_second",
            lambda core, group: [(group ^ (2 - core), 0, 2 - core, ((0, 0, HD), (1, 0, HD)), 1 - core)],
            3,
            near_got,
            first[2:],
            *ours,
        )
        halo = near_both, far_both, *near_got
        prob, attended, far_rows = last_probs(last, *ours[1:], halo)
        order = lambda core, group: [
            [(group, 0)],
            [(group ^ (1 + core), 1 + core)],
            [(group ^ (2 - core), 2 - core)],
        ]
        placed = settle(order, (own_dq, dq, second[0]), queries.shape)
        got_d, halo, prob, placed = lax.optimization_barrier((got_d, halo, prob, placed))
        sums = far(second[3]), near(second[2])
        edge = [near(x) for x in split(got_d)]
        known = prob, attended, far_rows, *ours[:2], ours[3], halo
        third = *last_head(last, True, *known, [got_d]), *last_head(last, False, *known, edge)
        return finish(order, last, *sums, (own[1], first[1], second[1]), third, placed)
    full = lax.all_gather(w_out, "fsdp", axis=0, tiled=True)
    ours = turned_rows(d_out, w_out)[0], queries, limits, (kv, near_kv, far_kv)
    steps = lambda core, group: [
        (i, i, i, ((0, i * PAIR, PAIR),), 0) for i in range(n_chunks)
    ]
    dq, own, to_core, to_far = heads("heads_all", steps, n_chunks, [full], (), *ours)
    order = lambda core, group: [[(i, i) for i in range(n_chunks)]]
    placed = settle(order, (dq,), queries.shape)
    return finish(order, last, far(to_far), near(to_core), (own,), (), placed)


def solution(mesh):
    rows = P("fsdp", "seq", None)
    in_specs = (rows, rows, rows, rows, P("fsdp", None), P(), P("fsdp", None))
    return jax.shard_map(
        body, mesh=mesh, in_specs=in_specs, out_specs=(rows,) * 3, check_vma=False
    )
```

```python
import functools

import jax
import jax.numpy as jnp
from jax import lax
from jax.experimental import pallas as pl
from jax.experimental.pallas import tpu as pltpu
from jax.sharding import PartitionSpec as P

HD = 128
PAIR = 2 * HD
BRIEF = pl.CostEstimate(flops=1, bytes_accessed=1, transcendentals=0)
F32 = jnp.float32
BF16 = jnp.bfloat16
NT = (((1,), (1,)), ((), ()))
NN = (((1,), (0,)), ((), ()))
TN = (((0,), (0,)), ((), ()))
ANY = pl.BlockSpec(memory_space=pl.ANY)
VMEM = pl.BlockSpec(memory_space=pltpu.VMEM)
SMEM = pl.BlockSpec(memory_space=pltpu.SMEM)
PARAMS = pltpu.CompilerParams(vmem_limit_bytes=40 * 2**20)
SCALE = HD ** (-0.5)


def dot(a, b, dims):
    return lax.dot_general(a, b, dims, preferred_element_type=F32)


def swap(n, offset):
    pairs = []
    for i in range(offset, n - 1, 2):
        pairs += [(i, i + 1), (i + 1, i)]
    return pairs


def place():
    return lax.rem(lax.axis_index("seq"), 2), lax.axis_index("fsdp")


def columns(chunk):
    return pl.ds(pl.multiple_of(chunk * PAIR, PAIR), PAIR)


def head_columns(first, head):
    return pl.ds(pl.multiple_of(first + head * HD, HD), HD)


def call(kernel, name, out_shape, in_specs, out_specs, scratch, *args):
    return pl.pallas_call(
        kernel,
        out_shape=out_shape,
        in_specs=in_specs,
        out_specs=out_specs,
        scratch_shapes=scratch,
        cost_estimate=BRIEF,
        compiler_params=PARAMS,
        name=name,
    )(*args)


def key_limits(pat_ref, val_ref):
    shard = lax.axis_index("seq")
    count = val_ref.shape[1]

    def pair(block):
        return block + 1 - 2 * lax.rem(block + 2, 2)

    def far(block):
        return block - 1 + 2 * lax.rem(block + 2, 2)

    wanted = [(shard, block) for block in (shard, pair(shard), far(shard))]
    for row, other in ((pair(shard), far(pair(shard))), (far(shard), pair(far(shard)))):
        wanted += [(row, block) for block in (row, shard, other)]
    limits = []
    for row, block in wanted:
        held = jnp.clip(row, 0, count - 1)
        listed = pat_ref[0, held] == block
        for entry in range(1, pat_ref.shape[0]):
            listed = jnp.logical_or(listed, pat_ref[entry, held] == block)
        inside = jnp.logical_and(row == held, jnp.logical_and(block >= 0, block < count))
        keys = val_ref[0, jnp.clip(block, 0, count - 1)]
        limits.append(jnp.where(jnp.logical_and(listed, inside), keys, 0))
    return limits


def limits_kernel(pat_ref, val_ref, limit_ref):
    limit_ref[...] = jnp.zeros_like(limit_ref)
    for row, limit in enumerate(key_limits(pat_ref, val_ref)):
        limit_ref[row : row + 1, :] = jnp.full((1, PAIR), limit, jnp.int32)


def limits_of(pattern, valid):
    shape = jax.ShapeDtypeStruct((16, PAIR), jnp.int32)
    return call(limits_kernel, "limits", shape, [SMEM] * 2, VMEM, [], pattern.T, valid)


def join_kernel(k_ref, v_ref, kv_ref):
    width = k_ref.shape[2]
    kv_ref[:, :width] = k_ref[0]
    kv_ref[:, width:] = v_ref[0]


def join(keys, values):
    tok, width = keys.shape[1:]
    shape = jax.ShapeDtypeStruct((tok, 2 * width), BF16)
    return call(join_kernel, "join", shape, [VMEM] * 2, VMEM, [], keys, values)


def hand_on_kernel(last, n_whole, *refs):
    core, group = place()
    whole, cut, out_ref = refs[:n_whole], refs[n_whole:-1], refs[-1]
    chunk = last(core, group)
    pieces = [ref[0] for ref in whole]
    for ref in cut:
        if ref.ndim == 3:
            pieces.append(ref[0, :, columns(chunk)])
        else:
            pieces.append(ref[:, columns(chunk)])
            pieces.append(ref[:, columns(chunk + ref.shape[1] // (2 * PAIR))])
    to = 0
    for piece in pieces:
        out_ref[:, to : to + piece.shape[1]] = piece
        to += piece.shape[1]


def hand_on(name, last, whole, cut):
    width = sum(x.shape[2] for x in whole) + sum(PAIR * (1 if x.ndim == 3 else 2) for x in cut)
    shape = jax.ShapeDtypeStruct((cut[0].shape[-2], width), BF16)
    kernel = functools.partial(hand_on_kernel, last, len(whole))
    return call(kernel, name, shape, [VMEM] * (len(whole) + len(cut)), VMEM, [], *whole, *cut)


def turned_kernel(dy_ref, w_ref, out_ref, d_ref):
    out_ref[...] = dy_ref[0].T
    d_ref[...] = dot(w_ref[...], out_ref[...], NN).astype(BF16)


def turned_rows(d_out, w_out):
    depth, tok = d_out.shape[:0:-1]
    shapes = (depth, tok), (w_out.shape[0], tok)
    shapes = tuple(jax.ShapeDtypeStruct(shape, BF16) for shape in shapes)
    return call(turned_kernel, "turned", shapes, [VMEM] * 2, (VMEM,) * 2, [], d_out, w_out)


def onward_kernel(last, w_ref, kv_ref, mine_ref, *both_refs):
    core, group = place()
    half, depth = mine_ref.shape
    chunk = last(core, group)
    mine_ref[...] = w_ref[pl.ds(pl.multiple_of(core * half, half), half), :]
    for side, (ref, which) in enumerate(zip(both_refs, (core, 1 - core))):
        ref[:, :depth] = w_ref[pl.ds(pl.multiple_of(which * half, half), half), :]
        ref[:, depth:] = kv_ref[:, columns(chunk + side * (kv_ref.shape[1] // (2 * PAIR)))]


def onward(last, got, kv):
    rows, depth = got.shape
    half, wide = (rows // 2, depth), (rows // 2, depth + PAIR)
    shapes = tuple(jax.ShapeDtypeStruct(shape, BF16) for shape in (half, wide, wide))
    kernel = functools.partial(onward_kernel, last)
    return call(kernel, "onward", shapes, [VMEM] * 2, (VMEM,) * 3, [], got, kv)


def split_kernel(x_ref, *out_refs):
    for i, ref in enumerate(out_refs):
        ref[...] = x_ref[i * ref.shape[0] : (i + 1) * ref.shape[0], :]


def split(x):
    half = jax.ShapeDtypeStruct((x.shape[0] // 2, x.shape[1]), BF16)
    return call(split_kernel, "split", (half, half), [VMEM], (VMEM,) * 2, [], x)


def diagonal(x):
    zero = jnp.zeros((x.shape[0], HD), x.dtype)
    return jnp.concatenate(
        [
            jnp.concatenate([x[:, :HD], zero], axis=1),
            jnp.concatenate([zero, x[:, HD:]], axis=1),
        ],
        axis=0,
    )


def diagonal_turned(one, two):
    zero = jnp.zeros_like(one)
    return jnp.concatenate(
        [jnp.concatenate([one, zero], axis=1), jnp.concatenate([zero, two], axis=1)], axis=0
    )


def in_order(rows, lead):
    one, two = rows[:HD], rows[HD:]
    if isinstance(lead, int):
        return (one, two) if lead == 0 else (two, one)
    return jnp.where(lead == 0, one, two), jnp.where(lead == 0, two, one)


def key_mask(limit_ref, rows, first, count):
    index = lax.broadcasted_iota(jnp.int32, (rows, PAIR), 0)
    return jnp.concatenate(
        [index < limit_ref[i : i + 1, :] for i in range(first, first + count)], axis=0
    )


def prob_of(k, qd, open_keys):
    score = jnp.where(open_keys, dot(k, qd, NT) * SCALE, -jnp.inf)
    top = jnp.maximum(jnp.max(score, axis=0, keepdims=True), -1e30)
    raised = jnp.exp(score - top)
    total = jnp.maximum(jnp.sum(raised, axis=0, keepdims=True), 1.0)
    return raised * (1.0 / total)


def score_grad(prob, prob_b, v, d):
    d_prob = dot(v, d, NN)
    delta = jnp.sum(prob_b.astype(F32) * d_prob, axis=0, keepdims=True)
    return (prob * (d_prob - delta)).astype(BF16)


def query_grad(d_score, k, tok):
    both = dot(d_score, k, TN) * SCALE
    return jnp.concatenate([both[:tok, :HD], both[tok:, HD:]], axis=1).astype(BF16)


def stacked(refs, cols):
    return jnp.concatenate([ref[:, cols] for ref in refs], axis=0)


def heads_kernel(steps, messages, dy_ref, q_ref, limit_ref, *refs):
    core, group = place()
    k_refs, w_refs = refs[:3], refs[3 : -4 - messages]
    earlier, (dq_ref, own_ref, *message_refs) = refs[-4 - messages : -4], refs[-4:]
    for old, out in zip(earlier, message_refs):
        out[...] = old[...]
    tok, depth = q_ref.shape[1], dy_ref.shape[0]
    values_at = k_refs[0].shape[1] // (2 * PAIR)
    open_keys = key_mask(limit_ref, tok, 0, 3)
    for chunk, slot, message_slot, pieces, lead in steps(core, group):
        cols, dest, message_dest = columns(chunk), columns(slot), columns(message_slot)
        w = jnp.concatenate([w_refs[i][row : row + rows, :depth] for i, row, rows in pieces], axis=0)
        if w_refs[pieces[0][0]].shape[1] >= depth:
            w = dot(w, dy_ref[...], NN).astype(BF16)
        d = diagonal_turned(*in_order(w, lead))
        qd = diagonal(q_ref[0, :, cols])
        k, v = stacked(k_refs, cols), stacked(k_refs, columns(chunk + values_at))
        prob = prob_of(k, qd, open_keys)
        prob_b = prob.astype(BF16)
        d_score = score_grad(prob, prob_b, v, d)
        dq_ref[:, dest] = query_grad(d_score, k, tok)
        for side, grad in enumerate((dot(d_score, qd, NN) * SCALE, dot(prob_b, d, NT))):
            own_ref[side, :, dest] = grad[:tok]
            for i, ref in enumerate(message_refs, 1):
                ref[side, :, message_dest] = grad[i * tok : (i + 1) * tok].astype(BF16)


def heads(name, steps, places, weights, earlier, d_out, q, limits, blocks):
    tok = q.shape[1]
    width = len(steps(0, 0)) * PAIR
    message = jax.ShapeDtypeStruct((2, tok, places * PAIR), BF16)
    return call(
        functools.partial(heads_kernel, steps, len(earlier)),
        name,
        (
            jax.ShapeDtypeStruct((tok, width), BF16),
            jax.ShapeDtypeStruct((2, tok, width), F32),
            message,
            message,
        ),
        [VMEM] * (6 + len(weights) + len(earlier)),
        (VMEM,) * 4,
        [],
        d_out,
        q,
        limits,
        *blocks,
        *weights,
        *earlier,
    )


def last_parts(last, q_ref, near_both, far_both, near_next, kv_refs):
    cols = columns(last(*place()))
    value_cols = columns(last(*place()) + kv_refs[0].shape[1] // (2 * PAIR))
    depth = far_both.shape[1] - 3 * PAIR
    own, near, far = ([ref[:, at] for at in (cols, value_cols)] for ref in kv_refs)
    past_near = [ref[:, depth:] for ref in near_next]
    past_far = [far_both[:, depth + PAIR : depth + 2 * PAIR], far_both[:, depth + 2 * PAIR :]]
    at_queries = slice(depth, depth + PAIR)
    return (
        (q_ref[0, :, cols], (own, near, far)),
        (near_both[:, at_queries], (near, own, past_near)),
        (far_both[:, at_queries], (far, own, past_far)),
    )


def joined(parts, side):
    return jnp.concatenate([part[side] for part in parts], axis=0)


def probs_kernel(last, q_ref, limit_ref, *refs):
    *kv_refs, near_both, far_both = refs[:5]
    near_next, (prob_ref, attended_ref, turned_ref) = refs[5:7], refs[7:]
    tok = q_ref.shape[1]
    depth = turned_ref.shape[0]
    turned_ref[:, :tok] = near_both[:, :depth].T
    turned_ref[:, tok:] = far_both[:, :depth].T
    blocks = last_parts(last, q_ref, near_both, far_both, near_next, kv_refs)
    for block, (q, parts) in enumerate(blocks):
        open_keys = key_mask(limit_ref, tok, 3 * block, 3)
        prob = prob_of(joined(parts, 0), diagonal(q), open_keys)
        prob_ref[block] = prob
        out = dot(joined(parts, 1), prob.astype(BF16), TN)
        attended_ref[block] = jnp.concatenate([out[:HD, :tok], out[HD:, tok:]], axis=1)


def last_probs(last, q, limits, blocks, halo):
    tok = q.shape[1]
    depth = halo[1].shape[1] - 3 * PAIR
    return call(
        functools.partial(probs_kernel, last),
        "probs_last",
        (
            jax.ShapeDtypeStruct((3, 3 * tok, PAIR), F32),
            jax.ShapeDtypeStruct((3, HD, 2 * tok), F32),
            jax.ShapeDtypeStruct((depth, 2 * tok), BF16),
        ),
        [VMEM] * 9,
        (VMEM,) * 3,
        [],
        q,
        limits,
        *blocks,
        *halo,
    )


def last_kernel(last, first, rows_ref, far_rows_ref, q_ref, prob_ref, attended_ref, *refs):
    core, group = place()
    head = core if first else 1 - core
    kv_refs, (near_both, far_both, *near_next) = refs[:3], refs[3:7]
    *w_refs, dq_ref, dk_ref, dv_ref = refs[7:]
    tok, depth = q_ref.shape[1], rows_ref.shape[0]
    w = jnp.concatenate([ref[...] for ref in w_refs], axis=0)
    turned = [dot(w, ref[...], NN).astype(BF16) for ref in (rows_ref, far_rows_ref)]
    turned = jnp.concatenate(turned, axis=1)
    start = last(core, group) * PAIR
    values_at = kv_refs[0].shape[1] // 2
    own, near, far = (
        [ref[:, head_columns(at, head)] for at in (start, start + values_at)] for ref in kv_refs
    )
    past_near = [ref[:, head_columns(depth, head)] for ref in near_next]
    past_far = [far_both[:, head_columns(depth + i * PAIR, head)] for i in (1, 2)]
    blocks = (
        (q_ref[0, :, head_columns(start, head)], (own, near, far)),
        (near_both[:, head_columns(depth, head)], (near, own, past_near)),
        (far_both[:, head_columns(depth, head)], (far, own, past_far)),
    )
    probs, scores, queries = [], [], []
    for block, (q, parts) in enumerate(blocks):
        d = turned[:, block * tok : (block + 1) * tok]
        lanes = head_columns(0, head)
        delta = jnp.sum(d.astype(F32) * attended_ref[block, :, lanes], axis=0, keepdims=True)
        if block == 0:
            prob, v = prob_ref[block, :, lanes], joined(parts, 1)
        else:
            prob, v = prob_ref[block, tok : 2 * tok, lanes], parts[1][1]
        d_score = (prob * (dot(v, d, NN) - delta)).astype(BF16)
        if block == 0:
            dq_ref[...] = (dot(d_score, joined(parts, 0), TN) * SCALE).astype(BF16)
        probs.append(prob[:tok].astype(BF16))
        scores.append(d_score[:tok])
        queries.append(q)
    scores, probs = jnp.concatenate(scores, axis=1), jnp.concatenate(probs, axis=1)
    dk_ref[...] = (dot(scores, jnp.concatenate(queries, axis=0), NN) * SCALE).astype(BF16)
    dv_ref[...] = dot(probs, turned, NT).astype(BF16)


def last_head(last, first, prob, attended, far_rows, rows, q, blocks, halo, w):
    tok = q.shape[1]
    return call(
        functools.partial(last_kernel, last, first),
        "heads_last" if first else "heads_end",
        (jax.ShapeDtypeStruct((tok, HD), BF16),) * 3,
        [VMEM] * (12 + len(w)),
        (VMEM,) * 3,
        [],
        rows,
        far_rows,
        q,
        prob,
        attended,
        *blocks,
        *halo,
        *w,
    )


class Columns:
    def __init__(self, stage, sems):
        self.stage, self.sems, self.copies = stage, sems, []

    def put(self, out_ref, chunk, value):
        at = len(self.copies)
        self.stage[at] = value
        target = out_ref.at[0, :, columns(chunk)]
        copy = pltpu.make_async_copy(self.stage.at[at], target, self.sems.at[at])
        copy.start()
        self.copies.append(copy)

    def wait(self):
        for copy in self.copies:
            copy.wait()


def scratch_of(count, tok):
    return [pltpu.VMEM((count, tok, PAIR), BF16), pltpu.SemaphoreType.DMA((count,))]


def settle_kernel(order, widths, *refs):
    out_ref, to = refs[-3], Columns(*refs[-2:])
    pairs = order(*place())
    for part, width in enumerate(widths):
        for step in range(width // PAIR):
            cols = slice(step * PAIR, (step + 1) * PAIR)
            to.put(out_ref, pairs[part][step][0], refs[part][:, cols])
    to.wait()


def settle(order, d_queries, shape):
    widths = tuple(x.shape[1] for x in d_queries)
    return call(
        functools.partial(settle_kernel, order, widths),
        "settle",
        jax.ShapeDtypeStruct(shape, BF16),
        [VMEM] * len(d_queries),
        ANY,
        scratch_of(sum(widths) // PAIR, shape[1]),
        *d_queries,
    )


def finish_kernel(order, last, widths, n_last, far, near, *refs):
    core, group = place()
    pairs = order(core, group)
    ends = refs[len(widths) : len(widths) + n_last]
    outs, (stage, sems) = refs[-5:-2], refs[-2:]
    start = last(core, group) * PAIR
    copies = []

    def send(held, target):
        copies.append(pltpu.make_async_copy(held, target, sems.at[len(copies)]))
        copies[-1].start()

    for side in range(3):
        for i, ref in enumerate(ends[side::3]):
            stage[side, :, head_columns(start, core if i == 0 else 1 - core)] = ref[...]
        if side == 0:
            if ends:
                cols = columns(last(core, group))
                send(stage.at[0, :, cols], outs[0].at[0, :, cols])
            continue
        for part, width in enumerate(widths):
            own = refs[part]
            for step in range(width // PAIR):
                cols = slice(step * PAIR, (step + 1) * PAIR)
                chunk, message_slot = pairs[part][step]
                at = columns(message_slot)
                total = own[side - 1, :, cols] + near[side - 1, :, at].astype(F32)
                total = (total + far[side - 1, :, at].astype(F32)).astype(BF16)
                stage[side, :, columns(chunk)] = total
        send(stage.at[side], outs[side].at[0])
    for copy in copies:
        copy.wait()


def finish(order, last, far, near, parts, third, d_queries):
    shape = d_queries.shape
    widths = tuple(x.shape[2] for x in parts)
    ins = [far, near, *parts, *third]
    return pl.pallas_call(
        functools.partial(finish_kernel, order, last, widths, len(third)),
        out_shape=(jax.ShapeDtypeStruct(shape, BF16),) * 3,
        in_specs=[VMEM] * len(ins) + [ANY],
        out_specs=(ANY,) * 3,
        scratch_shapes=[pltpu.VMEM((3, *shape[1:]), BF16), pltpu.SemaphoreType.DMA((3,))],
        input_output_aliases={len(ins): 0},
        cost_estimate=BRIEF,
        compiler_params=PARAMS,
        name="finish",
    )(*ins, d_queries)


def body(queries, keys, values, d_out, w_out, pattern, valid):
    n_seq, n_fsdp = lax.axis_size("seq"), lax.axis_size("fsdp")
    n_chunks = queries.shape[2] // PAIR
    near = functools.partial(lax.ppermute, axis_name="seq", perm=swap(n_seq, 0))
    far = functools.partial(lax.ppermute, axis_name="seq", perm=swap(n_seq, 1))

    def cross(x, bits):
        pairs = [
            (s * n_fsdp + g, s * n_fsdp + (g ^ bits[s % 2]))
            for s in range(n_seq)
            for g in range(n_fsdp)
        ]
        return lax.ppermute(x, ("seq", "fsdp"), pairs)

    last = lambda core, group: group ^ 3 if n_fsdp == 4 else 0
    kv = join(keys, values)
    limits = limits_of(pattern, valid)
    far_kv, near_kv = far(kv), near(kv)
    if n_fsdp == 4 and n_chunks == 4 and w_out.shape[0] == PAIR:
        got = cross(w_out, (1, 2))
        message = hand_on("hand_far", last, [d_out], [queries, near_kv])
        far_both, near_both = far(message), near(message)
        rows, d_own = turned_rows(d_out, w_out)
        ours = rows, queries, limits, (kv, near_kv, far_kv)
        own = heads("heads_own", lambda core, group: [(group, 0, 0, ((0, 0, PAIR),), 0)], 3, [d_own], (), *ours)
        early = got, near_kv, far_kv, limits, rows, own[0]
        got, near_kv, far_kv, limits, rows, own_dq = lax.optimization_barrier(early)
        ours = rows, queries, limits, (kv, near_kv, far_kv)
        mine, *both = onward(last, got, far_kv)
        got_d = cross(mine, (2, 1))
        near_got = [near(x) for x in both]
        first = heads(
            "heads_first",
            lambda core, group: [(group ^ (1 + core), 0, 1 + core, ((0, 0, PAIR),), 0)],
            3,
            [got],
            own[2:],
            *ours,
        )
        near_both, near_got, dq = lax.optimization_barrier((near_both, near_got, first[0]))
        second = heads(
            "heads_second",
            lambda core, group: [(group ^ (2 - core), 0, 2 - core, ((0, 0, HD), (1, 0, HD)), 1 - core)],
            3,
            near_got,
            first[2:],
            *ours,
        )
        halo = near_both, far_both, *near_got
        prob, attended, far_rows = last_probs(last, *ours[1:], halo)
        order = lambda core, group: [
            [(group, 0)],
            [(group ^ (1 + core), 1 + core)],
            [(group ^ (2 - core), 2 - core)],
        ]
        placed = settle(order, (own_dq, dq, second[0]), queries.shape)
        got_d, halo, prob, placed = lax.optimization_barrier((got_d, halo, prob, placed))
        sums = far(second[3]), near(second[2])
        edge = [near(x) for x in split(got_d)]
        known = prob, attended, far_rows, *ours[:2], ours[3], halo
        third = *last_head(last, True, *known, [got_d]), *last_head(last, False, *known, edge)
        return finish(order, last, *sums, (own[1], first[1], second[1]), third, placed)
    full = lax.all_gather(w_out, "fsdp", axis=0, tiled=True)
    ours = turned_rows(d_out, w_out)[0], queries, limits, (kv, near_kv, far_kv)
    steps = lambda core, group: [
        (i, i, i, ((0, i * PAIR, PAIR),), 0) for i in range(n_chunks)
    ]
    dq, own, to_core, to_far = heads("heads_all", steps, n_chunks, [full], (), *ours)
    order = lambda core, group: [[(i, i) for i in range(n_chunks)]]
    placed = settle(order, (dq,), queries.shape)
    return finish(order, last, far(to_far), near(to_core), (own,), (), placed)


def solution(mesh):
    rows = P("fsdp", "seq", None)
    in_specs = (rows, rows, rows, rows, P("fsdp", None), P(), P("fsdp", None))
    return jax.shard_map(
        body, mesh=mesh, in_specs=in_specs, out_specs=(rows,) * 3, check_vma=False
    )
```

```python
import functools

import jax
import jax.numpy as jnp
from jax import lax
from jax.experimental import pallas as pl
from jax.experimental.pallas import tpu as pltpu
from jax.sharding import PartitionSpec as P

HD = 128
PAIR = 2 * HD
BRIEF = pl.CostEstimate(flops=1, bytes_accessed=1, transcendentals=0)
F32 = jnp.float32
BF16 = jnp.bfloat16
NT = (((1,), (1,)), ((), ()))
NN = (((1,), (0,)), ((), ()))
TN = (((0,), (0,)), ((), ()))
ANY = pl.BlockSpec(memory_space=pl.ANY)
VMEM = pl.BlockSpec(memory_space=pltpu.VMEM)
SMEM = pl.BlockSpec(memory_space=pltpu.SMEM)
PARAMS = pltpu.CompilerParams(vmem_limit_bytes=40 * 2**20)
SCALE = HD ** (-0.5)


def dot(a, b, dims):
    return lax.dot_general(a, b, dims, preferred_element_type=F32)


def swap(n, offset):
    pairs = []
    for i in range(offset, n - 1, 2):
        pairs += [(i, i + 1), (i + 1, i)]
    return pairs


def place():
    return lax.rem(lax.axis_index("seq"), 2), lax.axis_index("fsdp")


def columns(chunk):
    return pl.ds(pl.multiple_of(chunk * PAIR, PAIR), PAIR)


def head_columns(first, head):
    return pl.ds(pl.multiple_of(first + head * HD, HD), HD)


def call(kernel, name, out_shape, in_specs, out_specs, scratch, *args):
    return pl.pallas_call(
        kernel,
        out_shape=out_shape,
        in_specs=in_specs,
        out_specs=out_specs,
        scratch_shapes=scratch,
        cost_estimate=BRIEF,
        compiler_params=PARAMS,
        name=name,
    )(*args)


def key_limits(pat_ref, val_ref):
    shard = lax.axis_index("seq")
    count = val_ref.shape[1]

    def pair(block):
        return block + 1 - 2 * lax.rem(block + 2, 2)

    def far(block):
        return block - 1 + 2 * lax.rem(block + 2, 2)

    wanted = [(shard, block) for block in (shard, pair(shard), far(shard))]
    for row, other in ((pair(shard), far(pair(shard))), (far(shard), pair(far(shard)))):
        wanted += [(row, block) for block in (row, shard, other)]
    limits = []
    for row, block in wanted:
        held = jnp.clip(row, 0, count - 1)
        listed = pat_ref[0, held] == block
        for entry in range(1, pat_ref.shape[0]):
            listed = jnp.logical_or(listed, pat_ref[entry, held] == block)
        inside = jnp.logical_and(row == held, jnp.logical_and(block >= 0, block < count))
        keys = val_ref[0, jnp.clip(block, 0, count - 1)]
        limits.append(jnp.where(jnp.logical_and(listed, inside), keys, 0))
    return limits


def limits_kernel(pat_ref, val_ref, limit_ref):
    limit_ref[...] = jnp.zeros_like(limit_ref)
    for row, limit in enumerate(key_limits(pat_ref, val_ref)):
        limit_ref[row : row + 1, :] = jnp.full((1, PAIR), limit, jnp.int32)


def limits_of(pattern, valid):
    shape = jax.ShapeDtypeStruct((16, PAIR), jnp.int32)
    return call(limits_kernel, "limits", shape, [SMEM] * 2, VMEM, [], pattern.T, valid)


def join_kernel(k_ref, v_ref, kv_ref):
    width = k_ref.shape[2]
    kv_ref[:, :width] = k_ref[0]
    kv_ref[:, width:] = v_ref[0]


def join(keys, values):
    tok, width = keys.shape[1:]
    shape = jax.ShapeDtypeStruct((tok, 2 * width), BF16)
    return call(join_kernel, "join", shape, [VMEM] * 2, VMEM, [], keys, values)


def hand_on_kernel(last, n_whole, *refs):
    core, group = place()
    whole, cut, out_ref = refs[:n_whole], refs[n_whole:-1], refs[-1]
    chunk = last(core, group)
    pieces = [ref[0] for ref in whole]
    for ref in cut:
        if ref.ndim == 3:
            pieces.append(ref[0, :, columns(chunk)])
        else:
            pieces.append(ref[:, columns(chunk)])
            pieces.append(ref[:, columns(chunk + ref.shape[1] // (2 * PAIR))])
    to = 0
    for piece in pieces:
        out_ref[:, to : to + piece.shape[1]] = piece
        to += piece.shape[1]


def hand_on(name, last, whole, cut):
    width = sum(x.shape[2] for x in whole) + sum(PAIR * (1 if x.ndim == 3 else 2) for x in cut)
    shape = jax.ShapeDtypeStruct((cut[0].shape[-2], width), BF16)
    kernel = functools.partial(hand_on_kernel, last, len(whole))
    return call(kernel, name, shape, [VMEM] * (len(whole) + len(cut)), VMEM, [], *whole, *cut)


def turned_kernel(dy_ref, w_ref, out_ref, d_ref):
    out_ref[...] = dy_ref[0].T
    d_ref[...] = dot(w_ref[...], out_ref[...], NN).astype(BF16)


def turned_rows(d_out, w_out):
    depth, tok = d_out.shape[:0:-1]
    shapes = (depth, tok), (w_out.shape[0], tok)
    shapes = tuple(jax.ShapeDtypeStruct(shape, BF16) for shape in shapes)
    return call(turned_kernel, "turned", shapes, [VMEM] * 2, (VMEM,) * 2, [], d_out, w_out)


def onward_kernel(last, w_ref, kv_ref, mine_ref, *both_refs):
    core, group = place()
    half, depth = mine_ref.shape
    chunk = last(core, group)
    mine_ref[...] = w_ref[pl.ds(pl.multiple_of(core * half, half), half), :]
    for side, (ref, which) in enumerate(zip(both_refs, (core, 1 - core))):
        ref[:, :depth] = w_ref[pl.ds(pl.multiple_of(which * half, half), half), :]
        ref[:, depth:] = kv_ref[:, columns(chunk + side * (kv_ref.shape[1] // (2 * PAIR)))]


def onward(last, got, kv):
    rows, depth = got.shape
    half, wide = (rows // 2, depth), (rows // 2, depth + PAIR)
    shapes = tuple(jax.ShapeDtypeStruct(shape, BF16) for shape in (half, wide, wide))
    kernel = functools.partial(onward_kernel, last)
    return call(kernel, "onward", shapes, [VMEM] * 2, (VMEM,) * 3, [], got, kv)


def split_kernel(x_ref, *out_refs):
    for i, ref in enumerate(out_refs):
        ref[...] = x_ref[i * ref.shape[0] : (i + 1) * ref.shape[0], :]


def split(x):
    half = jax.ShapeDtypeStruct((x.shape[0] // 2, x.shape[1]), BF16)
    return call(split_kernel, "split", (half, half), [VMEM], (VMEM,) * 2, [], x)


def diagonal(x):
    zero = jnp.zeros((x.shape[0], HD), x.dtype)
    return jnp.concatenate(
        [
            jnp.concatenate([x[:, :HD], zero], axis=1),
            jnp.concatenate([zero, x[:, HD:]], axis=1),
        ],
        axis=0,
    )


def diagonal_turned(one, two):
    zero = jnp.zeros_like(one)
    return jnp.concatenate(
        [jnp.concatenate([one, zero], axis=1), jnp.concatenate([zero, two], axis=1)], axis=0
    )


def in_order(rows, lead):
    one, two = rows[:HD], rows[HD:]
    if isinstance(lead, int):
        return (one, two) if lead == 0 else (two, one)
    return jnp.where(lead == 0, one, two), jnp.where(lead == 0, two, one)


def key_mask(limit_ref, rows, first, count):
    index = lax.broadcasted_iota(jnp.int32, (rows, PAIR), 0)
    return jnp.concatenate(
        [index < limit_ref[i : i + 1, :] for i in range(first, first + count)], axis=0
    )


def prob_of(k, qd, open_keys):
    score = jnp.where(open_keys, dot(k, qd, NT) * SCALE, -jnp.inf)
    top = jnp.maximum(jnp.max(score, axis=0, keepdims=True), -1e30)
    raised = jnp.exp(score - top)
    total = jnp.maximum(jnp.sum(raised, axis=0, keepdims=True), 1.0)
    return raised * (1.0 / total)


def score_grad(prob, prob_b, v, d):
    d_prob = dot(v, d, NN)
    delta = jnp.sum(prob_b.astype(F32) * d_prob, axis=0, keepdims=True)
    return (prob * (d_prob - delta)).astype(BF16)


def query_grad(d_score, k, tok):
    both = dot(d_score, k, TN) * SCALE
    return jnp.concatenate([both[:tok, :HD], both[tok:, HD:]], axis=1).astype(BF16)


def stacked(refs, cols):
    return jnp.concatenate([ref[:, cols] for ref in refs], axis=0)


def heads_kernel(steps, messages, dy_ref, q_ref, limit_ref, *refs):
    core, group = place()
    k_refs, w_refs = refs[:3], refs[3 : -4 - messages]
    earlier, (dq_ref, own_ref, *message_refs) = refs[-4 - messages : -4], refs[-4:]
    for old, out in zip(earlier, message_refs):
        out[...] = old[...]
    tok, depth = q_ref.shape[1], dy_ref.shape[0]
    values_at = k_refs[0].shape[1] // (2 * PAIR)
    open_keys = key_mask(limit_ref, tok, 0, 3)
    for chunk, slot, message_slot, pieces, lead in steps(core, group):
        cols, dest, message_dest = columns(chunk), columns(slot), columns(message_slot)
        w = jnp.concatenate([w_refs[i][row : row + rows, :depth] for i, row, rows in pieces], axis=0)
        if w_refs[pieces[0][0]].shape[1] >= depth:
            w = dot(w, dy_ref[...], NN).astype(BF16)
        d = diagonal_turned(*in_order(w, lead))
        qd = diagonal(q_ref[0, :, cols])
        k, v = stacked(k_refs, cols), stacked(k_refs, columns(chunk + values_at))
        prob = prob_of(k, qd, open_keys)
        prob_b = prob.astype(BF16)
        d_score = score_grad(prob, prob_b, v, d)
        dq_ref[:, dest] = query_grad(d_score, k, tok)
        for side, grad in enumerate((dot(d_score, qd, NN) * SCALE, dot(prob_b, d, NT))):
            own_ref[side, :, dest] = grad[:tok]
            for i, ref in enumerate(message_refs, 1):
                ref[side, :, message_dest] = grad[i * tok : (i + 1) * tok].astype(BF16)


def heads(name, steps, places, weights, earlier, d_out, q, limits, blocks):
    tok = q.shape[1]
    width = len(steps(0, 0)) * PAIR
    message = jax.ShapeDtypeStruct((2, tok, places * PAIR), BF16)
    return call(
        functools.partial(heads_kernel, steps, len(earlier)),
        name,
        (
            jax.ShapeDtypeStruct((tok, width), BF16),
            jax.ShapeDtypeStruct((2, tok, width), F32),
            message,
            message,
        ),
        [VMEM] * (6 + len(weights) + len(earlier)),
        (VMEM,) * 4,
        [],
        d_out,
        q,
        limits,
        *blocks,
        *weights,
        *earlier,
    )


def last_parts(last, q_ref, near_both, far_both, near_next, kv_refs):
    cols = columns(last(*place()))
    value_cols = columns(last(*place()) + kv_refs[0].shape[1] // (2 * PAIR))
    depth = far_both.shape[1] - 3 * PAIR
    own, near, far = ([ref[:, at] for at in (cols, value_cols)] for ref in kv_refs)
    past_near = [ref[:, depth:] for ref in near_next]
    past_far = [far_both[:, depth + PAIR : depth + 2 * PAIR], far_both[:, depth + 2 * PAIR :]]
    at_queries = slice(depth, depth + PAIR)
    return (
        (q_ref[0, :, cols], (own, near, far)),
        (near_both[:, at_queries], (near, own, past_near)),
        (far_both[:, at_queries], (far, own, past_far)),
    )


def joined(parts, side):
    return jnp.concatenate([part[side] for part in parts], axis=0)


def probs_kernel(last, q_ref, limit_ref, *refs):
    *kv_refs, near_both, far_both = refs[:5]
    near_next, prob_ref, turned_ref = refs[5:7], refs[7], refs[8]
    tok = q_ref.shape[1]
    depth = turned_ref.shape[0]
    turned_ref[:, :tok] = near_both[:, :depth].T
    turned_ref[:, tok:] = far_both[:, :depth].T
    blocks = last_parts(last, q_ref, near_both, far_both, near_next, kv_refs)
    for block, (q, parts) in enumerate(blocks):
        open_keys = key_mask(limit_ref, tok, 3 * block, 3)
        prob_ref[block] = prob_of(joined(parts, 0), diagonal(q), open_keys)


def last_probs(last, q, limits, blocks, halo):
    tok = q.shape[1]
    depth = halo[1].shape[1] - 3 * PAIR
    return call(
        functools.partial(probs_kernel, last),
        "probs_last",
        (
            jax.ShapeDtypeStruct((3, 3 * tok, PAIR), F32),
            jax.ShapeDtypeStruct((depth, 2 * tok), BF16),
        ),
        [VMEM] * 9,
        (VMEM,) * 2,
        [],
        q,
        limits,
        *blocks,
        *halo,
    )


def last_kernel(last, first, rows_ref, far_rows_ref, q_ref, prob_ref, *refs):
    core, group = place()
    head = core if first else 1 - core
    kv_refs, (near_both, far_both, *near_next) = refs[:3], refs[3:7]
    *w_refs, dq_ref, dk_ref, dv_ref = refs[7:]
    tok, depth = q_ref.shape[1], rows_ref.shape[0]
    w = jnp.concatenate([ref[...] for ref in w_refs], axis=0)
    turned = [dot(w, ref[...], NN).astype(BF16) for ref in (rows_ref, far_rows_ref)]
    turned = jnp.concatenate(turned, axis=1)
    start = last(core, group) * PAIR
    values_at = kv_refs[0].shape[1] // 2
    own, near, far = (
        [ref[:, head_columns(at, head)] for at in (start, start + values_at)] for ref in kv_refs
    )
    past_near = [ref[:, head_columns(depth, head)] for ref in near_next]
    past_far = [far_both[:, head_columns(depth + i * PAIR, head)] for i in (1, 2)]
    blocks = (
        (q_ref[0, :, head_columns(start, head)], (own, near, far)),
        (near_both[:, head_columns(depth, head)], (near, own, past_near)),
        (far_both[:, head_columns(depth, head)], (far, own, past_far)),
    )
    probs, scores, queries = [], [], []
    for block, (q, parts) in enumerate(blocks):
        prob = prob_ref[block, :, head_columns(0, head)]
        prob_b = prob.astype(BF16)
        d = turned[:, block * tok : (block + 1) * tok]
        d_score = score_grad(prob, prob_b, joined(parts, 1), d)
        if block == 0:
            dq_ref[...] = (dot(d_score, joined(parts, 0), TN) * SCALE).astype(BF16)
        mine = slice(0, tok) if block == 0 else slice(tok, 2 * tok)
        probs.append(prob_b[mine])
        scores.append(d_score[mine])
        queries.append(q)
    scores, probs = jnp.concatenate(scores, axis=1), jnp.concatenate(probs, axis=1)
    dk_ref[...] = (dot(scores, jnp.concatenate(queries, axis=0), NN) * SCALE).astype(BF16)
    dv_ref[...] = dot(probs, turned, NT).astype(BF16)


def last_head(last, first, prob, far_rows, rows, q, blocks, halo, w):
    tok = q.shape[1]
    return call(
        functools.partial(last_kernel, last, first),
        "heads_last" if first else "heads_end",
        (jax.ShapeDtypeStruct((tok, HD), BF16),) * 3,
        [VMEM] * (11 + len(w)),
        (VMEM,) * 3,
        [],
        rows,
        far_rows,
        q,
        prob,
        *blocks,
        *halo,
        *w,
    )


class Columns:
    def __init__(self, stage, sems):
        self.stage, self.sems, self.copies = stage, sems, []

    def put(self, out_ref, chunk, value, head=None):
        at = len(self.copies)
        if head is None:
            held, target = self.stage.at[at], out_ref.at[0, :, columns(chunk)]
        else:
            held = self.stage.at[at, :, pl.ds(0, HD)]
            target = out_ref.at[0, :, head_columns(chunk * PAIR, head)]
        held[...] = value
        copy = pltpu.make_async_copy(held, target, self.sems.at[at])
        copy.start()
        self.copies.append(copy)

    def wait(self):
        for copy in self.copies:
            copy.wait()


def scratch_of(count, tok):
    return [pltpu.VMEM((count, tok, PAIR), BF16), pltpu.SemaphoreType.DMA((count,))]


def settle_kernel(order, widths, *refs):
    out_ref, to = refs[-3], Columns(*refs[-2:])
    pairs = order(*place())
    for part, width in enumerate(widths):
        for step in range(width // PAIR):
            cols = slice(step * PAIR, (step + 1) * PAIR)
            to.put(out_ref, pairs[part][step][0], refs[part][:, cols])
    to.wait()


def settle(order, d_queries, shape):
    widths = tuple(x.shape[1] for x in d_queries)
    return call(
        functools.partial(settle_kernel, order, widths),
        "settle",
        jax.ShapeDtypeStruct(shape, BF16),
        [VMEM] * len(d_queries),
        ANY,
        scratch_of(sum(widths) // PAIR, shape[1]),
        *d_queries,
    )


def finish_kernel(order, last, widths, n_last, far, near, *refs):
    outs, to = refs[-5:-2], Columns(*refs[-2:])
    pairs = order(*place())
    core, group = place()
    for i, ref in enumerate(refs[len(widths) : len(widths) + n_last]):
        to.put(outs[i % 3], last(core, group), ref[...], core if i < 3 else 1 - core)
    for part, width in enumerate(widths):
        own = refs[part]
        for step in range(width // PAIR):
            cols = slice(step * PAIR, (step + 1) * PAIR)
            chunk, message_slot = pairs[part][step]
            at = columns(message_slot)
            for side, out_ref in enumerate(outs[1:]):
                total = own[side, :, cols] + near[side, :, at].astype(F32)
                to.put(out_ref, chunk, (total + far[side, :, at].astype(F32)).astype(BF16))
    to.wait()


def finish(order, last, far, near, parts, third, d_queries):
    shape = d_queries.shape
    widths = tuple(x.shape[2] for x in parts)
    ins = [far, near, *parts, *third]
    return pl.pallas_call(
        functools.partial(finish_kernel, order, last, widths, len(third)),
        out_shape=(jax.ShapeDtypeStruct(shape, BF16),) * 3,
        in_specs=[VMEM] * len(ins) + [ANY],
        out_specs=(ANY,) * 3,
        scratch_shapes=scratch_of(2 * sum(widths) // PAIR + len(third), shape[1]),
        input_output_aliases={len(ins): 0},
        cost_estimate=BRIEF,
        compiler_params=PARAMS,
        name="finish",
    )(*ins, d_queries)


def body(queries, keys, values, d_out, w_out, pattern, valid):
    n_seq, n_fsdp = lax.axis_size("seq"), lax.axis_size("fsdp")
    n_chunks = queries.shape[2] // PAIR
    near = functools.partial(lax.ppermute, axis_name="seq", perm=swap(n_seq, 0))
    far = functools.partial(lax.ppermute, axis_name="seq", perm=swap(n_seq, 1))

    def cross(x, bits):
        pairs = [
            (s * n_fsdp + g, s * n_fsdp + (g ^ bits[s % 2]))
            for s in range(n_seq)
            for g in range(n_fsdp)
        ]
        return lax.ppermute(x, ("seq", "fsdp"), pairs)

    last = lambda core, group: group ^ 3 if n_fsdp == 4 else 0
    kv = join(keys, values)
    limits = limits_of(pattern, valid)
    far_kv, near_kv = far(kv), near(kv)
    if n_fsdp == 4 and n_chunks == 4 and w_out.shape[0] == PAIR:
        got = cross(w_out, (1, 2))
        message = hand_on("hand_far", last, [d_out], [queries, near_kv])
        far_both, near_both = far(message), near(message)
        rows, d_own = turned_rows(d_out, w_out)
        ours = rows, queries, limits, (kv, near_kv, far_kv)
        own = heads("heads_own", lambda core, group: [(group, 0, 0, ((0, 0, PAIR),), 0)], 3, [d_own], (), *ours)
        early = got, near_kv, far_kv, limits, rows, own[0]
        got, near_kv, far_kv, limits, rows, own_dq = lax.optimization_barrier(early)
        ours = rows, queries, limits, (kv, near_kv, far_kv)
        mine, *both = onward(last, got, far_kv)
        got_d = cross(mine, (2, 1))
        near_got = [near(x) for x in both]
        first = heads(
            "heads_first",
            lambda core, group: [(group ^ (1 + core), 0, 1 + core, ((0, 0, PAIR),), 0)],
            3,
            [got],
            own[2:],
            *ours,
        )
        near_both, near_got, dq = lax.optimization_barrier((near_both, near_got, first[0]))
        second = heads(
            "heads_second",
            lambda core, group: [(group ^ (2 - core), 0, 2 - core, ((0, 0, HD), (1, 0, HD)), 1 - core)],
            3,
            near_got,
            first[2:],
            *ours,
        )
        halo = near_both, far_both, *near_got
        prob, far_rows = last_probs(last, *ours[1:], halo)
        order = lambda core, group: [
            [(group, 0)],
            [(group ^ (1 + core), 1 + core)],
            [(group ^ (2 - core), 2 - core)],
        ]
        placed = settle(order, (own_dq, dq, second[0]), queries.shape)
        got_d, halo, placed = lax.optimization_barrier((got_d, halo, placed))
        sums = far(second[3]), near(second[2])
        edge = [near(x) for x in split(got_d)]
        known = prob, far_rows, *ours[:2], ours[3], halo
        third = *last_head(last, True, *known, [got_d]), *last_head(last, False, *known, edge)
        return finish(order, last, *sums, (own[1], first[1], second[1]), third, placed)
    full = lax.all_gather(w_out, "fsdp", axis=0, tiled=True)
    ours = turned_rows(d_out, w_out)[0], queries, limits, (kv, near_kv, far_kv)
    steps = lambda core, group: [
        (i, i, i, ((0, i * PAIR, PAIR),), 0) for i in range(n_chunks)
    ]
    dq, own, to_core, to_far = heads("heads_all", steps, n_chunks, [full], (), *ours)
    order = lambda core, group: [[(i, i) for i in range(n_chunks)]]
    placed = settle(order, (dq,), queries.shape)
    return finish(order, last, far(to_far), near(to_core), (own,), (), placed)


def solution(mesh):
    rows = P("fsdp", "seq", None)
    in_specs = (rows, rows, rows, rows, P("fsdp", None), P(), P("fsdp", None))
    return jax.shard_map(
        body, mesh=mesh, in_specs=in_specs, out_specs=(rows,) * 3, check_vma=False
    )
```
